32 devices in a mesh: gx: 4 (over y, x), gy: 8 (over z, core).
Axes of the slice: x: 2, y: 2, z: 4, core: 2. Of those that a mesh axis runs over, the one named last changes fastest.
Arguments:
- adjoint_source: float32 [2, 64, 64, 128], P(None, 'gx', 'gy'), may hold values from -16 to 16
- storage: float32 [4, 64, 64, 128], P(None, 'gx', 'gy'), may hold values from -0.2 to 2, as said below
- soil_ids: int32 [64, 64, 128], P('gx', 'gy'), may hold values from 0 to 15
- bc_mask: int32 [64, 64], P('gx', 'gy'), may hold values 0 or 1
- soil_props: float32 [3, 16], replicated, may hold values from 0.1 to 1
Outputs:
- adjoint: float32 [2, 64, 64, 128], P(None, 'gx', 'gy')
- residual: float32 [2, 64, 64, 128], P(None, 'gx', 'gy')
- next_basis: float32 [2, 64, 64, 128], P(None, 'gx', 'gy')
The draws below stay inside these ranges and needn't reach their ends.
Inputs may be any that keep to these rules, and one draw needn't show every extreme that they name: `storage`: sp and St lie in 0.2 to 2, Spt within -0.04 to 0.04, Stp within -0.2 to 0.2.
All inputs are finite; a program needn't handle non-finite values. No bound on the sum of `bc_mask` on one device may be relied on, other than what follows from the above.
Results may differ from the reference program's by a relative error of at most 0.0008.
Values sent between devices are 32-bit elements; how exact they have to be, the bound alone decides.
No kernel may reach another device: no remote copies, remote signals or barrier semaphores. Data moves between devices by JAX's collectives and lax.ppermute only.
A program may use at most 64 MiB of HBM per device.

```python
import math
import jax
import jax.numpy as jnp
from jax import lax

CX = 16
CY = 8
NZ = 128
NMAT = 16
MARGIN = 4
SWEEPS = 6
ITERS = 2
NX = 64
NY = 64
N_GX = 4
N_GY = 8


def draw_storage(key, part):
    keys = jax.random.split(key, 4)
    shape = (NX, NY, NZ)
    diag_press = jnp.exp(jax.random.uniform(keys[0], shape, jnp.float32, math.log(0.2), math.log(2.0)))
    diag_heat = jnp.exp(jax.random.uniform(keys[1], shape, jnp.float32, math.log(0.2), math.log(2.0)))
    cross_pt = jax.random.uniform(keys[2], shape, jnp.float32, -0.04, 0.04)
    cross_tp = jax.random.uniform(keys[3], shape, jnp.float32, -0.2, 0.2)
    return jnp.stack([diag_press, cross_pt, cross_tp, diag_heat])


def draw_adjoint_source(key, part):
    shape = (2, NX, NY, NZ)
    ramp_x = jnp.arange(NX, dtype=jnp.float32) / (NX - 1)
    ramp_y = jnp.arange(NY, dtype=jnp.float32) / (NY - 1)
    level = ramp_x[:, None] + ramp_y[None, :] - 1.0
    amplitude = jnp.exp(math.log(3.0) * level)[None, :, :, None]
    noise = jnp.clip(jax.random.normal(key, shape, jnp.float32), -4.0, 4.0)
    return amplitude * noise


def set_ends(values, own_key, low, largest):
    shape = values.shape
    spot = [jax.random.randint(jax.random.fold_in(own_key, axis), (), 0, shape[axis]) for axis in range(len(shape))]
    values = values.at[tuple(spot)].set(low)
    longest = shape.index(max(shape))
    spot[longest] = (spot[longest] + 1) % shape[longest]
    return values.at[tuple(spot)].set(largest)


def setup_inputs(seed: int = 0) -> dict:
    seeds = jax.random.split(jax.random.key(seed), 6)
    adjoint_source = draw_adjoint_source(jax.random.fold_in(seeds[5], 71), 0)
    storage = draw_storage(jax.random.fold_in(seeds[5], 71), 0)
    soil_ids = set_ends(jax.random.randint(seeds[2], (NX, NY, NZ), 0, NMAT), jax.random.fold_in(seeds[2], 1), 0, NMAT - 1).astype(jnp.int32)
    bc_mask = set_ends((jax.random.randint(seeds[3], (NX, NY), 0, 2) < 1).astype(jnp.int32), jax.random.fold_in(seeds[3], 1), 0, 1)
    soil_props = jnp.clip(jnp.exp(jax.random.uniform(seeds[4], (3, NMAT), jnp.float32, math.log(0.1), math.log(1.0))), 0.1, 1.0)
    return {"adjoint_source": adjoint_source, "storage": storage, "soil_ids": soil_ids, "bc_mask": bc_mask, "soil_props": soil_props}


epsilon = 1e-06

def neighbour_list(field):
    middle = field[1:-1, 1:-1]
    below = jnp.pad(middle[:, :, :-1], ((0, 0), (0, 0), (1, 0)))
    above = jnp.pad(middle[:, :, 1:], ((0, 0), (0, 0), (0, 1)))
    return [field[:-2, 1:-1], field[2:, 1:-1], field[1:-1, :-2], field[1:-1, 2:], below, above]

def face_parts(coefficients):
    centre = coefficients[:, 1:-1, 1:-1]
    press_faces = jnp.stack([jnp.sqrt(centre[0] * other) for other in neighbour_list(coefficients[0])])
    heat_faces = jnp.stack([jnp.sqrt(centre[1] * other) for other in neighbour_list(coefficients[1])])
    return (press_faces, heat_faces, centre)

def laplace(field, faces, diagonal):
    total = diagonal * field[1:-1, 1:-1]
    for index, other in enumerate(neighbour_list(field)):
        total = total - faces[index] * other
    return total

def apply_adjoint(padded, spread_e, press_faces, heat_faces, centre):
    press_part = padded[0]
    heat_part = padded[1]
    mixed = press_part + spread_e * heat_part
    press_diag = lax.optimization_barrier(jnp.sum(press_faces, axis=0)) + centre[7]
    heat_diag = lax.optimization_barrier(jnp.sum(heat_faces, axis=0))
    press_mid = press_part[1:-1, 1:-1]
    heat_mid = heat_part[1:-1, 1:-1]
    press_out = centre[3] * press_mid + laplace(mixed, press_faces, press_diag) + centre[5] * heat_mid
    heat_out = centre[4] * press_mid + centre[6] * heat_mid + laplace(heat_part, heat_faces, heat_diag)
    return jnp.stack([press_out, heat_out])

def block_inverse(press_faces, heat_faces, centre, outside):
    press_diag = lax.optimization_barrier(jnp.sum(press_faces, axis=0)) + centre[7]
    heat_diag = lax.optimization_barrier(jnp.sum(heat_faces, axis=0))
    first = centre[3] + press_diag + outside
    cross = centre[5] + centre[2] * press_diag
    lower = centre[4]
    last = centre[6] + heat_diag + outside
    determinant = first * last - cross * lower
    return (last / determinant, -cross / determinant, -lower / determinant, first / determinant)

def subdomain_solve(rhs, press_faces, heat_faces, centre, inverse, spread_e):
    solution = jnp.zeros_like(rhs)
    for sweep in range(SWEEPS):
        padded = jnp.pad(solution, ((0, 0), (1, 1), (1, 1), (0, 0)))
        remain = rhs - apply_adjoint(padded, spread_e, press_faces, heat_faces, centre)
        step_p = inverse[0] * remain[0] + inverse[1] * remain[1]
        step_t = inverse[2] * remain[0] + inverse[3] * remain[1]
        solution = solution + jnp.stack([step_p, step_t])
    return solution

def assemble(material, storage, bc_mask):
    depth = material.shape[3]
    top = lax.broadcasted_iota(jnp.int32, (1, 1, depth), 2) == depth - 1
    boundary = jnp.where(top, 2.0 * material[0] * bc_mask[:, :, None].astype(jnp.float32), 0.0)
    return jnp.concatenate([material, storage, boundary[None]], axis=0)

def least_squares(columns, beta):
    count = len(columns)
    target = [beta] + [0.0 * beta for index in range(count)]
    rotations = []
    upper = []
    for column_index, column in enumerate(columns):
        values = list(column)
        for index, pair in enumerate(rotations):
            high = pair[0] * values[index] + pair[1] * values[index + 1]
            low = -pair[1] * values[index] + pair[0] * values[index + 1]
            values[index] = high
            values[index + 1] = low
        radius = jnp.sqrt(values[column_index] * values[column_index] + values[column_index + 1] * values[column_index + 1])
        cosine = values[column_index] / radius
        sine = values[column_index + 1] / radius
        values[column_index] = radius
        rotations.append((cosine, sine))
        high = cosine * target[column_index] + sine * target[column_index + 1]
        low = -sine * target[column_index] + cosine * target[column_index + 1]
        target[column_index] = high
        target[column_index + 1] = low
        upper.append(values[:column_index + 1])
    weights = [None] * count
    for index in reversed(range(count)):
        accum = target[index]
        for later in range(index + 1, count):
            accum = accum - upper[later][index] * weights[later]
        weights[index] = accum / upper[index][index]
    return weights

def reference(adjoint_source, storage, soil_ids, bc_mask, soil_props):
    material = jnp.take(soil_props, soil_ids, axis=1)
    coefficients = assemble(material, storage, bc_mask)
    cycle = MARGIN + 1
    padded_coeffs = jnp.pad(coefficients, ((0, 0), (cycle, cycle), (cycle, cycle), (0, 0)))
    own_coeffs = padded_coeffs[:, MARGIN:-MARGIN, MARGIN:-MARGIN]
    own_press, own_heat, own_centre = face_parts(own_coeffs)

    def image_of(vector):
        padded = jnp.pad(vector, ((0, 0), (1, 1), (1, 1), (0, 0)))
        return apply_adjoint(padded, own_coeffs[2], own_press, own_heat, own_centre)
    span_x = jnp.arange(CX + 2 * MARGIN, dtype=jnp.int32)
    span_y = jnp.arange(CY + 2 * MARGIN, dtype=jnp.int32)

    def precondition(vector):
        accum = jnp.zeros((2, NX + 2 * MARGIN, NY + 2 * MARGIN, NZ), jnp.float32)

        def one_domain(domain, accum):
            start_x = (domain // N_GY * CX).astype(jnp.int32)
            start_y = (domain % N_GY * CY).astype(jnp.int32)
            zero = jnp.zeros((), jnp.int32)
            local = lax.dynamic_slice(padded_coeffs, (zero, start_x, start_y, zero), (8, CX + 2 * cycle, CY + 2 * cycle, NZ))
            owned = lax.dynamic_slice(vector, (zero, start_x, start_y, zero), (2, CX, CY, NZ))
            rhs = jnp.pad(owned, ((0, 0), (MARGIN, MARGIN), (MARGIN, MARGIN), (0, 0)))
            along_x = start_x - MARGIN + span_x
            along_y = start_y - MARGIN + span_y
            inside_x = (along_x >= 0) & (along_x < NX)
            inside_y = (along_y >= 0) & (along_y < NY)
            outside = (1.0 - (inside_x[:, None] & inside_y[None, :]).astype(jnp.float32))[:, :, None]
            press_faces, heat_faces, centre = face_parts(local)
            inverse = block_inverse(press_faces, heat_faces, centre, outside)
            solved = subdomain_solve(rhs, press_faces, heat_faces, centre, inverse, local[2])
            current = lax.dynamic_slice(accum, (zero, start_x, start_y, zero), solved.shape)
            return lax.dynamic_update_slice(accum, current + solved, (zero, start_x, start_y, zero))
        accum = lax.fori_loop(0, N_GX * N_GY, one_domain, accum)
        return accum[:, MARGIN:-MARGIN, MARGIN:-MARGIN]
    beta = jnp.sqrt(jnp.sum(adjoint_source * adjoint_source) + epsilon)
    basis = [adjoint_source / beta]
    directions = []
    columns = []
    for column_index in range(ITERS):
        direction = precondition(basis[-1])
        directions.append(direction)
        image = image_of(direction)
        heights = [jnp.sum(image * prior) for prior in basis]
        for height, prior in zip(heights, basis):
            image = image - height * prior
        length = jnp.sqrt(jnp.sum(image * image) + epsilon)
        heights.append(length)
        columns.append(heights)
        basis.append(image / length)
    weights = least_squares(columns, beta)
    adjoint = weights[0] * directions[0]
    for index in range(1, ITERS):
        adjoint = adjoint + weights[index] * directions[index]
    residual = jnp.zeros_like(adjoint_source)
    for row in range(ITERS + 1):
        factor = beta if row == 0 else 0.0 * beta
        for column_index in range(ITERS):
            if row <= column_index + 1:
                factor = factor - columns[column_index][row] * weights[column_index]
        residual = residual + factor * basis[row]
    next_basis = basis[-1] * math.sqrt(2.0 * NX * NY * NZ)
    return (adjoint, residual, next_basis)
```

```python
import functools
import math

import jax
import jax.numpy as jnp
from jax import lax
from jax.experimental import pallas as pl
from jax.experimental.pallas import tpu as pltpu
from jax.sharding import PartitionSpec as P

MARGIN = 4
SWEEPS = 6
SUB = 8
LANE = 128
TILE = (SUB, LANE)
RIM = MARGIN + 1
EPSILON = 1e-06
F32 = jnp.float32


def sublane():
    return lax.broadcasted_iota(jnp.int32, TILE, 0)


def lane():
    return lax.broadcasted_iota(jnp.int32, TILE, 1)


def up_y(tile):
    return pltpu.roll(tile, SUB - 1, 0)


def down_y(tile):
    return pltpu.roll(tile, 1, 0)


def half_turn(tile):
    return pltpu.roll(tile, SUB // 2, 0)


def along_z(tile, spot):
    above = jnp.where(spot == LANE - 1, 0.0, pltpu.roll(tile, LANE - 1, 1))
    below = jnp.where(spot == 0, 0.0, pltpu.roll(tile, 1, 1))
    return above + below


def along_y(own, side, row, last_up, last_down):
    own_up, own_down = up_y(own), down_y(own)
    side_up, side_down = up_y(side), down_y(side)
    own_sum = jnp.where(row == 7, side_up, own_up) + jnp.where(row == 0, side_down, own_down)
    side_sum = jnp.where(row == 7, own_up, jnp.where(row == 3, last_up, side_up))
    side_sum = side_sum + jnp.where(row == 0, own_down, jnp.where(row == 4, last_down, side_down))
    return own_sum, side_sum


def along_y_own(own, side, row):
    up = jnp.where(row == 7, up_y(side), up_y(own))
    down = jnp.where(row == 0, down_y(side), down_y(own))
    return up + down


def position(axis):
    place = lax.axis_index(axis)
    first = lax.rem(place, 2) == 0
    return first, place > 0, place < lax.axis_size(axis) - 1


def from_sides(first, even, odd):
    return jnp.where(first, odd, even), jnp.where(first, even, odd)


def lookup(table, wire):
    index = jnp.maximum(wire.astype(jnp.int32) - 1, 0)
    return jnp.where(wire > 0.0, jnp.take_along_axis(table, index, axis=1), 0.0)


def wide_tables(props_ref):
    pad = jnp.zeros((props_ref.shape[0], LANE - props_ref.shape[1]), F32)
    wide = jnp.concatenate([props_ref[...], pad], axis=1)
    return [jnp.broadcast_to(wide[k : k + 1], TILE) for k in range(3)]


def pack_x_kernel(props_ref, storage_ref, ids_ref, bc_ref, fields_ref, wire_ref, even_ref, odd_ref):
    rows = ids_ref.shape[0]
    tables = wide_tables(props_ref)
    row, spot = sublane(), lane()
    diagonal = row == spot
    for x in range(rows):
        wire = (ids_ref[x] + 1).astype(F32)
        wire_ref[x] = wire
        kp = lookup(tables[0], wire)
        carried = lookup(tables[2], wire)
        line = jnp.concatenate(
            [bc_ref[pl.ds(x, 1), :].astype(F32), jnp.zeros((1, LANE - SUB), F32)], axis=1
        )
        held = jnp.sum(jnp.where(diagonal, jnp.broadcast_to(line, TILE), 0.0), axis=1, keepdims=True)
        bound = jnp.where(spot == LANE - 1, 2.0 * kp * held, 0.0)
        press = storage_ref[0, x]
        lower = storage_ref[1, x]
        fields_ref[0, x] = press + bound
        fields_ref[1, x] = carried * press - storage_ref[2, x]
        fields_ref[2, x] = lower
        fields_ref[3, x] = storage_ref[3, x] - carried * lower
    first, _, _ = position("gx")
    high, low = rows - MARGIN, 0
    start_even = jnp.where(first, high, low)
    start_odd = jnp.where(first, low, high)
    wire_even = jnp.where(first, rows - RIM, 0)
    wire_odd = jnp.where(first, 0, rows - RIM)
    for k in range(4):
        even_ref[pl.ds(k * MARGIN, MARGIN)] = fields_ref[k, pl.ds(start_even, MARGIN)]
        odd_ref[pl.ds(k * MARGIN, MARGIN)] = fields_ref[k, pl.ds(start_odd, MARGIN)]
    even_ref[pl.ds(4 * MARGIN, RIM)] = wire_ref[pl.ds(wire_even, RIM)]
    odd_ref[pl.ds(4 * MARGIN, RIM)] = wire_ref[pl.ds(wire_odd, RIM)]


def widen_x(fields_ref, wire_ref, even_ref, odd_ref):
    rows = wire_ref.shape[0]
    first, has_low, has_high = position("gx")
    fields = []
    for k in range(4):
        low, high = from_sides(
            first, even_ref[pl.ds(k * MARGIN, MARGIN)], odd_ref[pl.ds(k * MARGIN, MARGIN)]
        )
        fields.append(
            [low[i] for i in range(MARGIN)]
            + [fields_ref[k, x] for x in range(rows)]
            + [high[i] for i in range(MARGIN)]
        )
    low, high = from_sides(
        first, even_ref[pl.ds(4 * MARGIN, RIM)], odd_ref[pl.ds(4 * MARGIN, RIM)]
    )
    low = jnp.where(has_low, low, 0.0)
    high = jnp.where(has_high, high, 0.0)
    wire = (
        [low[i] for i in range(RIM)] + [wire_ref[x] for x in range(rows)] + [high[i] for i in range(RIM)]
    )
    return fields, wire


def pack_y_kernel(fields_ref, wire_ref, xe_ref, xo_ref, even_ref, odd_ref):
    fields, wire = widen_x(fields_ref, wire_ref, xe_ref, xo_ref)
    wide = len(fields[0])
    first, _, _ = position("gy")
    even_low = (sublane() < 4) != first
    for pair in range(2):
        for i in range(wide):
            one = fields[2 * pair][i]
            other = half_turn(fields[2 * pair + 1][i])
            even_ref[pair * wide + i] = jnp.where(even_low, one, other)
            odd_ref[pair * wide + i] = jnp.where(even_low, other, one)
    for j in range(wide + 2):
        even_ref[2 * wide + j] = wire[j]
        odd_ref[2 * wide + j] = wire[j]


def sweep_row(q_ref, t_ref, coeff_ref, j, row, spot, rhs):
    sums = []
    for ref in (q_ref, t_ref):
        own, side = ref[j, 0], ref[j, 1]
        own_sum, side_sum = along_y(own, side, row, 0.0, 0.0)
        own_sum = own_sum + (along_z(own, spot) + (ref[j - 1, 0] + ref[j + 1, 0]))
        side_sum = side_sum + (along_z(side, spot) + (ref[j - 1, 1] + ref[j + 1, 1]))
        sums.append([own_sum, side_sum])
    if rhs is not None:
        sums[0][0] = sums[0][0] + rhs[0]
        sums[1][0] = sums[1][0] + rhs[1]
    out = []
    for tile in range(2):
        flow, heat = sums[0][tile], sums[1][tile]
        out.append(
            (
                coeff_ref[0, j - 1, tile] * flow + coeff_ref[1, j - 1, tile] * heat,
                coeff_ref[2, j - 1, tile] * flow + coeff_ref[3, j - 1, tile] * heat,
            )
        )
    return out


def subdomain_sweeps(rhs_ref, coeff_ref, solved_ref, even_ref, odd_ref, buffers, rows):
    row, spot = sublane(), lane()
    wide = rows + 2 * MARGIN
    zero = jnp.zeros(TILE, F32)
    for buffer in buffers:
        for j in range(wide + 2):
            for tile in range(2):
                buffer[j, tile] = zero
    current, following = buffers[:2], buffers[2:]
    for x in range(rows):
        j = x + RIM
        flow, heat = rhs_ref[0, x], rhs_ref[1, x]
        current[0][j, 0] = coeff_ref[0, j - 1, 0] * flow + coeff_ref[1, j - 1, 0] * heat
        current[1][j, 0] = coeff_ref[2, j - 1, 0] * flow + coeff_ref[3, j - 1, 0] * heat
    first, _, _ = position("gy")
    even_low = (row < 4) != first
    for sweep in range(1, SWEEPS):
        reach = min(sweep, MARGIN)
        for x in range(-reach, rows + reach):
            j = x + RIM
            rhs = (rhs_ref[0, x], rhs_ref[1, x]) if 0 <= x < rows else None
            out = sweep_row(current[0], current[1], coeff_ref, j, row, spot, rhs)
            if sweep < SWEEPS - 1:
                for tile in range(2):
                    following[0][j, tile] = out[tile][0]
                    following[1][j, tile] = out[tile][1]
            else:
                for k in range(2):
                    own, side = out[0][k], out[1][k]
                    solved_ref[k, j - 1, 0] = own
                    solved_ref[k, j - 1, 1] = side
                    even_ref[k, j - 1] = jnp.where(even_low, own, side)
                    odd_ref[k, j - 1] = jnp.where(even_low, side, own)
        current, following = following, current


def coefficients_kernel(
    props_ref, fields_ref, wire_ref, xe_ref, xo_ref, ye_ref, yo_ref, source_ref,
    coeff_ref, image_ref, scale_ref, solved_ref, even_ref, odd_ref,
    gp_ref, gt_ref, rhs_ref, *buffers,
):
    rows = wire_ref.shape[0]
    wide = rows + 2 * MARGIN
    row, spot = sublane(), lane()
    tables = wide_tables(props_ref)
    roots = [jnp.sqrt(jnp.maximum(tables[0], 0.0)), jnp.sqrt(jnp.maximum(tables[1], 0.0))]
    fields, wire = widen_x(fields_ref, wire_ref, xe_ref, xo_ref)
    first, has_low, has_high = position("gy")
    out_wire = []
    for j in range(wide + 2):
        low, high = from_sides(first, ye_ref[2 * wide + j], yo_ref[2 * wide + j])
        low = jnp.where(has_low, low, 0.0)
        high = jnp.where(has_high, high, 0.0)
        own = wire[j]
        side = jnp.where(row < 4, high, low)
        beyond = jnp.where(row < 4, low, high)
        out_wire.append((own, side))
        for g, ref in enumerate((gp_ref, gt_ref)):
            ref[j, 0] = lookup(roots[g], own)
            ref[j, 1] = lookup(roots[g], side)
            ref[j, 2] = lookup(roots[g], beyond)
    for i in range(wide):
        j = i + 1
        stores = []
        for pair in range(2):
            low, high = from_sides(first, ye_ref[pair * wide + i], yo_ref[pair * wide + i])
            stores.append(jnp.where(row < 4, high, low))
            stores.append(half_turn(jnp.where(row < 4, low, high)))
        diagonals = []
        for ref in (gp_ref, gt_ref):
            beyond = ref[j, 2]
            own_sum, side_sum = along_y(ref[j, 0], ref[j, 1], row, up_y(beyond), down_y(beyond))
            own_sum = own_sum + along_z(ref[j, 0], spot) + (ref[j - 1, 0] + ref[j + 1, 0])
            side_sum = side_sum + along_z(ref[j, 1], spot) + (ref[j - 1, 1] + ref[j + 1, 1])
            diagonals.append((ref[j, 0] * own_sum, ref[j, 1] * side_sum))
        for tile in range(2):
            if tile == 0:
                press, cross, lower, heat = (fields[k][i] for k in range(4))
            else:
                press, cross, lower, heat = stores
            outside = jnp.where(out_wire[j][tile] > 0.0, 0.0, 1.0)
            gp, gt = gp_ref[j, tile], gt_ref[j, tile]
            a = press + diagonals[0][tile] + outside
            d = heat + diagonals[1][tile] + outside
            inverse = 1.0 / (a * d + cross * lower)
            pp, pt, tt = gp * gp, gp * gt, gt * gt
            coeff_ref[0, i, tile] = pp * d * inverse
            coeff_ref[1, i, tile] = pt * cross * inverse
            coeff_ref[2, i, tile] = -pt * lower * inverse
            coeff_ref[3, i, tile] = tt * a * inverse
            if tile == 0 and MARGIN <= i < wide - MARGIN:
                x = i - MARGIN
                over_p, over_t = 1.0 / gp, 1.0 / gt
                over = over_p * over_t
                image_ref[0, x] = a * (over_p * over_p)
                image_ref[1, x] = -cross * over
                image_ref[2, x] = lower * over
                image_ref[3, x] = d * (over_t * over_t)
                scale_ref[0, x] = gp
                scale_ref[1, x] = gt
                scale_ref[2, x] = over_p
                scale_ref[3, x] = over_t
                scale_ref[4, x] = lookup(tables[2], out_wire[j][0])
                rhs_ref[0, x] = source_ref[0, x] * over_p
                rhs_ref[1, x] = source_ref[1, x] * over_t
    subdomain_sweeps(rhs_ref, coeff_ref, solved_ref, even_ref, odd_ref, buffers, rows)


def fold_y_kernel(solved_ref, ye_ref, yo_ref, summed_ref, even_ref, odd_ref):
    wide = solved_ref.shape[1]
    row = sublane()
    first, has_low, has_high = position("gy")
    for k in range(2):
        for i in range(wide):
            low, high = from_sides(first, ye_ref[k, i], yo_ref[k, i])
            low = jnp.where(has_low, low, 0.0)
            high = jnp.where(has_high, high, 0.0)
            summed_ref[k, i, 0] = solved_ref[k, i, 0] + jnp.where(row < 4, low, high)
            summed_ref[k, i, 1] = solved_ref[k, i, 1] + jnp.where(row < 4, high, low)
    first, _, _ = position("gx")
    margin_even = jnp.where(first, wide - MARGIN, 0)
    margin_odd = jnp.where(first, 0, wide - MARGIN)
    rim_even = jnp.where(first, wide - MARGIN - 1, MARGIN)
    rim_odd = jnp.where(first, MARGIN, wide - MARGIN - 1)
    for k in range(2):
        for ref, margin, rim in ((even_ref, margin_even, rim_even), (odd_ref, margin_odd, rim_odd)):
            for tile in range(2):
                ref[k, pl.ds(tile * MARGIN, MARGIN)] = summed_ref[k, pl.ds(margin, MARGIN), tile]
            ref[k, 2 * MARGIN] = summed_ref[k, rim, 0]


def fold_x(summed_ref, xe_ref, xo_ref, field_refs):
    wide = summed_ref.shape[1]
    rows = wide - 2 * MARGIN
    first, has_low, has_high = position("gx")
    for k in range(2):
        low, high = from_sides(first, xe_ref[k], xo_ref[k])
        low = jnp.where(has_low, low, 0.0)
        high = jnp.where(has_high, high, 0.0)
        for x in range(-1, rows + 1):
            for tile in range(2):
                value = summed_ref[k, x + MARGIN, tile]
                if 0 <= x < MARGIN:
                    value = value + low[tile * MARGIN + x]
                if rows - MARGIN <= x < rows:
                    value = value + high[tile * MARGIN + x - (rows - MARGIN)]
                if tile == 0 and x == -1:
                    value = value + low[2 * MARGIN]
                if tile == 0 and x == rows:
                    value = value + high[2 * MARGIN]
                field_refs[k][x + 1, tile] = value


def image_row(field_refs, image_ref, x, row, spot):
    sums = []
    for ref in field_refs:
        own = ref[x + 1, 0]
        total = along_y_own(own, ref[x + 1, 1], row) + along_z(own, spot)
        sums.append(total + (ref[x, 0] + ref[x + 2, 0]))
    flow, heat = field_refs[0][x + 1, 0], field_refs[1][x + 1, 0]
    return (
        image_ref[0, x] * flow + image_ref[1, x] * heat - sums[0],
        image_ref[2, x] * flow + image_ref[3, x] * heat - sums[1],
    )


def keep_direction(direction_ref, scale_ref, field_refs, x):
    heat = field_refs[1][x + 1, 0] * scale_ref[3, x]
    direction_ref[1, x] = heat
    direction_ref[0, x] = field_refs[0][x + 1, 0] * scale_ref[2, x] - scale_ref[4, x] * heat


def gram_rows(pairs, row, offset):
    total = jnp.zeros(TILE, F32)
    for index, value in enumerate(pairs):
        line = jnp.broadcast_to(jnp.sum(value, axis=0, keepdims=True), TILE)
        total = total + jnp.where(row == index + offset, line, 0.0)
    return total


def step_kernel(
    summed_ref, xe_ref, xo_ref, coeff_ref, image_ref, scale_ref, source_ref,
    direction_ref, power_ref, gram_ref, solved_ref, even_ref, odd_ref,
    rhs_ref, q_ref, t_ref, *buffers,
):
    rows = source_ref.shape[1]
    row, spot = sublane(), lane()
    fields = (q_ref, t_ref)
    fold_x(summed_ref, xe_ref, xo_ref, fields)
    products = [jnp.zeros(TILE, F32) for _ in range(3)]
    for x in range(rows):
        keep_direction(direction_ref, scale_ref, fields, x)
        for k, part in enumerate(image_row(fields, image_ref, x, row, spot)):
            source = source_ref[k, x]
            scaled = part - source * scale_ref[2 + k, x]
            power = scaled * scale_ref[k, x]
            rhs_ref[k, x] = scaled
            power_ref[k, x] = power
            products[0] = products[0] + source * source
            products[1] = products[1] + source * power
            products[2] = products[2] + power * power
    gram_ref[...] = gram_rows(products, row, 0)
    subdomain_sweeps(rhs_ref, coeff_ref, solved_ref, even_ref, odd_ref, buffers, rows)


def last_kernel(
    summed_ref, xe_ref, xo_ref, image_ref, scale_ref, source_ref, power_ref, gram_in_ref,
    direction_ref, second_ref, gram_ref, q_ref, t_ref,
):
    rows = source_ref.shape[1]
    row, spot = sublane(), lane()
    fields = (q_ref, t_ref)
    fold_x(summed_ref, xe_ref, xo_ref, fields)
    products = [jnp.zeros(TILE, F32) for _ in range(3)]
    for x in range(rows):
        keep_direction(direction_ref, scale_ref, fields, x)
        for k, part in enumerate(image_row(fields, image_ref, x, row, spot)):
            power = power_ref[k, x]
            second = part * scale_ref[k, x] - power
            second_ref[k, x] = second
            products[0] = products[0] + source_ref[k, x] * second
            products[1] = products[1] + power * second
            products[2] = products[2] + second * second
    total = gram_in_ref[...] + gram_rows(products, row, 3)
    for device in range(gram_ref.shape[0]):
        gram_ref[device] = total


def combine_kernel(
    gram_ref, source_ref, power_ref, second_ref, one_ref, two_ref,
    adjoint_ref, residual_ref, basis_ref, *, scale,
):
    parts = [gram_ref[device] for device in range(gram_ref.shape[0])]
    while len(parts) > 1:
        parts = [parts[i] + parts[i + 1] if i + 1 < len(parts) else parts[i] for i in range(0, len(parts), 2)]
    sums = jnp.broadcast_to(jnp.sum(parts[0], axis=1, keepdims=True), TILE)
    g00, g01, g11, g02, g12, g22 = (sums[k : k + 1] for k in range(6))
    beta2 = g00 + EPSILON
    beta = jnp.sqrt(beta2)
    less = (EPSILON - g01) / beta2
    h11 = (g00 + g01) / beta2
    square = (less * less * g00 + 2.0 * less * g01 + g11) / beta2
    square = jnp.maximum(square, 0.0)
    h21 = jnp.sqrt(square + EPSILON)
    b = 1.0 / (beta * h21)
    a = less * b
    h12 = EPSILON * h11 / (beta2 * h21) + (a * g01 + b * g02) / beta
    short = EPSILON / (square + EPSILON) - (a * a * g01 + a * b * (g11 + g02) + b * b * g12)
    h22 = 1.0 - short
    c0 = a * short - h12 / beta
    c1 = a + b * short
    c2 = b
    square = c0 * (c0 * g00 + 2.0 * (c1 * g01 + c2 * g02)) + c1 * (c1 * g11 + 2.0 * c2 * g12) + c2 * c2 * g22
    h32 = jnp.sqrt(jnp.maximum(square, 0.0) + EPSILON)
    n0, n1, n2 = h21 * h32, -h11 * h32, h11 * h22 - h12 * h21
    factor = beta * n0 / (n0 * n0 + n1 * n1 + n2 * n2)
    f0, f1, f2 = factor * n0, factor * n1, factor * n2
    y2 = -f2 / h32
    y1 = (h11 * (beta - f0 - h12 * y2) - h21 * (f1 + h22 * y2)) / (h11 * h11 + h21 * h21)
    over = 1.0 / h32
    v0, v1, v2 = c0 * over, c1 * over, c2 * over
    wide = lambda value: jnp.broadcast_to(value, TILE)
    z_one, z_two = wide(y1 / beta + y2 * a), wide(y2 * b)
    r0, r1, r2 = wide(f0 / beta + f1 * a + f2 * v0), wide(f1 * b + f2 * v1), wide(f2 * v2)
    s0, s1, s2 = wide(scale * v0), wide(scale * v1), wide(scale * v2)
    for k in range(2):
        for x in range(source_ref.shape[1]):
            source, power, second = source_ref[k, x], power_ref[k, x], second_ref[k, x]
            adjoint_ref[k, x] = z_one * one_ref[k, x] + z_two * two_ref[k, x]
            residual_ref[k, x] = r0 * source + r1 * power + r2 * second
            basis_ref[k, x] = s0 * source + s1 * power + s2 * second


def call(kernel, outs, scratch=(), name=None):
    def run(*args):
        return pl.pallas_call(
            kernel,
            out_shape=[jax.ShapeDtypeStruct(shape, F32) for shape in outs],
            in_specs=[pl.BlockSpec(memory_space=pltpu.VMEM)] * len(args),
            out_specs=[pl.BlockSpec(memory_space=pltpu.VMEM)] * len(outs),
            scratch_shapes=[pltpu.VMEM(shape, F32) for shape in scratch],
            compiler_params=pltpu.CompilerParams(vmem_limit_bytes=32 * 1024 * 1024),
            name=name,
        )(*args)

    return run


def exchange(axis, even, odd):
    count = lax.axis_size(axis)
    pairs = [(i, i ^ 1) for i in range(count)]
    others = [(i, (((i - 1) % count) ^ 1) + 1) for i in range(count)]
    others = [(i, j % count) for i, j in others]
    return lax.ppermute(even, axis, pairs), lax.ppermute(odd, axis, others)


def shards(adjoint_source, storage, soil_ids, bc_mask, soil_props):
    rows, _, depth = soil_ids.shape
    wide = rows + 2 * MARGIN
    devices = lax.axis_size("gx") * lax.axis_size("gy")
    cells = 2.0 * rows * soil_ids.shape[1] * depth * devices
    own = (rows, *TILE)
    slab = (4 * MARGIN + RIM, *TILE)
    fields, wire, even, odd = call(pack_x_kernel, [(4, *own), own, slab, slab], name="pack_x")(
        soil_props, storage, soil_ids, bc_mask
    )
    xe, xo = exchange("gx", even, odd)
    slab = (3 * wide + 2, *TILE)
    even, odd = call(pack_y_kernel, [slab, slab], name="pack_y")(fields, wire, xe, xo)
    ye, yo = exchange("gy", even, odd)
    buffers = [(wide + 2, 2, *TILE)] * 4
    solved_shapes = [(2, wide, 2, *TILE), (2, wide, *TILE), (2, wide, *TILE)]
    coeff, image, scales, solved, even, odd = call(
        coefficients_kernel,
        [(4, wide, 2, *TILE), (4, *own), (5, *own)] + solved_shapes,
        [(wide + 2, 3, *TILE)] * 2 + [(2, *own)] + buffers,
        name="first_solve",
    )(soil_props, fields, wire, xe, xo, ye, yo, adjoint_source)

    fold_shapes = [(2, wide, 2, *TILE)] + [(2, 2 * MARGIN + 1, *TILE)] * 2
    ye, yo = exchange("gy", even, odd)
    summed, even, odd = call(fold_y_kernel, fold_shapes, name="fold_y")(solved, ye, yo)
    xe, xo = exchange("gx", even, odd)
    halo = [(rows + 2, 2, *TILE)] * 2
    one, power, gram, solved, even, odd = call(
        step_kernel,
        [(2, *own), (2, *own), TILE] + solved_shapes,
        [(2, *own)] + halo + buffers,
        name="second_solve",
    )(summed, xe, xo, coeff, image, scales, adjoint_source)

    ye, yo = exchange("gy", even, odd)
    summed, even, odd = call(fold_y_kernel, fold_shapes, name="fold_y")(solved, ye, yo)
    xe, xo = exchange("gx", even, odd)
    two, second, gram = call(
        last_kernel, [(2, *own), (2, *own), (devices, *TILE)], halo, name="last_image"
    )(summed, xe, xo, image, scales, adjoint_source, power, gram)
    gram = lax.all_to_all(gram, ("gx", "gy"), 0, 0)
    return tuple(
        call(
            functools.partial(combine_kernel, scale=math.sqrt(cells)), [(2, *own)] * 3, name="combine"
        )(gram, adjoint_source, power, second, one, two)
    )


def solution(mesh):
    in_specs = (
        P(None, "gx", "gy", None),
        P(None, "gx", "gy", None),
        P("gx", "gy", None),
        P("gx", "gy"),
        P(),
    )
    out_specs = (P(None, "gx", "gy", None), P(None, "gx", "gy", None), P(None, "gx", "gy", None))
    return jax.shard_map(shards, mesh=mesh, in_specs=in_specs, out_specs=out_specs, check_vma=False)
```

```python
import functools
import math

import jax
import jax.numpy as jnp
from jax import lax
from jax.experimental import pallas as pl
from jax.experimental.pallas import tpu as pltpu
from jax.sharding import PartitionSpec as P

MARGIN = 4
SWEEPS = 6
SUB = 8
LANE = 128
TILE = (SUB, LANE)
RIM = MARGIN + 1
EPSILON = 1e-06
F32 = jnp.float32


def sublane():
    return lax.broadcasted_iota(jnp.int32, TILE, 0)


def lane():
    return lax.broadcasted_iota(jnp.int32, TILE, 1)


def up_y(tile):
    return pltpu.roll(tile, SUB - 1, 0)


def down_y(tile):
    return pltpu.roll(tile, 1, 0)


def half_turn(tile):
    return pltpu.roll(tile, SUB // 2, 0)


def along_z(tile, spot):
    above = jnp.where(spot == LANE - 1, 0.0, pltpu.roll(tile, LANE - 1, 1))
    below = jnp.where(spot == 0, 0.0, pltpu.roll(tile, 1, 1))
    return above + below


def along_y(own, side, row, last_up, last_down):
    own_up, own_down = up_y(own), down_y(own)
    side_up, side_down = up_y(side), down_y(side)
    own_sum = jnp.where(row == 7, side_up, own_up) + jnp.where(row == 0, side_down, own_down)
    side_sum = jnp.where(row == 7, own_up, jnp.where(row == 3, last_up, side_up))
    side_sum = side_sum + jnp.where(row == 0, own_down, jnp.where(row == 4, last_down, side_down))
    return own_sum, side_sum


def along_y_own(own, side, row):
    up = jnp.where(row == 7, up_y(side), up_y(own))
    down = jnp.where(row == 0, down_y(side), down_y(own))
    return up + down


def position(axis):
    place = lax.axis_index(axis)
    first = lax.rem(place, 2) == 0
    return first, place > 0, place < lax.axis_size(axis) - 1


def from_sides(first, even, odd):
    return jnp.where(first, odd, even), jnp.where(first, even, odd)


def lookup(table, wire):
    index = jnp.maximum(wire.astype(jnp.int32) - 1, 0)
    return jnp.where(wire > 0.0, jnp.take_along_axis(table, index, axis=1), 0.0)


def wide_tables(props_ref):
    pad = jnp.zeros((props_ref.shape[0], LANE - props_ref.shape[1]), F32)
    wide = jnp.concatenate([props_ref[...], pad], axis=1)
    return [jnp.broadcast_to(wide[k : k + 1], TILE) for k in range(3)]


def pack_x_kernel(props_ref, storage_ref, ids_ref, bc_ref, fields_ref, wire_ref, even_ref, odd_ref):
    rows = ids_ref.shape[0]
    tables = wide_tables(props_ref)
    row, spot = sublane(), lane()
    diagonal = row == spot
    for x in range(rows):
        wire = (ids_ref[x] + 1).astype(F32)
        wire_ref[x] = wire
        kp = lookup(tables[0], wire)
        carried = lookup(tables[2], wire)
        line = jnp.concatenate(
            [bc_ref[pl.ds(x, 1), :].astype(F32), jnp.zeros((1, LANE - SUB), F32)], axis=1
        )
        held = jnp.sum(jnp.where(diagonal, jnp.broadcast_to(line, TILE), 0.0), axis=1, keepdims=True)
        bound = jnp.where(spot == LANE - 1, 2.0 * kp * held, 0.0)
        press = storage_ref[0, x]
        lower = storage_ref[1, x]
        fields_ref[0, x] = press + bound
        fields_ref[1, x] = carried * press - storage_ref[2, x]
        fields_ref[2, x] = lower
        fields_ref[3, x] = storage_ref[3, x] - carried * lower
    first, _, _ = position("gx")
    high, low = rows - MARGIN, 0
    start_even = jnp.where(first, high, low)
    start_odd = jnp.where(first, low, high)
    wire_even = jnp.where(first, rows - RIM, 0)
    wire_odd = jnp.where(first, 0, rows - RIM)
    for k in range(4):
        even_ref[pl.ds(k * MARGIN, MARGIN)] = fields_ref[k, pl.ds(start_even, MARGIN)]
        odd_ref[pl.ds(k * MARGIN, MARGIN)] = fields_ref[k, pl.ds(start_odd, MARGIN)]
    even_ref[pl.ds(4 * MARGIN, RIM)] = wire_ref[pl.ds(wire_even, RIM)]
    odd_ref[pl.ds(4 * MARGIN, RIM)] = wire_ref[pl.ds(wire_odd, RIM)]


def widen_x(fields_ref, wire_ref, even_ref, odd_ref):
    rows = wire_ref.shape[0]
    first, has_low, has_high = position("gx")
    fields = []
    for k in range(4):
        low, high = from_sides(
            first, even_ref[pl.ds(k * MARGIN, MARGIN)], odd_ref[pl.ds(k * MARGIN, MARGIN)]
        )
        fields.append(
            [low[i] for i in range(MARGIN)]
            + [fields_ref[k, x] for x in range(rows)]
            + [high[i] for i in range(MARGIN)]
        )
    low, high = from_sides(
        first, even_ref[pl.ds(4 * MARGIN, RIM)], odd_ref[pl.ds(4 * MARGIN, RIM)]
    )
    low = jnp.where(has_low, low, 0.0)
    high = jnp.where(has_high, high, 0.0)
    wire = (
        [low[i] for i in range(RIM)] + [wire_ref[x] for x in range(rows)] + [high[i] for i in range(RIM)]
    )
    return fields, wire


def pack_y_kernel(fields_ref, wire_ref, xe_ref, xo_ref, even_ref, odd_ref):
    fields, wire = widen_x(fields_ref, wire_ref, xe_ref, xo_ref)
    wide = len(fields[0])
    first, _, _ = position("gy")
    even_low = (sublane() < 4) != first
    for pair in range(2):
        for i in range(wide):
            one = fields[2 * pair][i]
            other = half_turn(fields[2 * pair + 1][i])
            even_ref[pair * wide + i] = jnp.where(even_low, one, other)
            odd_ref[pair * wide + i] = jnp.where(even_low, other, one)
    for j in range(wide + 2):
        even_ref[2 * wide + j] = wire[j]
        odd_ref[2 * wide + j] = wire[j]


def sweep_row(q_ref, t_ref, coeff_ref, j, row, spot, rhs):
    sums = []
    for ref in (q_ref, t_ref):
        own, side = ref[j, 0], ref[j, 1]
        own_sum, side_sum = along_y(own, side, row, 0.0, 0.0)
        own_sum = own_sum + (along_z(own, spot) + (ref[j - 1, 0] + ref[j + 1, 0]))
        side_sum = side_sum + (along_z(side, spot) + (ref[j - 1, 1] + ref[j + 1, 1]))
        sums.append([own_sum, side_sum])
    if rhs is not None:
        sums[0][0] = sums[0][0] + rhs[0]
        sums[1][0] = sums[1][0] + rhs[1]
    out = []
    for tile in range(2):
        flow, heat = sums[0][tile], sums[1][tile]
        out.append(
            (
                coeff_ref[0, j - 1, tile] * flow + coeff_ref[1, j - 1, tile] * heat,
                coeff_ref[2, j - 1, tile] * flow + coeff_ref[3, j - 1, tile] * heat,
            )
        )
    return out


def subdomain_sweeps(rhs_ref, coeff_ref, solved_ref, even_ref, odd_ref, buffers, rows):
    row, spot = sublane(), lane()
    wide = rows + 2 * MARGIN
    zero = jnp.zeros(TILE, F32)
    for buffer in buffers:
        for j in range(wide + 2):
            for tile in range(2):
                buffer[j, tile] = zero
    current, following = buffers[:2], buffers[2:]
    for x in range(rows):
        j = x + RIM
        flow, heat = rhs_ref[0, x], rhs_ref[1, x]
        current[0][j, 0] = coeff_ref[0, j - 1, 0] * flow + coeff_ref[1, j - 1, 0] * heat
        current[1][j, 0] = coeff_ref[2, j - 1, 0] * flow + coeff_ref[3, j - 1, 0] * heat
    first, _, _ = position("gy")
    even_low = (row < 4) != first
    for sweep in range(1, SWEEPS):
        reach = min(sweep, MARGIN)
        for x in range(-reach, rows + reach):
            j = x + RIM
            rhs = (rhs_ref[0, x], rhs_ref[1, x]) if 0 <= x < rows else None
            out = sweep_row(current[0], current[1], coeff_ref, j, row, spot, rhs)
            if sweep < SWEEPS - 1:
                for tile in range(2):
                    following[0][j, tile] = out[tile][0]
                    following[1][j, tile] = out[tile][1]
            else:
                for k in range(2):
                    own, side = out[0][k], out[1][k]
                    solved_ref[k, j - 1, 0] = own
                    solved_ref[k, j - 1, 1] = side
                    even_ref[k, j - 1] = jnp.where(even_low, own, side)
                    odd_ref[k, j - 1] = jnp.where(even_low, side, own)
        current, following = following, current


def coefficients_kernel(
    props_ref, fields_ref, wire_ref, xe_ref, xo_ref, ye_ref, yo_ref, source_ref,
    coeff_ref, image_ref, scale_ref, solved_ref, even_ref, odd_ref,
    gp_ref, gt_ref, rhs_ref, *buffers,
):
    rows = wire_ref.shape[0]
    wide = rows + 2 * MARGIN
    row, spot = sublane(), lane()
    tables = wide_tables(props_ref)
    roots = [jnp.sqrt(jnp.maximum(tables[0], 0.0)), jnp.sqrt(jnp.maximum(tables[1], 0.0))]
    fields, wire = widen_x(fields_ref, wire_ref, xe_ref, xo_ref)
    first, has_low, has_high = position("gy")
    out_wire = []
    for j in range(wide + 2):
        low, high = from_sides(first, ye_ref[2 * wide + j], yo_ref[2 * wide + j])
        low = jnp.where(has_low, low, 0.0)
        high = jnp.where(has_high, high, 0.0)
        own = wire[j]
        side = jnp.where(row < 4, high, low)
        beyond = jnp.where(row < 4, low, high)
        out_wire.append((own, side))
        for g, ref in enumerate((gp_ref, gt_ref)):
            ref[j, 0] = lookup(roots[g], own)
            ref[j, 1] = lookup(roots[g], side)
            ref[j, 2] = lookup(roots[g], beyond)
    for i in range(wide):
        j = i + 1
        stores = []
        for pair in range(2):
            low, high = from_sides(first, ye_ref[pair * wide + i], yo_ref[pair * wide + i])
            stores.append(jnp.where(row < 4, high, low))
            stores.append(half_turn(jnp.where(row < 4, low, high)))
        diagonals = []
        for ref in (gp_ref, gt_ref):
            beyond = ref[j, 2]
            own_sum, side_sum = along_y(ref[j, 0], ref[j, 1], row, up_y(beyond), down_y(beyond))
            own_sum = own_sum + along_z(ref[j, 0], spot) + (ref[j - 1, 0] + ref[j + 1, 0])
            side_sum = side_sum + along_z(ref[j, 1], spot) + (ref[j - 1, 1] + ref[j + 1, 1])
            diagonals.append((ref[j, 0] * own_sum, ref[j, 1] * side_sum))
        for tile in range(2):
            if tile == 0:
                press, cross, lower, heat = (fields[k][i] for k in range(4))
            else:
                press, cross, lower, heat = stores
            outside = jnp.where(out_wire[j][tile] > 0.0, 0.0, 1.0)
            gp, gt = gp_ref[j, tile], gt_ref[j, tile]
            a = press + diagonals[0][tile] + outside
            d = heat + diagonals[1][tile] + outside
            inverse = 1.0 / (a * d + cross * lower)
            pp, pt, tt = gp * gp, gp * gt, gt * gt
            coeff_ref[0, i, tile] = pp * d * inverse
            coeff_ref[1, i, tile] = pt * cross * inverse
            coeff_ref[2, i, tile] = -pt * lower * inverse
            coeff_ref[3, i, tile] = tt * a * inverse
            if tile == 0 and MARGIN <= i < wide - MARGIN:
                x = i - MARGIN
                over_p, over_t = 1.0 / gp, 1.0 / gt
                over = over_p * over_t
                image_ref[0, x] = a * (over_p * over_p)
                image_ref[1, x] = -cross * over
                image_ref[2, x] = lower * over
                image_ref[3, x] = d * (over_t * over_t)
                scale_ref[0, x] = gp
                scale_ref[1, x] = gt
                scale_ref[2, x] = over_p
                scale_ref[3, x] = over_t
                scale_ref[4, x] = lookup(tables[2], out_wire[j][0])
                rhs_ref[0, x] = source_ref[0, x] * over_p
                rhs_ref[1, x] = source_ref[1, x] * over_t
    subdomain_sweeps(rhs_ref, coeff_ref, solved_ref, even_ref, odd_ref, buffers, rows)


def fold_y_kernel(solved_ref, ye_ref, yo_ref, summed_ref, even_ref, odd_ref):
    wide = solved_ref.shape[1]
    row = sublane()
    first, has_low, has_high = position("gy")
    for k in range(2):
        for i in range(wide):
            low, high = from_sides(first, ye_ref[k, i], yo_ref[k, i])
            low = jnp.where(has_low, low, 0.0)
            high = jnp.where(has_high, high, 0.0)
            summed_ref[k, i, 0] = solved_ref[k, i, 0] + jnp.where(row < 4, low, high)
            summed_ref[k, i, 1] = solved_ref[k, i, 1] + jnp.where(row < 4, high, low)
    first, _, _ = position("gx")
    margin_even = jnp.where(first, wide - MARGIN, 0)
    margin_odd = jnp.where(first, 0, wide - MARGIN)
    rim_even = jnp.where(first, wide - MARGIN - 1, MARGIN)
    rim_odd = jnp.where(first, MARGIN, wide - MARGIN - 1)
    for k in range(2):
        for ref, margin, rim in ((even_ref, margin_even, rim_even), (odd_ref, margin_odd, rim_odd)):
            for tile in range(2):
                ref[k, pl.ds(tile * MARGIN, MARGIN)] = summed_ref[k, pl.ds(margin, MARGIN), tile]
            ref[k, 2 * MARGIN] = summed_ref[k, rim, 0]


def fold_x(summed_ref, xe_ref, xo_ref, field_refs):
    wide = summed_ref.shape[1]
    rows = wide - 2 * MARGIN
    first, has_low, has_high = position("gx")
    for k in range(2):
        low, high = from_sides(first, xe_ref[k], xo_ref[k])
        low = jnp.where(has_low, low, 0.0)
        high = jnp.where(has_high, high, 0.0)
        for x in range(-1, rows + 1):
            for tile in range(2):
                value = summed_ref[k, x + MARGIN, tile]
                if 0 <= x < MARGIN:
                    value = value + low[tile * MARGIN + x]
                if rows - MARGIN <= x < rows:
                    value = value + high[tile * MARGIN + x - (rows - MARGIN)]
                if tile == 0 and x == -1:
                    value = value + low[2 * MARGIN]
                if tile == 0 and x == rows:
                    value = value + high[2 * MARGIN]
                field_refs[k][x + 1, tile] = value


def image_row(field_refs, image_ref, x, row, spot):
    sums = []
    for ref in field_refs:
        own = ref[x + 1, 0]
        total = along_y_own(own, ref[x + 1, 1], row) + along_z(own, spot)
        sums.append(total + (ref[x, 0] + ref[x + 2, 0]))
    flow, heat = field_refs[0][x + 1, 0], field_refs[1][x + 1, 0]
    return (
        image_ref[0, x] * flow + image_ref[1, x] * heat - sums[0],
        image_ref[2, x] * flow + image_ref[3, x] * heat - sums[1],
    )


def keep_direction(direction_ref, scale_ref, field_refs, x):
    heat = field_refs[1][x + 1, 0] * scale_ref[3, x]
    direction_ref[1, x] = heat
    direction_ref[0, x] = field_refs[0][x + 1, 0] * scale_ref[2, x] - scale_ref[4, x] * heat


def gram_rows(pairs, row, offset):
    total = jnp.zeros(TILE, F32)
    for index, value in enumerate(pairs):
        line = jnp.broadcast_to(jnp.sum(value, axis=0, keepdims=True), TILE)
        total = total + jnp.where(row == index + offset, line, 0.0)
    return total


def step_kernel(
    summed_ref, xe_ref, xo_ref, coeff_ref, image_ref, scale_ref, source_ref,
    direction_ref, power_ref, gram_ref, solved_ref, even_ref, odd_ref,
    rhs_ref, q_ref, t_ref, *buffers,
):
    rows = source_ref.shape[1]
    row, spot = sublane(), lane()
    fields = (q_ref, t_ref)
    fold_x(summed_ref, xe_ref, xo_ref, fields)
    products = [jnp.zeros(TILE, F32) for _ in range(3)]
    for x in range(rows):
        keep_direction(direction_ref, scale_ref, fields, x)
        for k, part in enumerate(image_row(fields, image_ref, x, row, spot)):
            source = source_ref[k, x]
            scaled = part - source * scale_ref[2 + k, x]
            power = scaled * scale_ref[k, x]
            rhs_ref[k, x] = scaled
            power_ref[k, x] = power
            products[0] = products[0] + source * source
            products[1] = products[1] + source * power
            products[2] = products[2] + power * power
    gram_ref[...] = gram_rows(products, row, 0)
    subdomain_sweeps(rhs_ref, coeff_ref, solved_ref, even_ref, odd_ref, buffers, rows)


def last_kernel(
    summed_ref, xe_ref, xo_ref, image_ref, scale_ref, source_ref, power_ref, gram_in_ref,
    direction_ref, second_ref, gram_ref, q_ref, t_ref,
):
    rows = source_ref.shape[1]
    row, spot = sublane(), lane()
    fields = (q_ref, t_ref)
    fold_x(summed_ref, xe_ref, xo_ref, fields)
    products = [jnp.zeros(TILE, F32) for _ in range(3)]
    for x in range(rows):
        keep_direction(direction_ref, scale_ref, fields, x)
        for k, part in enumerate(image_row(fields, image_ref, x, row, spot)):
            power = power_ref[k, x]
            second = part * scale_ref[k, x] - power
            second_ref[k, x] = second
            products[0] = products[0] + source_ref[k, x] * second
            products[1] = products[1] + power * second
            products[2] = products[2] + second * second
    total = gram_in_ref[...] + gram_rows(products, row, 3)
    for device in range(gram_ref.shape[0]):
        gram_ref[device] = total


def combine_kernel(
    gram_ref, source_ref, power_ref, second_ref, one_ref, two_ref,
    adjoint_ref, residual_ref, basis_ref, *, scale,
):
    parts = [gram_ref[device] for device in range(gram_ref.shape[0])]
    while len(parts) > 1:
        parts = [parts[i] + parts[i + 1] if i + 1 < len(parts) else parts[i] for i in range(0, len(parts), 2)]
    sums = jnp.broadcast_to(jnp.sum(parts[0], axis=1, keepdims=True), TILE)
    g00, g01, g11, g02, g12, g22 = (sums[k : k + 1] for k in range(6))
    beta2 = g00 + EPSILON
    beta = jnp.sqrt(beta2)
    less = (EPSILON - g01) / beta2
    h11 = (g00 + g01) / beta2
    square = (less * less * g00 + 2.0 * less * g01 + g11) / beta2
    square = jnp.maximum(square, 0.0)
    h21 = jnp.sqrt(square + EPSILON)
    b = 1.0 / (beta * h21)
    a = less * b
    h12 = EPSILON * h11 / (beta2 * h21) + (a * g01 + b * g02) / beta
    short = EPSILON / (square + EPSILON) - (a * a * g01 + a * b * (g11 + g02) + b * b * g12)
    h22 = 1.0 - short
    c0 = a * short - h12 / beta
    c1 = a + b * short
    c2 = b
    square = c0 * (c0 * g00 + 2.0 * (c1 * g01 + c2 * g02)) + c1 * (c1 * g11 + 2.0 * c2 * g12) + c2 * c2 * g22
    h32 = jnp.sqrt(jnp.maximum(square, 0.0) + EPSILON)
    n0, n1, n2 = h21 * h32, -h11 * h32, h11 * h22 - h12 * h21
    factor = beta * n0 / (n0 * n0 + n1 * n1 + n2 * n2)
    f0, f1, f2 = factor * n0, factor * n1, factor * n2
    y2 = -f2 / h32
    y1 = (h11 * (beta - f0 - h12 * y2) - h21 * (f1 + h22 * y2)) / (h11 * h11 + h21 * h21)
    over = 1.0 / h32
    v0, v1, v2 = c0 * over, c1 * over, c2 * over
    wide = lambda value: jnp.broadcast_to(value, TILE)
    z_one, z_two = wide(y1 / beta + y2 * a), wide(y2 * b)
    r0, r1, r2 = wide(f0 / beta + f1 * a + f2 * v0), wide(f1 * b + f2 * v1), wide(f2 * v2)
    s0, s1, s2 = wide(scale * v0), wide(scale * v1), wide(scale * v2)
    for k in range(2):
        for x in range(source_ref.shape[1]):
            source, power, second = source_ref[k, x], power_ref[k, x], second_ref[k, x]
            adjoint_ref[k, x] = z_one * one_ref[k, x] + z_two * two_ref[k, x]
            residual_ref[k, x] = r0 * source + r1 * power + r2 * second
            basis_ref[k, x] = s0 * source + s1 * power + s2 * second


def call(kernel, outs, scratch=(), name=None):
    def run(*args):
        return pl.pallas_call(
            kernel,
            out_shape=[jax.ShapeDtypeStruct(shape, F32) for shape in outs],
            in_specs=[pl.BlockSpec(memory_space=pltpu.VMEM)] * len(args),
            out_specs=[pl.BlockSpec(memory_space=pltpu.VMEM)] * len(outs),
            scratch_shapes=[pltpu.VMEM(shape, F32) for shape in scratch],
            compiler_params=pltpu.CompilerParams(vmem_limit_bytes=32 * 1024 * 1024),
            name=name,
        )(*args)

    return run


def exchange(axis, even, odd):
    n_x, n_y = lax.axis_size("gx"), lax.axis_size("gy")
    count = lax.axis_size(axis)
    pairs = [(i, i ^ 1) for i in range(count)]
    others = []
    for x in range(n_x):
        for y in range(n_y):
            place = x if axis == "gx" else y
            if 0 < place < count - 1:
                partner = ((place - 1) ^ 1) + 1
                target = (partner, y) if axis == "gx" else (x, partner)
            else:
                target = (x, y ^ 1) if axis == "gx" else (x ^ 1, y)
            others.append((x * n_y + y, target[0] * n_y + target[1]))
    return lax.ppermute(even, axis, pairs), lax.ppermute(odd, ("gx", "gy"), others)


def shards(adjoint_source, storage, soil_ids, bc_mask, soil_props):
    rows, _, depth = soil_ids.shape
    wide = rows + 2 * MARGIN
    devices = lax.axis_size("gx") * lax.axis_size("gy")
    cells = 2.0 * rows * soil_ids.shape[1] * depth * devices
    own = (rows, *TILE)
    slab = (4 * MARGIN + RIM, *TILE)
    fields, wire, even, odd = call(pack_x_kernel, [(4, *own), own, slab, slab], name="pack_x")(
        soil_props, storage, soil_ids, bc_mask
    )
    xe, xo = exchange("gx", even, odd)
    slab = (3 * wide + 2, *TILE)
    even, odd = call(pack_y_kernel, [slab, slab], name="pack_y")(fields, wire, xe, xo)
    ye, yo = exchange("gy", even, odd)
    buffers = [(wide + 2, 2, *TILE)] * 4
    solved_shapes = [(2, wide, 2, *TILE), (2, wide, *TILE), (2, wide, *TILE)]
    coeff, image, scales, solved, even, odd = call(
        coefficients_kernel,
        [(4, wide, 2, *TILE), (4, *own), (5, *own)] + solved_shapes,
        [(wide + 2, 3, *TILE)] * 2 + [(2, *own)] + buffers,
        name="first_solve",
    )(soil_props, fields, wire, xe, xo, ye, yo, adjoint_source)

    fold_shapes = [(2, wide, 2, *TILE)] + [(2, 2 * MARGIN + 1, *TILE)] * 2
    ye, yo = exchange("gy", even, odd)
    summed, even, odd = call(fold_y_kernel, fold_shapes, name="fold_y")(solved, ye, yo)
    xe, xo = exchange("gx", even, odd)
    halo = [(rows + 2, 2, *TILE)] * 2
    one, power, gram, solved, even, odd = call(
        step_kernel,
        [(2, *own), (2, *own), TILE] + solved_shapes,
        [(2, *own)] + halo + buffers,
        name="second_solve",
    )(summed, xe, xo, coeff, image, scales, adjoint_source)

    ye, yo = exchange("gy", even, odd)
    summed, even, odd = call(fold_y_kernel, fold_shapes, name="fold_y")(solved, ye, yo)
    xe, xo = exchange("gx", even, odd)
    two, second, gram = call(
        last_kernel, [(2, *own), (2, *own), (devices, *TILE)], halo, name="last_image"
    )(summed, xe, xo, image, scales, adjoint_source, power, gram)
    gram = lax.all_to_all(gram, ("gx", "gy"), 0, 0)
    return tuple(
        call(
            functools.partial(combine_kernel, scale=math.sqrt(cells)), [(2, *own)] * 3, name="combine"
        )(gram, adjoint_source, power, second, one, two)
    )


def solution(mesh):
    in_specs = (
        P(None, "gx", "gy", None),
        P(None, "gx", "gy", None),
        P("gx", "gy", None),
        P("gx", "gy"),
        P(),
    )
    out_specs = (P(None, "gx", "gy", None), P(None, "gx", "gy", None), P(None, "gx", "gy", None))
    return jax.shard_map(shards, mesh=mesh, in_specs=in_specs, out_specs=out_specs, check_vma=False)
```

```python
import functools
import math

import jax
import jax.numpy as jnp
from jax import lax
from jax.experimental import pallas as pl
from jax.experimental.pallas import tpu as pltpu
from jax.sharding import PartitionSpec as P

MARGIN = 4
SWEEPS = 6
SUB = 8
LANE = 128
TILE = (SUB, LANE)
RIM = MARGIN + 1
EPSILON = 1e-06
F32 = jnp.float32


def sublane():
    return lax.broadcasted_iota(jnp.int32, TILE, 0)


def lane():
    return lax.broadcasted_iota(jnp.int32, TILE, 1)


def up_y(tile):
    return pltpu.roll(tile, SUB - 1, 0)


def down_y(tile):
    return pltpu.roll(tile, 1, 0)


def half_turn(tile):
    return pltpu.roll(tile, SUB // 2, 0)


def along_z(tile, spot):
    above = jnp.where(spot == LANE - 1, 0.0, pltpu.roll(tile, LANE - 1, 1))
    below = jnp.where(spot == 0, 0.0, pltpu.roll(tile, 1, 1))
    return above + below


def along_y(own, side, row, last_up, last_down):
    own_up, own_down = up_y(own), down_y(own)
    side_up, side_down = up_y(side), down_y(side)
    own_sum = jnp.where(row == 7, side_up, own_up) + jnp.where(row == 0, side_down, own_down)
    side_sum = jnp.where(row == 7, own_up, jnp.where(row == 3, last_up, side_up))
    side_sum = side_sum + jnp.where(row == 0, own_down, jnp.where(row == 4, last_down, side_down))
    return own_sum, side_sum


def position(axis):
    place = lax.axis_index(axis)
    first = lax.rem(place, 2) == 0
    return first, place > 0, place < lax.axis_size(axis) - 1


def from_sides(first, even, odd):
    return jnp.where(first, odd, even), jnp.where(first, even, odd)


def lookup(table, wire):
    index = jnp.maximum(wire.astype(jnp.int32) - 1, 0)
    return jnp.where(wire > 0.0, jnp.take_along_axis(table, index, axis=1), 0.0)


def wide_tables(props_ref):
    pad = jnp.zeros((props_ref.shape[0], LANE - props_ref.shape[1]), F32)
    wide = jnp.concatenate([props_ref[...], pad], axis=1)
    return [jnp.broadcast_to(wide[k : k + 1], TILE) for k in range(3)]


def pack_x_kernel(
    props_hbm, storage_hbm, ids_hbm, bc_hbm, fields_ref, wire_ref, even_ref, odd_ref,
    props_ref, storage_ref, ids_ref, bc_ref, sems,
):
    places = ((ids_hbm, ids_ref), (storage_hbm, storage_ref), (props_hbm, props_ref), (bc_hbm, bc_ref))
    copies = [pltpu.make_async_copy(src, dst, sems.at[k]) for k, (src, dst) in enumerate(places)]
    for copy in copies:
        copy.start()
    rows = ids_ref.shape[0]
    spot = lane()
    for copy in copies:
        copy.wait()
    tables = wide_tables(props_ref)
    for x in range(rows):
        wire = (ids_ref[x] + 1).astype(F32)
        wire_ref[x] = wire
        kp = lookup(tables[0], wire)
        carried = lookup(tables[2], wire)
        held = jnp.broadcast_to(bc_ref[:, x : x + 1].astype(F32), TILE)
        bound = jnp.where(spot == LANE - 1, 2.0 * kp * held, 0.0)
        press = storage_ref[0, x]
        lower = storage_ref[1, x]
        fields_ref[0, x] = press + bound
        fields_ref[1, x] = carried * press - storage_ref[2, x]
        fields_ref[2, x] = lower
        fields_ref[3, x] = storage_ref[3, x] - carried * lower
    first, _, _ = position("gx")
    high, low = rows - MARGIN, 0
    start_even = jnp.where(first, high, low)
    start_odd = jnp.where(first, low, high)
    wire_even = jnp.where(first, rows - RIM, 0)
    wire_odd = jnp.where(first, 0, rows - RIM)
    for k in range(4):
        even_ref[pl.ds(k * MARGIN, MARGIN)] = fields_ref[k, pl.ds(start_even, MARGIN)]
        odd_ref[pl.ds(k * MARGIN, MARGIN)] = fields_ref[k, pl.ds(start_odd, MARGIN)]
    even_ref[pl.ds(4 * MARGIN, RIM)] = wire_ref[pl.ds(wire_even, RIM)]
    odd_ref[pl.ds(4 * MARGIN, RIM)] = wire_ref[pl.ds(wire_odd, RIM)]


def widen_x(fields_ref, wire_ref, even_ref, odd_ref):
    rows = wire_ref.shape[0]
    first, has_low, has_high = position("gx")
    fields = []
    for k in range(4):
        low, high = from_sides(
            first, even_ref[pl.ds(k * MARGIN, MARGIN)], odd_ref[pl.ds(k * MARGIN, MARGIN)]
        )
        fields.append(
            [low[i] for i in range(MARGIN)]
            + [fields_ref[k, x] for x in range(rows)]
            + [high[i] for i in range(MARGIN)]
        )
    low, high = from_sides(
        first, even_ref[pl.ds(4 * MARGIN, RIM)], odd_ref[pl.ds(4 * MARGIN, RIM)]
    )
    low = jnp.where(has_low, low, 0.0)
    high = jnp.where(has_high, high, 0.0)
    wire = (
        [low[i] for i in range(RIM)] + [wire_ref[x] for x in range(rows)] + [high[i] for i in range(RIM)]
    )
    return fields, wire


def rim_rows(even_ref, odd_ref, base, tiles, rows_even, rows_odd):
    for j, (tile_ref, index) in enumerate(tiles):
        line = (base + j // SUB, pl.ds(j % SUB, 1))
        even_ref[line] = tile_ref[(*index, pl.ds(rows_even, 1))]
        odd_ref[line] = tile_ref[(*index, pl.ds(rows_odd, 1))]


def pack_y_kernel(fields_ref, wire_ref, xe_ref, xo_ref, even_ref, odd_ref, all_wire_ref):
    fields, wire = widen_x(fields_ref, wire_ref, xe_ref, xo_ref)
    wide = len(fields[0])
    first, _, _ = position("gy")
    even_low = (sublane() < 4) != first

    def put(spot, one, other):
        other = half_turn(other)
        even_ref[spot] = jnp.where(even_low, one, other)
        odd_ref[spot] = jnp.where(even_low, other, one)

    for pair in range(2):
        for i in range(wide):
            put(pair * wide + i, fields[2 * pair][i], fields[2 * pair + 1][i])
    half = wide // 2 + 1
    for j in range(half):
        put(2 * wide + j, wire[j], wire[j + half])
    for j in range(2 * half):
        all_wire_ref[j] = wire[j]
    rows_even, rows_odd = jnp.where(first, 3, 4), jnp.where(first, 4, 3)
    spots = [(all_wire_ref, (j,)) for j in range(2 * half)]
    last = even_ref.shape[0] - 1
    even_ref[last] = odd_ref[last] = jnp.zeros(TILE, F32)
    rim_rows(even_ref, odd_ref, 2 * wide + half, spots, rows_even, rows_odd)


def sweep_row(q_ref, t_ref, coeff_ref, j, row, spot, rhs):
    sums = []
    for ref in (q_ref, t_ref):
        own, side = ref[j, 0], ref[j, 1]
        own_sum, side_sum = along_y(own, side, row, 0.0, 0.0)
        own_sum = own_sum + (along_z(own, spot) + (ref[j - 1, 0] + ref[j + 1, 0]))
        side_sum = side_sum + (along_z(side, spot) + (ref[j - 1, 1] + ref[j + 1, 1]))
        sums.append([own_sum, side_sum])
    if rhs is not None:
        sums[0][0] = sums[0][0] + rhs[0]
        sums[1][0] = sums[1][0] + rhs[1]
    out = []
    for tile in range(2):
        flow, heat = sums[0][tile], sums[1][tile]
        out.append(
            (
                coeff_ref[0, j - 1, tile] * flow + coeff_ref[1, j - 1, tile] * heat,
                coeff_ref[2, j - 1, tile] * flow + coeff_ref[3, j - 1, tile] * heat,
            )
        )
    return out


def subdomain_sweeps(rhs_ref, coeff_ref, solved_ref, rims_ref, even_ref, odd_ref, buffers, rows):
    row, spot = sublane(), lane()
    wide = rows + 2 * MARGIN
    zero = jnp.zeros(TILE, F32)
    for buffer in buffers:
        for j in range(wide + 2):
            for tile in range(2):
                buffer[j, tile] = zero
    current, following = buffers[:2], buffers[2:]
    for x in range(rows):
        j = x + RIM
        flow, heat = rhs_ref[0, x], rhs_ref[1, x]
        current[0][j, 0] = coeff_ref[0, j - 1, 0] * flow + coeff_ref[1, j - 1, 0] * heat
        current[1][j, 0] = coeff_ref[2, j - 1, 0] * flow + coeff_ref[3, j - 1, 0] * heat
    first, _, _ = position("gy")
    even_low = (row < 4) != first
    for sweep in range(1, SWEEPS):
        reach = min(sweep, MARGIN)
        for x in range(-reach, rows + reach):
            j = x + RIM
            rhs = (rhs_ref[0, x], rhs_ref[1, x]) if 0 <= x < rows else None
            out = sweep_row(current[0], current[1], coeff_ref, j, row, spot, rhs)
            if sweep < SWEEPS - 1:
                for tile in range(2):
                    following[0][j, tile] = out[tile][0]
                    following[1][j, tile] = out[tile][1]
            else:
                i = j - 1
                (own_q, own_t), (side_q, side_t) = out
                solved_ref[0, i], solved_ref[1, i] = own_q, own_t
                turned = half_turn(side_t)
                even_ref[i] = jnp.where(even_low, turned, side_q)
                odd_ref[i] = jnp.where(even_low, side_q, turned)
                for k, side in enumerate((side_q, side_t)):
                    line = (i // SUB, pl.ds(i % SUB, 1))
                    rims_ref[(2 * k, *line)] = side[7:8]
                    rims_ref[(2 * k + 1, *line)] = side[0:1]
        current, following = following, current
    rows_even, rows_odd = jnp.where(first, 7, 0), jnp.where(first, 0, 7)
    for k in range(2):
        spots = [(solved_ref, (k, i)) for i in range(wide)]
        rim_rows(even_ref, odd_ref, wide + k * (wide // SUB), spots, rows_even, rows_odd)


def coefficients_kernel(
    props_ref, fields_ref, wire_ref, xe_ref, xo_ref, ye_ref, yo_ref, source_ref,
    coeff_ref, image_ref, scale_ref, solved_ref, rims_ref, even_ref, odd_ref,
    gp_ref, gt_ref, beyond_ref, rhs_ref, *buffers,
):
    rows = wire_ref.shape[0]
    wide = rows + 2 * MARGIN
    row, spot = sublane(), lane()
    tables = wide_tables(props_ref)
    roots = [jnp.sqrt(jnp.maximum(tables[0], 0.0)), jnp.sqrt(jnp.maximum(tables[1], 0.0))]
    fields, wire = widen_x(fields_ref, wire_ref, xe_ref, xo_ref)
    first, has_low, has_high = position("gy")
    half = wide // 2 + 1
    sides = []
    for j in range(half):
        low, high = from_sides(first, ye_ref[2 * wide + j], yo_ref[2 * wide + j])
        low = jnp.where(has_low, low, 0.0)
        high = jnp.where(has_high, high, 0.0)
        sides.append((jnp.where(row < 4, high, low), half_turn(jnp.where(row < 4, low, high))))
    sides = [side[0] for side in sides] + [side[1] for side in sides]
    for tile in range(beyond_ref.shape[2]):
        ends = from_sides(first, ye_ref[2 * wide + half + tile], yo_ref[2 * wide + half + tile])
        for end, (there, value) in enumerate(zip((has_low, has_high), ends)):
            value = jnp.where(there, value, 0.0)
            for g in range(2):
                beyond_ref[g, end, tile] = lookup(roots[g], value)
    out_wire = list(zip(wire, sides))
    for j in range(wide + 2):
        for g, ref in enumerate((gp_ref, gt_ref)):
            ref[j, 0] = lookup(roots[g], wire[j])
            ref[j, 1] = lookup(roots[g], sides[j])
    for i in range(wide):
        j = i + 1
        stores = []
        for pair in range(2):
            low, high = from_sides(first, ye_ref[pair * wide + i], yo_ref[pair * wide + i])
            stores.append(jnp.where(row < 4, high, low))
            stores.append(half_turn(jnp.where(row < 4, low, high)))
        diagonals = []
        for g, ref in enumerate((gp_ref, gt_ref)):
            last_down, last_up = (
                jnp.broadcast_to(beyond_ref[g, end, j // SUB, pl.ds(j % SUB, 1)], TILE) for end in range(2)
            )
            own_sum, side_sum = along_y(ref[j, 0], ref[j, 1], row, last_up, last_down)
            own_sum = own_sum + along_z(ref[j, 0], spot) + (ref[j - 1, 0] + ref[j + 1, 0])
            side_sum = side_sum + along_z(ref[j, 1], spot) + (ref[j - 1, 1] + ref[j + 1, 1])
            diagonals.append((ref[j, 0] * own_sum, ref[j, 1] * side_sum))
        for tile in range(2):
            if tile == 0:
                press, cross, lower, heat = (fields[k][i] for k in range(4))
            else:
                press, cross, lower, heat = stores
            outside = jnp.where(out_wire[j][tile] > 0.0, 0.0, 1.0)
            gp, gt = gp_ref[j, tile], gt_ref[j, tile]
            a = press + diagonals[0][tile] + outside
            d = heat + diagonals[1][tile] + outside
            inverse = 1.0 / (a * d + cross * lower)
            pp, pt, tt = gp * gp, gp * gt, gt * gt
            coeff_ref[0, i, tile] = pp * d * inverse
            coeff_ref[1, i, tile] = pt * cross * inverse
            coeff_ref[2, i, tile] = -pt * lower * inverse
            coeff_ref[3, i, tile] = tt * a * inverse
            if tile == 0 and MARGIN <= i < wide - MARGIN:
                x = i - MARGIN
                over_p, over_t = 1.0 / gp, 1.0 / gt
                over = over_p * over_t
                image_ref[0, x] = a * (over_p * over_p)
                image_ref[1, x] = -cross * over
                image_ref[2, x] = lower * over
                image_ref[3, x] = d * (over_t * over_t)
                scale_ref[0, x] = gp
                scale_ref[1, x] = gt
                scale_ref[2, x] = over_p
                scale_ref[3, x] = over_t
                scale_ref[4, x] = lookup(tables[2], out_wire[j][0])
                rhs_ref[0, x] = source_ref[0, x] * over_p
                rhs_ref[1, x] = source_ref[1, x] * over_t
    subdomain_sweeps(rhs_ref, coeff_ref, solved_ref, rims_ref, even_ref, odd_ref, buffers, rows)


def fold_y_kernel(solved_ref, rims_ref, ye_ref, yo_ref, summed_ref, edges_ref, even_ref, odd_ref):
    wide = solved_ref.shape[1]
    row = sublane()
    first, has_low, has_high = position("gy")
    for i in range(wide):
        low, high = from_sides(first, ye_ref[i], yo_ref[i])
        low = jnp.where(has_low, low, 0.0)
        high = jnp.where(has_high, high, 0.0)
        summed_ref[0, i] = solved_ref[0, i] + jnp.where(row < 4, low, high)
        summed_ref[1, i] = solved_ref[1, i] + half_turn(jnp.where(row < 4, high, low))
    count = wide // SUB
    for k in range(2):
        for tile in range(count):
            spot = wide + k * count + tile
            low, high = from_sides(first, ye_ref[spot], yo_ref[spot])
            edges_ref[2 * k, tile] = rims_ref[2 * k, tile] + jnp.where(has_low, low, 0.0)
            edges_ref[2 * k + 1, tile] = rims_ref[2 * k + 1, tile] + jnp.where(has_high, high, 0.0)
    first, _, _ = position("gx")
    margin_even = jnp.where(first, wide - MARGIN, 0)
    margin_odd = jnp.where(first, 0, wide - MARGIN)
    rim_even = jnp.where(first, wide - MARGIN - 1, MARGIN)
    rim_odd = jnp.where(first, MARGIN, wide - MARGIN - 1)
    for k in range(2):
        base = k * (MARGIN + 2)
        for ref, margin, rim in ((even_ref, margin_even, rim_even), (odd_ref, margin_odd, rim_odd)):
            ref[pl.ds(base, MARGIN)] = summed_ref[k, pl.ds(margin, MARGIN)]
            ref[base + MARGIN] = summed_ref[k, rim]
        to_low = jnp.where(row < 4, edges_ref[2 * k, 0], half_turn(edges_ref[2 * k + 1, 0]))
        last = count - 1
        to_high = jnp.where(row < 4, half_turn(edges_ref[2 * k + 1, last]), edges_ref[2 * k, last])
        even_ref[base + MARGIN + 1] = jnp.where(first, to_high, to_low)
        odd_ref[base + MARGIN + 1] = jnp.where(first, to_low, to_high)


def fold_x(summed_ref, edges_ref, xe_ref, xo_ref, field_refs, edge_ref):
    wide = summed_ref.shape[1]
    rows = wide - 2 * MARGIN
    row = sublane()
    first, has_low, has_high = position("gx")
    for k in range(2):
        base = k * (MARGIN + 2)
        low, high = from_sides(first, xe_ref[pl.ds(base, MARGIN + 2)], xo_ref[pl.ds(base, MARGIN + 2)])
        low = jnp.where(has_low, low, 0.0)
        high = jnp.where(has_high, high, 0.0)
        for x in range(-1, rows + 1):
            value = summed_ref[k, x + MARGIN]
            if 0 <= x < MARGIN:
                value = value + low[x]
            if rows - MARGIN <= x < rows:
                value = value + high[x - (rows - MARGIN)]
            if x == -1:
                value = value + low[MARGIN]
            if x == rows:
                value = value + high[MARGIN]
            field_refs[k][x + 1] = value
        from_low, from_high = low[MARGIN + 1], high[MARGIN + 1]
        last = edge_ref.shape[1] - 1
        for end in range(2):
            for tile in range(last + 1):
                value = edges_ref[2 * k + end, tile]
                if tile == 0:
                    part = half_turn(from_low) if end == 1 else from_low
                    value = value + jnp.where(row < 4, 0.0, part)
                if tile == last:
                    part = half_turn(from_high) if end == 1 else from_high
                    value = value + jnp.where(row < 4, part, 0.0)
                edge_ref[2 * k + end, tile] = value


def image_row(field_refs, edge_ref, image_ref, x, row, spot):
    sums = []
    i = x + MARGIN
    for k, ref in enumerate(field_refs):
        own = ref[x + 1]
        down, up = (
            jnp.broadcast_to(edge_ref[2 * k + end, i // SUB, pl.ds(i % SUB, 1)], TILE) for end in range(2)
        )
        total = jnp.where(row == 7, up, up_y(own)) + jnp.where(row == 0, down, down_y(own))
        sums.append(total + along_z(own, spot) + (ref[x] + ref[x + 2]))
    flow, heat = field_refs[0][x + 1], field_refs[1][x + 1]
    return (
        image_ref[0, x] * flow + image_ref[1, x] * heat - sums[0],
        image_ref[2, x] * flow + image_ref[3, x] * heat - sums[1],
    )


def keep_direction(direction_ref, scale_ref, field_refs, x):
    heat = field_refs[1][x + 1] * scale_ref[3, x]
    direction_ref[1, x] = heat
    direction_ref[0, x] = field_refs[0][x + 1] * scale_ref[2, x] - scale_ref[4, x] * heat


def gram_rows(pairs, row, offset):
    total = jnp.zeros(TILE, F32)
    for index, value in enumerate(pairs):
        line = jnp.broadcast_to(jnp.sum(value, axis=0, keepdims=True), TILE)
        total = total + jnp.where(row == index + offset, line, 0.0)
    return total


def step_kernel(
    summed_ref, edges_ref, xe_ref, xo_ref, coeff_ref, image_ref, scale_ref, source_ref,
    direction_ref, power_ref, gram_ref, solved_ref, rims_ref, even_ref, odd_ref,
    rhs_ref, q_ref, t_ref, edge_ref, *buffers,
):
    rows = source_ref.shape[1]
    row, spot = sublane(), lane()
    fields = (q_ref, t_ref)
    fold_x(summed_ref, edges_ref, xe_ref, xo_ref, fields, edge_ref)
    products = [jnp.zeros(TILE, F32) for _ in range(3)]
    for x in range(rows):
        keep_direction(direction_ref, scale_ref, fields, x)
        for k, part in enumerate(image_row(fields, edge_ref, image_ref, x, row, spot)):
            source = source_ref[k, x]
            scaled = part - source * scale_ref[2 + k, x]
            power = scaled * scale_ref[k, x]
            rhs_ref[k, x] = scaled
            power_ref[k, x] = power
            products[0] = products[0] + source * source
            products[1] = products[1] + source * power
            products[2] = products[2] + power * power
    gram_ref[...] = gram_rows(products, row, 0)
    subdomain_sweeps(rhs_ref, coeff_ref, solved_ref, rims_ref, even_ref, odd_ref, buffers, rows)


def last_kernel(
    summed_ref, edges_ref, xe_ref, xo_ref, image_ref, scale_ref, source_ref, power_ref, gram_in_ref,
    direction_ref, second_ref, gram_ref, q_ref, t_ref, edge_ref,
):
    rows = source_ref.shape[1]
    row, spot = sublane(), lane()
    fields = (q_ref, t_ref)
    fold_x(summed_ref, edges_ref, xe_ref, xo_ref, fields, edge_ref)
    products = [jnp.zeros(TILE, F32) for _ in range(3)]
    for x in range(rows):
        keep_direction(direction_ref, scale_ref, fields, x)
        for k, part in enumerate(image_row(fields, edge_ref, image_ref, x, row, spot)):
            power = power_ref[k, x]
            second = part * scale_ref[k, x] - power
            second_ref[k, x] = second
            products[0] = products[0] + source_ref[k, x] * second
            products[1] = products[1] + power * second
            products[2] = products[2] + second * second
    total = jnp.sum(gram_in_ref[...] + gram_rows(products, row, 3), axis=1, keepdims=True)
    line = jnp.sum(jnp.where(row == spot, jnp.broadcast_to(total, TILE), 0.0), axis=0, keepdims=True)
    gram_ref[...] = jnp.broadcast_to(line, gram_ref.shape)


def combine_kernel(
    gram_ref, source_ref, power_ref, second_ref, one_ref, two_ref,
    adjoint_hbm, residual_hbm, basis_hbm, adjoint_ref, residual_ref, basis_ref, sems, *, scale,
):
    sums = jnp.sum(gram_ref[...], axis=0, keepdims=True)
    spot = lax.broadcasted_iota(jnp.int32, sums.shape, 1)
    g00, g01, g11, g02, g12, g22 = (
        jnp.sum(jnp.where(spot == k, sums, 0.0), axis=1, keepdims=True) for k in range(6)
    )
    beta2 = g00 + EPSILON
    beta = jnp.sqrt(beta2)
    less = (EPSILON - g01) / beta2
    h11 = (g00 + g01) / beta2
    square = (less * less * g00 + 2.0 * less * g01 + g11) / beta2
    square = jnp.maximum(square, 0.0)
    h21 = jnp.sqrt(square + EPSILON)
    b = 1.0 / (beta * h21)
    a = less * b
    h12 = EPSILON * h11 / (beta2 * h21) + (a * g01 + b * g02) / beta
    short = EPSILON / (square + EPSILON) - (a * a * g01 + a * b * (g11 + g02) + b * b * g12)
    h22 = 1.0 - short
    c0 = a * short - h12 / beta
    c1 = a + b * short
    c2 = b
    square = c0 * (c0 * g00 + 2.0 * (c1 * g01 + c2 * g02)) + c1 * (c1 * g11 + 2.0 * c2 * g12) + c2 * c2 * g22
    h32 = jnp.sqrt(jnp.maximum(square, 0.0) + EPSILON)
    n0, n1, n2 = h21 * h32, -h11 * h32, h11 * h22 - h12 * h21
    factor = beta * n0 / (n0 * n0 + n1 * n1 + n2 * n2)
    f0, f1, f2 = factor * n0, factor * n1, factor * n2
    y2 = -f2 / h32
    y1 = (h11 * (beta - f0 - h12 * y2) - h21 * (f1 + h22 * y2)) / (h11 * h11 + h21 * h21)
    over = 1.0 / h32
    v0, v1, v2 = c0 * over, c1 * over, c2 * over
    wide = lambda value: jnp.broadcast_to(value, TILE)
    z_one, z_two = wide(y1 / beta + y2 * a), wide(y2 * b)
    r0, r1, r2 = wide(f0 / beta + f1 * a + f2 * v0), wide(f1 * b + f2 * v1), wide(f2 * v2)
    s0, s1, s2 = wide(scale * v0), wide(scale * v1), wide(scale * v2)
    copies = []
    for k in range(2):
        for x in range(source_ref.shape[1]):
            source, power, second = source_ref[k, x], power_ref[k, x], second_ref[k, x]
            adjoint_ref[k, x] = z_one * one_ref[k, x] + z_two * two_ref[k, x]
            residual_ref[k, x] = r0 * source + r1 * power + r2 * second
            basis_ref[k, x] = s0 * source + s1 * power + s2 * second
        pairs = ((adjoint_ref, adjoint_hbm), (residual_ref, residual_hbm), (basis_ref, basis_hbm))
        for index, (src, dst) in enumerate(pairs):
            copy = pltpu.make_async_copy(src.at[k], dst.at[k], sems.at[k, index])
            copy.start()
            copies.append(copy)
    for copy in copies:
        copy.wait()


def call(kernel, outs, scratch=(), name=None, inside=pltpu.VMEM, outside=pltpu.VMEM):
    def run(*args):
        return pl.pallas_call(
            kernel,
            out_shape=[jax.ShapeDtypeStruct(shape, F32) for shape in outs],
            in_specs=[pl.BlockSpec(memory_space=inside)] * len(args),
            out_specs=[pl.BlockSpec(memory_space=outside)] * len(outs),
            scratch_shapes=[pltpu.VMEM(spec, F32) if isinstance(spec, tuple) else spec for spec in scratch],
            compiler_params=pltpu.CompilerParams(vmem_limit_bytes=32 * 1024 * 1024),
            name=name,
        )(*args)

    return run


def exchange(axis, even, odd):
    n_x, n_y = lax.axis_size("gx"), lax.axis_size("gy")
    count = lax.axis_size(axis)
    pairs = [(i, i ^ 1) for i in range(count)]
    others = []
    for x in range(n_x):
        for y in range(n_y):
            place = x if axis == "gx" else y
            if 0 < place < count - 1:
                partner = ((place - 1) ^ 1) + 1
                target = (partner, y) if axis == "gx" else (x, partner)
            else:
                target = (x, y ^ 1) if axis == "gx" else (x ^ 1, y)
            others.append((x * n_y + y, target[0] * n_y + target[1]))
    return lax.ppermute(even, axis, pairs), lax.ppermute(odd, ("gx", "gy"), others)


def shards(adjoint_source, storage, soil_ids, bc_mask, soil_props):
    rows, _, depth = soil_ids.shape
    wide = rows + 2 * MARGIN
    devices = lax.axis_size("gx") * lax.axis_size("gy")
    cells = 2.0 * rows * soil_ids.shape[1] * depth * devices
    own = (rows, *TILE)
    slab = (4 * MARGIN + RIM, *TILE)
    fields, wire, even, odd = call(
        pack_x_kernel,
        [(4, *own), own, slab, slab],
        [soil_props.shape, (4, *own), pltpu.VMEM(own, jnp.int32), pltpu.VMEM((SUB, rows), jnp.int32)]
        + [pltpu.SemaphoreType.DMA((4,))],
        name="pack_x",
        inside=pltpu.HBM,
    )(*(pltpu.with_memory_space_constraint(x, pltpu.HBM) for x in (soil_props, storage, soil_ids, bc_mask.T)))
    xe, xo = exchange("gx", even, odd)
    half = wide // 2 + 1
    rims = -(-2 * half // SUB)
    slab = (2 * wide + half + rims, *TILE)
    even, odd = call(pack_y_kernel, [slab, slab], [(2 * half, *TILE)], name="pack_y")(fields, wire, xe, xo)
    ye, yo = exchange("gy", even, odd)
    buffers = [(wide + 2, 2, *TILE)] * 4
    count = wide // SUB
    slab = (wide + 2 * count, *TILE)
    solved_shapes = [(2, wide, *TILE), (4, count, *TILE), slab, slab]
    coeff, image, scales, solved, edges, even, odd = call(
        coefficients_kernel,
        [(4, wide, 2, *TILE), (4, *own), (5, *own)] + solved_shapes,
        [(wide + 2, 2, *TILE)] * 2 + [(2, 2, rims, *TILE), (2, *own)] + buffers,
        name="first_solve",
    )(soil_props, fields, wire, xe, xo, ye, yo, adjoint_source)

    slab = (2 * (MARGIN + 2), *TILE)
    fold_shapes = [(2, wide, *TILE), (4, count, *TILE), slab, slab]
    ye, yo = exchange("gy", even, odd)
    summed, edges, even, odd = call(fold_y_kernel, fold_shapes, name="fold_y")(solved, edges, ye, yo)
    xe, xo = exchange("gx", even, odd)
    halo = [(rows + 2, *TILE)] * 2 + [(4, count, *TILE)]
    one, power, gram, solved, rest, even, odd = call(
        step_kernel,
        [(2, *own), (2, *own), TILE] + solved_shapes,
        [(2, *own)] + halo + buffers,
        name="second_solve",
    )(summed, edges, xe, xo, coeff, image, scales, adjoint_source)

    ye, yo = exchange("gy", even, odd)
    summed, edges, even, odd = call(fold_y_kernel, fold_shapes, name="fold_y")(solved, rest, ye, yo)
    xe, xo = exchange("gx", even, odd)
    two, second, gram = call(
        last_kernel, [(2, *own), (2, *own), (devices, LANE)], halo, name="last_image"
    )(summed, edges, xe, xo, image, scales, adjoint_source, power, gram)
    gram = lax.all_to_all(gram, ("gx", "gy"), 0, 0, tiled=True)
    return tuple(
        call(
            functools.partial(combine_kernel, scale=math.sqrt(cells)),
            [(2, *own)] * 3,
            [(2, *own)] * 3 + [pltpu.SemaphoreType.DMA((2, 3))],
            name="combine",
            outside=pltpu.HBM,
        )(gram, adjoint_source, power, second, one, two)
    )


def solution(mesh):
    in_specs = (
        P(None, "gx", "gy", None),
        P(None, "gx", "gy", None),
        P("gx", "gy", None),
        P("gx", "gy"),
        P(),
    )
    out_specs = (P(None, "gx", "gy", None), P(None, "gx", "gy", None), P(None, "gx", "gy", None))
    return jax.shard_map(shards, mesh=mesh, in_specs=in_specs, out_specs=out_specs, check_vma=False)
```

```python
import functools
import math

import jax
import jax.numpy as jnp
from jax import lax
from jax.experimental import pallas as pl
from jax.experimental.pallas import tpu as pltpu
from jax.sharding import PartitionSpec as P

MARGIN = 4
SWEEPS = 6
SUB = 8
LANE = 128
TILE = (SUB, LANE)
RIM = MARGIN + 1
EPSILON = 1e-06
F32 = jnp.float32


def sublane():
    return lax.broadcasted_iota(jnp.int32, TILE, 0)


def lane():
    return lax.broadcasted_iota(jnp.int32, TILE, 1)


def up_y(tile):
    return pltpu.roll(tile, SUB - 1, 0)


def down_y(tile):
    return pltpu.roll(tile, 1, 0)


def half_turn(tile):
    return pltpu.roll(tile, SUB // 2, 0)


def along_z(tile, spot):
    above = jnp.where(spot == LANE - 1, 0.0, pltpu.roll(tile, LANE - 1, 1))
    below = jnp.where(spot == 0, 0.0, pltpu.roll(tile, 1, 1))
    return above + below


def along_y(own, side, row, last_up, last_down):
    own_up, own_down = up_y(own), down_y(own)
    side_up, side_down = up_y(side), down_y(side)
    own_sum = jnp.where(row == 7, side_up, own_up) + jnp.where(row == 0, side_down, own_down)
    if last_up is None:
        return own_sum, None
    side_sum = jnp.where(row == 7, own_up, jnp.where(row == 3, last_up, side_up))
    side_sum = side_sum + jnp.where(row == 0, own_down, jnp.where(row == 4, last_down, side_down))
    return own_sum, side_sum


def position(axis):
    place = lax.axis_index(axis)
    first = lax.rem(place, 2) == 0
    return first, place > 0, place < lax.axis_size(axis) - 1


def from_sides(first, even, odd):
    return jnp.where(first, odd, even), jnp.where(first, even, odd)


def lookup(table, wire):
    index = jnp.maximum(wire.astype(jnp.int32) - 1, 0)
    return jnp.where(wire > 0.0, jnp.take_along_axis(table, index, axis=1), 0.0)


def wide_tables(props_ref):
    pad = jnp.zeros((props_ref.shape[0], LANE - props_ref.shape[1]), F32)
    wide = jnp.concatenate([props_ref[...], pad], axis=1)
    return [jnp.broadcast_to(wide[k : k + 1], TILE) for k in range(3)]


def rim_rows(even_ref, odd_ref, base, tiles, rows_even, rows_odd):
    for j, (tile_ref, index) in enumerate(tiles):
        line = (base + j // SUB, pl.ds(j % SUB, 1))
        even_ref[line] = tile_ref[(*index, pl.ds(rows_even, 1))]
        odd_ref[line] = tile_ref[(*index, pl.ds(rows_odd, 1))]


def pack_y(fields, wire_ref, even_ref, odd_ref):
    first, _, _ = position("gy")
    even_low = (sublane() < 4) != first
    count, half = len(fields[0]), wire_ref.shape[0] // 2

    def put(spot, one, other):
        other = half_turn(other)
        even_ref[spot] = jnp.where(even_low, one, other)
        odd_ref[spot] = jnp.where(even_low, other, one)

    for pair in range(2):
        for i in range(count):
            put(pair * count + i, fields[2 * pair][i], fields[2 * pair + 1][i])
    for j in range(half):
        put(2 * count + j, wire_ref[j], wire_ref[j + half])
    rows_even, rows_odd = jnp.where(first, 3, 4), jnp.where(first, 4, 3)
    if 2 * half % SUB:
        last = even_ref.shape[0] - 1
        even_ref[last] = odd_ref[last] = jnp.zeros(TILE, F32)
    spots = [(wire_ref, (j,)) for j in range(2 * half)]
    rim_rows(even_ref, odd_ref, 2 * count + half, spots, rows_even, rows_odd)


def y_slab(count, ids):
    return (2 * count + ids // 2 + -(-ids // SUB), *TILE)


def unpack_fields(even_ref, odd_ref, count, i):
    first, _, _ = position("gy")
    row = sublane()
    out = []
    for pair in range(2):
        low, high = from_sides(first, even_ref[pair * count + i], odd_ref[pair * count + i])
        out.append(jnp.where(row < 4, high, low))
        out.append(half_turn(jnp.where(row < 4, low, high)))
    return out


def unpack_wire(even_ref, odd_ref, count, ids):
    first, has_low, has_high = position("gy")
    row = sublane()

    def sides(spot):
        low, high = from_sides(first, even_ref[spot], odd_ref[spot])
        return jnp.where(has_low, low, 0.0), jnp.where(has_high, high, 0.0)

    one, other = [], []
    for j in range(ids // 2):
        low, high = sides(2 * count + j)
        one.append(jnp.where(row < 4, high, low))
        other.append(half_turn(jnp.where(row < 4, low, high)))
    beyond = [sides(2 * count + ids // 2 + tile) for tile in range(-(-ids // SUB))]
    return one + other, beyond


def halo_x(even_ref, odd_ref):
    first, has_low, has_high = position("gx")
    fields = []
    for k in range(4):
        spots = pl.ds(k * MARGIN, MARGIN)
        low, high = from_sides(first, even_ref[spots], odd_ref[spots])
        fields.append([low[i] for i in range(MARGIN)] + [high[i] for i in range(MARGIN)])
    spots = pl.ds(4 * MARGIN, RIM)
    low, high = from_sides(first, even_ref[spots], odd_ref[spots])
    low = jnp.where(has_low, low, 0.0)
    high = jnp.where(has_high, high, 0.0)
    return fields, [low[i] for i in range(RIM)] + [high[i] for i in range(RIM)]


def first_pack_kernel(
    props_hbm, storage_hbm, ids_hbm, bc_hbm,
    fields_ref, wire_ref, x_even_ref, x_odd_ref, y_even_ref, y_odd_ref,
    props_ref, storage_ref, ids_ref, bc_ref, sems,
):
    places = ((ids_hbm, ids_ref), (storage_hbm, storage_ref), (props_hbm, props_ref), (bc_hbm, bc_ref))
    copies = [pltpu.make_async_copy(src, dst, sems.at[k]) for k, (src, dst) in enumerate(places)]
    for copy in copies:
        copy.start()
    rows = ids_ref.shape[0]
    spot = lane()
    for copy in copies:
        copy.wait()
    tables = wide_tables(props_ref)
    fields = [[] for _ in range(4)]
    for x in range(rows):
        wire = (ids_ref[x] + 1).astype(F32)
        wire_ref[x] = wire
        kp = lookup(tables[0], wire)
        carried = lookup(tables[2], wire)
        held = jnp.broadcast_to(bc_ref[:, x : x + 1].astype(F32), TILE)
        bound = jnp.where(spot == LANE - 1, 2.0 * kp * held, 0.0)
        press = storage_ref[0, x]
        lower = storage_ref[1, x]
        fields[0].append(press + bound)
        fields[1].append(carried * press - storage_ref[2, x])
        fields[2].append(lower)
        fields[3].append(storage_ref[3, x] - carried * lower)
        for k in range(4):
            fields_ref[k, x] = fields[k][x]
    first, _, _ = position("gx")
    high, low = rows - MARGIN, 0
    start_even = jnp.where(first, high, low)
    start_odd = jnp.where(first, low, high)
    wire_even = jnp.where(first, rows - RIM, 0)
    wire_odd = jnp.where(first, 0, rows - RIM)
    for k in range(4):
        x_even_ref[pl.ds(k * MARGIN, MARGIN)] = fields_ref[k, pl.ds(start_even, MARGIN)]
        x_odd_ref[pl.ds(k * MARGIN, MARGIN)] = fields_ref[k, pl.ds(start_odd, MARGIN)]
    x_even_ref[pl.ds(4 * MARGIN, RIM)] = wire_ref[pl.ds(wire_even, RIM)]
    x_odd_ref[pl.ds(4 * MARGIN, RIM)] = wire_ref[pl.ds(wire_odd, RIM)]
    pack_y(fields, wire_ref, y_even_ref, y_odd_ref)


def corner_pack_kernel(xe_ref, xo_ref, even_ref, odd_ref, wire_ref):
    fields, wire = halo_x(xe_ref, xo_ref)
    for j, value in enumerate(wire):
        wire_ref[j] = value
    pack_y(fields, wire_ref, even_ref, odd_ref)


def sweep_row(q_ref, t_ref, coeff, j, row, spot, rhs):
    sums = []
    for ref in (q_ref, t_ref):
        own, side = ref[j, 0], ref[j, 1]
        own_sum, side_sum = along_y(own, side, row, 0.0, 0.0)
        own_sum = own_sum + (along_z(own, spot) + (ref[j - 1, 0] + ref[j + 1, 0]))
        side_sum = side_sum + (along_z(side, spot) + (ref[j - 1, 1] + ref[j + 1, 1]))
        sums.append([own_sum, side_sum])
    if rhs is not None:
        sums[0][0] = sums[0][0] + rhs[0]
        sums[1][0] = sums[1][0] + rhs[1]
    out = []
    for tile in range(2):
        flow, heat = sums[0][tile], sums[1][tile]
        out.append(
            (
                coeff(0, j - 1, tile) * flow + coeff(1, j - 1, tile) * heat,
                coeff(2, j - 1, tile) * flow + coeff(3, j - 1, tile) * heat,
            )
        )
    return out


def subdomain_sweeps(rhs_ref, coeff, solved_ref, rims_ref, even_ref, odd_ref, buffers, rows):
    row, spot = sublane(), lane()
    wide = rows + 2 * MARGIN
    zero = jnp.zeros(TILE, F32)
    for buffer in buffers:
        for j in range(wide + 2):
            for tile in range(2):
                buffer[j, tile] = zero
    current, following = buffers[:2], buffers[2:]
    for x in range(rows):
        j = x + RIM
        flow, heat = rhs_ref[0, x], rhs_ref[1, x]
        current[0][j, 0] = coeff(0, j - 1, 0) * flow + coeff(1, j - 1, 0) * heat
        current[1][j, 0] = coeff(2, j - 1, 0) * flow + coeff(3, j - 1, 0) * heat
    first, _, _ = position("gy")
    even_low = (row < 4) != first
    for sweep in range(1, SWEEPS):
        reach = min(sweep, MARGIN)
        for x in range(-reach, rows + reach):
            j = x + RIM
            rhs = (rhs_ref[0, x], rhs_ref[1, x]) if 0 <= x < rows else None
            out = sweep_row(current[0], current[1], coeff, j, row, spot, rhs)
            if sweep < SWEEPS - 1:
                for tile in range(2):
                    following[0][j, tile] = out[tile][0]
                    following[1][j, tile] = out[tile][1]
            else:
                i = j - 1
                (own_q, own_t), (side_q, side_t) = out
                solved_ref[0, i], solved_ref[1, i] = own_q, own_t
                turned = half_turn(side_t)
                even_ref[i] = jnp.where(even_low, turned, side_q)
                odd_ref[i] = jnp.where(even_low, side_q, turned)
                for k, side in enumerate((side_q, side_t)):
                    line = (i // SUB, pl.ds(i % SUB, 1))
                    rims_ref[(2 * k, *line)] = side[7:8]
                    rims_ref[(2 * k + 1, *line)] = side[0:1]
        current, following = following, current
    rows_even, rows_odd = jnp.where(first, 7, 0), jnp.where(first, 0, 7)
    for k in range(2):
        spots = [(solved_ref, (k, i)) for i in range(wide)]
        rim_rows(even_ref, odd_ref, wide + k * (wide // SUB), spots, rows_even, rows_odd)


def getter(own_ref, own_side_ref, rest_ref, rest_side_ref):
    rows = own_ref.shape[1]

    def coeff(k, i, tile):
        ref, rest, start, count = (own_ref, rest_ref, MARGIN, rows)
        if tile:
            ref, rest, start, count = (own_side_ref, rest_side_ref, MARGIN + 1, rows - 2)
        if start <= i < start + count:
            return ref[k, i - start]
        return rest[k, i if i < start else i - count]

    return coeff


def diagonal(tiles, index, spot):
    j, last_up, last_down = index
    own_sum, side_sum = along_y(tiles(j, 0), tiles(j, 1), sublane(), last_up, last_down)
    out = []
    for tile, total in ((0, own_sum), (1, side_sum)):
        if tile == 1 and last_up is None:
            break
        centre = tiles(j, tile)
        total = total + along_z(centre, spot) + (tiles(j - 1, tile) + tiles(j + 1, tile))
        out.append(centre * total)
    return out


def block_tiles(stores, sums, scales, wire):
    press, cross, lower, heat = stores
    gp, gt = scales
    outside = jnp.where(wire > 0.0, 0.0, 1.0)
    a = press + sums[0] + outside
    d = heat + sums[1] + outside
    inverse = 1.0 / (a * d + cross * lower)
    pp, pt, tt = gp * gp * inverse, gp * gt * inverse, gt * gt * inverse
    return a, d, (pp * d, pt * cross, -(pt * lower), tt * a)


def root_tables(props_ref):
    tables = wide_tables(props_ref)
    return [jnp.sqrt(jnp.maximum(table, 0.0)) for table in tables[:2]], tables[2]


def beyond_lines(beyond_ref, g, j):
    return tuple(
        jnp.broadcast_to(beyond_ref[g, end, j // SUB, pl.ds(j % SUB, 1)], TILE) for end in (1, 0)
    )


def own_coefficients_kernel(
    props_ref, fields_ref, wire_ref, xe_ref, xo_ref, ye_ref, yo_ref, source_ref,
    own_ref, own_side_ref, image_ref, scale_ref, rhs_ref, roots_ref, roots_side_ref, beyond_ref,
):
    rows = wire_ref.shape[0]
    spot = lane()
    roots, carried = root_tables(props_ref)
    _, x_wire = halo_x(xe_ref, xo_ref)
    sides, beyond = unpack_wire(ye_ref, yo_ref, rows, rows)
    wire = x_wire[:RIM] + [wire_ref[x] for x in range(rows)] + x_wire[RIM:]
    for g in range(2):
        for j, value in enumerate(wire):
            roots_ref[g, j] = lookup(roots[g], value)
        for x in range(rows):
            roots_side_ref[g, x] = lookup(roots[g], sides[x])
        for tile, ends in enumerate(beyond):
            for end in range(2):
                beyond_ref[g, end, tile] = lookup(roots[g], ends[end])
    for x in range(rows):
        inner = 0 < x < rows - 1
        sums = []
        for g in range(2):
            tiles = lambda j, tile: roots_side_ref[g, j - RIM] if tile else roots_ref[g, j]
            lines = beyond_lines(beyond_ref, g, x) if inner else (None, None)
            sums.append(diagonal(tiles, (x + RIM, *lines), spot))
        stores = [fields_ref[k, x] for k in range(4)]
        gp, gt = (roots_ref[g, x + RIM] for g in range(2))
        a, d, coeffs = block_tiles(stores, (sums[0][0], sums[1][0]), (gp, gt), wire_ref[x])
        for k in range(4):
            own_ref[k, x] = coeffs[k]
        over_p, over_t = 1.0 / gp, 1.0 / gt
        over = over_p * over_t
        image_ref[0, x] = a * (over_p * over_p)
        image_ref[1, x] = -(stores[1] * over)
        image_ref[2, x] = stores[2] * over
        image_ref[3, x] = d * (over_t * over_t)
        for k, value in enumerate((gp, gt, over_p, over_t, lookup(carried, wire_ref[x]))):
            scale_ref[k, x] = value
        rhs_ref[0, x] = source_ref[0, x] * over_p
        rhs_ref[1, x] = source_ref[1, x] * over_t
        if inner:
            stores = unpack_fields(ye_ref, yo_ref, rows, x)
            scales = [roots_side_ref[g, x] for g in range(2)]
            _, _, coeffs = block_tiles(stores, (sums[0][1], sums[1][1]), scales, sides[x])
            for k in range(4):
                own_side_ref[k, x - 1] = coeffs[k]


def first_solve_kernel(
    props_ref, xe_ref, xo_ref, ye_ref, yo_ref, ce_ref, co_ref,
    own_ref, own_side_ref, rhs_ref, roots_ref, roots_side_ref, beyond_ref,
    rest_ref, rest_side_ref, solved_ref, rims_ref, even_ref, odd_ref,
    corner_roots_ref, corner_beyond_ref, *buffers,
):
    rows = own_ref.shape[1]
    wide = rows + 2 * MARGIN
    spot = lane()
    roots, _ = root_tables(props_ref)
    x_fields, x_wire = halo_x(xe_ref, xo_ref)
    sides, beyond = unpack_wire(ce_ref, co_ref, 2 * MARGIN, 2 * RIM)
    own_sides, _ = unpack_wire(ye_ref, yo_ref, rows, rows)
    for g in range(2):
        for j, value in enumerate(sides):
            corner_roots_ref[g, j] = lookup(roots[g], value)
        for tile, ends in enumerate(beyond):
            for end in range(2):
                corner_beyond_ref[g, end, tile] = lookup(roots[g], ends[end])
    for i in list(range(RIM)) + list(range(wide - RIM, wide)):
        j, x = i + 1, i - MARGIN
        own_row = 0 <= x < rows
        sums = []
        for g in range(2):

            def tiles(j, tile):
                if not tile:
                    return roots_ref[g, j]
                if RIM <= j < RIM + rows:
                    return roots_side_ref[g, j - RIM]
                return corner_roots_ref[g, j if j < RIM else j - rows]

            if own_row:
                lines = beyond_lines(beyond_ref, g, x)
            else:
                lines = beyond_lines(corner_beyond_ref, g, j if j < RIM else j - rows)
            sums.append((diagonal(tiles, (j, *lines), spot), tiles(j, 0), tiles(j, 1)))
        corner = i if i < MARGIN else i - rows
        if not own_row:
            stores = [x_fields[k][corner] for k in range(4)]
            scales = (sums[0][1], sums[1][1])
            spare = x_wire[j if j < RIM else j - rows]
            _, _, coeffs = block_tiles(stores, (sums[0][0][0], sums[1][0][0]), scales, spare)
            for k in range(4):
                rest_ref[k, corner] = coeffs[k]
            stores = unpack_fields(ce_ref, co_ref, 2 * MARGIN, corner)
            spare = sides[j if j < RIM else j - rows]
        else:
            stores = unpack_fields(ye_ref, yo_ref, rows, x)
            spare = own_sides[x]
        scales = (sums[0][2], sums[1][2])
        _, _, coeffs = block_tiles(stores, (sums[0][0][1], sums[1][0][1]), scales, spare)
        for k in range(4):
            rest_side_ref[k, i if i < RIM else i - (rows - 2)] = coeffs[k]
    coeff = getter(own_ref, own_side_ref, rest_ref, rest_side_ref)
    subdomain_sweeps(rhs_ref, coeff, solved_ref, rims_ref, even_ref, odd_ref, buffers, rows)


def fold_y_kernel(solved_ref, rims_ref, ye_ref, yo_ref, summed_ref, edges_ref, even_ref, odd_ref):
    wide = solved_ref.shape[1]
    row = sublane()
    first, has_low, has_high = position("gy")
    for i in range(wide):
        low, high = from_sides(first, ye_ref[i], yo_ref[i])
        low = jnp.where(has_low, low, 0.0)
        high = jnp.where(has_high, high, 0.0)
        summed_ref[0, i] = solved_ref[0, i] + jnp.where(row < 4, low, high)
        summed_ref[1, i] = solved_ref[1, i] + half_turn(jnp.where(row < 4, high, low))
    count = wide // SUB
    for k in range(2):
        for tile in range(count):
            spot = wide + k * count + tile
            low, high = from_sides(first, ye_ref[spot], yo_ref[spot])
            edges_ref[2 * k, tile] = rims_ref[2 * k, tile] + jnp.where(has_low, low, 0.0)
            edges_ref[2 * k + 1, tile] = rims_ref[2 * k + 1, tile] + jnp.where(has_high, high, 0.0)
    first, _, _ = position("gx")
    margin_even = jnp.where(first, wide - MARGIN, 0)
    margin_odd = jnp.where(first, 0, wide - MARGIN)
    rim_even = jnp.where(first, wide - MARGIN - 1, MARGIN)
    rim_odd = jnp.where(first, MARGIN, wide - MARGIN - 1)
    for k in range(2):
        base = k * (MARGIN + 2)
        for ref, margin, rim in ((even_ref, margin_even, rim_even), (odd_ref, margin_odd, rim_odd)):
            ref[pl.ds(base, MARGIN)] = summed_ref[k, pl.ds(margin, MARGIN)]
            ref[base + MARGIN] = summed_ref[k, rim]
        to_low = jnp.where(row < 4, edges_ref[2 * k, 0], half_turn(edges_ref[2 * k + 1, 0]))
        last = count - 1
        to_high = jnp.where(row < 4, half_turn(edges_ref[2 * k + 1, last]), edges_ref[2 * k, last])
        even_ref[base + MARGIN + 1] = jnp.where(first, to_high, to_low)
        odd_ref[base + MARGIN + 1] = jnp.where(first, to_low, to_high)


def fold_x(summed_ref, edges_ref, xe_ref, xo_ref, field_refs, edge_ref):
    wide = summed_ref.shape[1]
    rows = wide - 2 * MARGIN
    row = sublane()
    first, has_low, has_high = position("gx")
    for k in range(2):
        base = k * (MARGIN + 2)
        low, high = from_sides(first, xe_ref[pl.ds(base, MARGIN + 2)], xo_ref[pl.ds(base, MARGIN + 2)])
        low = jnp.where(has_low, low, 0.0)
        high = jnp.where(has_high, high, 0.0)
        for x in range(-1, rows + 1):
            value = summed_ref[k, x + MARGIN]
            if 0 <= x < MARGIN:
                value = value + low[x]
            if rows - MARGIN <= x < rows:
                value = value + high[x - (rows - MARGIN)]
            if x == -1:
                value = value + low[MARGIN]
            if x == rows:
                value = value + high[MARGIN]
            field_refs[k][x + 1] = value
        from_low, from_high = low[MARGIN + 1], high[MARGIN + 1]
        last = edge_ref.shape[1] - 1
        for end in range(2):
            for tile in range(last + 1):
                value = edges_ref[2 * k + end, tile]
                if tile == 0:
                    part = half_turn(from_low) if end == 1 else from_low
                    value = value + jnp.where(row < 4, 0.0, part)
                if tile == last:
                    part = half_turn(from_high) if end == 1 else from_high
                    value = value + jnp.where(row < 4, part, 0.0)
                edge_ref[2 * k + end, tile] = value


def image_row(field_refs, edge_ref, image_ref, x, row, spot):
    sums = []
    i = x + MARGIN
    for k, ref in enumerate(field_refs):
        own = ref[x + 1]
        down, up = (
            jnp.broadcast_to(edge_ref[2 * k + end, i // SUB, pl.ds(i % SUB, 1)], TILE) for end in range(2)
        )
        total = jnp.where(row == 7, up, up_y(own)) + jnp.where(row == 0, down, down_y(own))
        sums.append(total + along_z(own, spot) + (ref[x] + ref[x + 2]))
    flow, heat = field_refs[0][x + 1], field_refs[1][x + 1]
    return (
        image_ref[0, x] * flow + image_ref[1, x] * heat - sums[0],
        image_ref[2, x] * flow + image_ref[3, x] * heat - sums[1],
    )


def keep_direction(direction_ref, scale_ref, field_refs, x):
    heat = field_refs[1][x + 1] * scale_ref[3, x]
    direction_ref[1, x] = heat
    direction_ref[0, x] = field_refs[0][x + 1] * scale_ref[2, x] - scale_ref[4, x] * heat


def gram_rows(pairs, row, offset):
    total = jnp.zeros(TILE, F32)
    for index, value in enumerate(pairs):
        line = jnp.broadcast_to(jnp.sum(value, axis=0, keepdims=True), TILE)
        total = total + jnp.where(row == index + offset, line, 0.0)
    return total


def step_kernel(
    summed_ref, edges_ref, xe_ref, xo_ref, own_ref, own_side_ref, rest_ref, rest_side_ref, image_ref, scale_ref, source_ref,
    direction_ref, power_ref, gram_ref, solved_ref, rims_ref, even_ref, odd_ref,
    rhs_ref, q_ref, t_ref, edge_ref, *buffers,
):
    rows = source_ref.shape[1]
    row, spot = sublane(), lane()
    fields = (q_ref, t_ref)
    fold_x(summed_ref, edges_ref, xe_ref, xo_ref, fields, edge_ref)
    products = [jnp.zeros(TILE, F32) for _ in range(3)]
    for x in range(rows):
        keep_direction(direction_ref, scale_ref, fields, x)
        for k, part in enumerate(image_row(fields, edge_ref, image_ref, x, row, spot)):
            source = source_ref[k, x]
            scaled = part - source * scale_ref[2 + k, x]
            power = scaled * scale_ref[k, x]
            rhs_ref[k, x] = scaled
            power_ref[k, x] = power
            products[0] = products[0] + source * source
            products[1] = products[1] + source * power
            products[2] = products[2] + power * power
    gram_ref[...] = gram_rows(products, row, 0)
    coeff = getter(own_ref, own_side_ref, rest_ref, rest_side_ref)
    subdomain_sweeps(rhs_ref, coeff, solved_ref, rims_ref, even_ref, odd_ref, buffers, rows)


def last_kernel(
    summed_ref, edges_ref, xe_ref, xo_ref, image_ref, scale_ref, source_ref, power_ref, gram_in_ref,
    direction_ref, second_ref, gram_ref, q_ref, t_ref, edge_ref,
):
    rows = source_ref.shape[1]
    row, spot = sublane(), lane()
    fields = (q_ref, t_ref)
    fold_x(summed_ref, edges_ref, xe_ref, xo_ref, fields, edge_ref)
    products = [jnp.zeros(TILE, F32) for _ in range(3)]
    for x in range(rows):
        keep_direction(direction_ref, scale_ref, fields, x)
        for k, part in enumerate(image_row(fields, edge_ref, image_ref, x, row, spot)):
            power = power_ref[k, x]
            second = part * scale_ref[k, x] - power
            second_ref[k, x] = second
            products[0] = products[0] + source_ref[k, x] * second
            products[1] = products[1] + power * second
            products[2] = products[2] + second * second
    total = jnp.sum(gram_in_ref[...] + gram_rows(products, row, 3), axis=1, keepdims=True)
    line = jnp.sum(jnp.where(row == spot, jnp.broadcast_to(total, TILE), 0.0), axis=0, keepdims=True)
    gram_ref[...] = jnp.broadcast_to(line, gram_ref.shape)


def combine_kernel(
    gram_ref, source_ref, power_ref, second_ref, one_ref, two_ref,
    adjoint_hbm, residual_hbm, basis_hbm, adjoint_ref, residual_ref, basis_ref, sems, *, scale,
):
    sums = jnp.sum(gram_ref[...], axis=0, keepdims=True)
    spot = lax.broadcasted_iota(jnp.int32, sums.shape, 1)
    g00, g01, g11, g02, g12, g22 = (
        jnp.sum(jnp.where(spot == k, sums, 0.0), axis=1, keepdims=True) for k in range(6)
    )
    beta2 = g00 + EPSILON
    beta = jnp.sqrt(beta2)
    less = (EPSILON - g01) / beta2
    h11 = (g00 + g01) / beta2
    square = (less * less * g00 + 2.0 * less * g01 + g11) / beta2
    square = jnp.maximum(square, 0.0)
    h21 = jnp.sqrt(square + EPSILON)
    b = 1.0 / (beta * h21)
    a = less * b
    h12 = EPSILON * h11 / (beta2 * h21) + (a * g01 + b * g02) / beta
    short = EPSILON / (square + EPSILON) - (a * a * g01 + a * b * (g11 + g02) + b * b * g12)
    h22 = 1.0 - short
    c0 = a * short - h12 / beta
    c1 = a + b * short
    c2 = b
    square = c0 * (c0 * g00 + 2.0 * (c1 * g01 + c2 * g02)) + c1 * (c1 * g11 + 2.0 * c2 * g12) + c2 * c2 * g22
    h32 = jnp.sqrt(jnp.maximum(square, 0.0) + EPSILON)
    n0, n1, n2 = h21 * h32, -h11 * h32, h11 * h22 - h12 * h21
    factor = beta * n0 / (n0 * n0 + n1 * n1 + n2 * n2)
    f0, f1, f2 = factor * n0, factor * n1, factor * n2
    y2 = -f2 / h32
    y1 = (h11 * (beta - f0 - h12 * y2) - h21 * (f1 + h22 * y2)) / (h11 * h11 + h21 * h21)
    over = 1.0 / h32
    v0, v1, v2 = c0 * over, c1 * over, c2 * over
    wide = lambda value: jnp.broadcast_to(value, TILE)
    z_one, z_two = wide(y1 / beta + y2 * a), wide(y2 * b)
    r0, r1, r2 = wide(f0 / beta + f1 * a + f2 * v0), wide(f1 * b + f2 * v1), wide(f2 * v2)
    s0, s1, s2 = wide(scale * v0), wide(scale * v1), wide(scale * v2)
    copies = []
    for k in range(2):
        for x in range(source_ref.shape[1]):
            source, power, second = source_ref[k, x], power_ref[k, x], second_ref[k, x]
            adjoint_ref[k, x] = z_one * one_ref[k, x] + z_two * two_ref[k, x]
            residual_ref[k, x] = r0 * source + r1 * power + r2 * second
            basis_ref[k, x] = s0 * source + s1 * power + s2 * second
        pairs = ((adjoint_ref, adjoint_hbm), (residual_ref, residual_hbm), (basis_ref, basis_hbm))
        for index, (src, dst) in enumerate(pairs):
            copy = pltpu.make_async_copy(src.at[k], dst.at[k], sems.at[k, index])
            copy.start()
            copies.append(copy)
    for copy in copies:
        copy.wait()


def call(kernel, outs, scratch=(), name=None, inside=pltpu.VMEM, outside=pltpu.VMEM):
    def run(*args):
        return pl.pallas_call(
            kernel,
            out_shape=[jax.ShapeDtypeStruct(shape, F32) for shape in outs],
            in_specs=[pl.BlockSpec(memory_space=inside)] * len(args),
            out_specs=[pl.BlockSpec(memory_space=outside)] * len(outs),
            scratch_shapes=[pltpu.VMEM(spec, F32) if isinstance(spec, tuple) else spec for spec in scratch],
            compiler_params=pltpu.CompilerParams(vmem_limit_bytes=32 * 1024 * 1024),
            name=name,
        )(*args)

    return run


def exchange(axis, even, odd):
    n_x, n_y = lax.axis_size("gx"), lax.axis_size("gy")
    count = lax.axis_size(axis)
    pairs = [(i, i ^ 1) for i in range(count)]
    others = []
    for x in range(n_x):
        for y in range(n_y):
            place = x if axis == "gx" else y
            if 0 < place < count - 1:
                partner = ((place - 1) ^ 1) + 1
                target = (partner, y) if axis == "gx" else (x, partner)
            else:
                target = (x, y ^ 1) if axis == "gx" else (x ^ 1, y)
            others.append((x * n_y + y, target[0] * n_y + target[1]))
    return lax.ppermute(even, axis, pairs), lax.ppermute(odd, ("gx", "gy"), others)


def shards(adjoint_source, storage, soil_ids, bc_mask, soil_props):
    rows, _, depth = soil_ids.shape
    wide = rows + 2 * MARGIN
    devices = lax.axis_size("gx") * lax.axis_size("gy")
    cells = 2.0 * rows * soil_ids.shape[1] * depth * devices
    own = (rows, *TILE)
    x_slab = (4 * MARGIN + RIM, *TILE)
    slab = y_slab(rows, rows)
    fields, wire, x_even, x_odd, y_even, y_odd = call(
        first_pack_kernel,
        [(4, *own), own, x_slab, x_slab, slab, slab],
        [soil_props.shape, (4, *own), pltpu.VMEM(own, jnp.int32), pltpu.VMEM((SUB, rows), jnp.int32)]
        + [pltpu.SemaphoreType.DMA((4,))],
        name="first_pack",
        inside=pltpu.HBM,
    )(*(pltpu.with_memory_space_constraint(x, pltpu.HBM) for x in (soil_props, storage, soil_ids, bc_mask.T)))
    xe, xo = exchange("gx", x_even, x_odd)
    ye, yo = exchange("gy", y_even, y_odd)
    slab = y_slab(2 * MARGIN, 2 * RIM)
    even, odd = call(corner_pack_kernel, [slab, slab], [(2 * RIM, *TILE)], name="corner_pack")(xe, xo)
    ce, co = exchange("gy", even, odd)
    count = wide // SUB
    own_coeff, own_side, image, scales, rhs, roots, roots_side, beyond = call(
        own_coefficients_kernel,
        [(4, *own), (4, rows - 2, *TILE), (4, *own), (5, *own), (2, *own)]
        + [(2, rows + 2 * RIM, *TILE), (2, *own), (2, 2, -(-rows // SUB), *TILE)],
        name="own_coefficients",
    )(soil_props, fields, wire, xe, xo, ye, yo, adjoint_source)
    buffers = [(wide + 2, 2, *TILE)] * 4
    slab = (wide + 2 * count, *TILE)
    solved_shapes = [(2, wide, *TILE), (4, count, *TILE), slab, slab]
    rest, rest_side, solved, edges, even, odd = call(
        first_solve_kernel,
        [(4, 2 * MARGIN, *TILE), (4, 2 * RIM, *TILE)] + solved_shapes,
        [(2, 2 * RIM, *TILE), (2, 2, -(-2 * RIM // SUB), *TILE)] + buffers,
        name="first_solve",
    )(soil_props, xe, xo, ye, yo, ce, co, own_coeff, own_side, rhs, roots, roots_side, beyond)
    coeffs = (own_coeff, own_side, rest, rest_side)

    slab = (2 * (MARGIN + 2), *TILE)
    fold_shapes = [(2, wide, *TILE), (4, count, *TILE), slab, slab]
    ye, yo = exchange("gy", even, odd)
    summed, edges, even, odd = call(fold_y_kernel, fold_shapes, name="fold_y")(solved, edges, ye, yo)
    xe, xo = exchange("gx", even, odd)
    halo = [(rows + 2, *TILE)] * 2 + [(4, count, *TILE)]
    one, power, gram, solved, edges, even, odd = call(
        step_kernel,
        [(2, *own), (2, *own), TILE] + solved_shapes,
        [(2, *own)] + halo + buffers,
        name="second_solve",
    )(summed, edges, xe, xo, *coeffs, image, scales, adjoint_source)

    ye, yo = exchange("gy", even, odd)
    summed, edges, even, odd = call(fold_y_kernel, fold_shapes, name="fold_y")(solved, edges, ye, yo)
    xe, xo = exchange("gx", even, odd)
    two, second, gram = call(
        last_kernel, [(2, *own), (2, *own), (devices, LANE)], halo, name="last_image"
    )(summed, edges, xe, xo, image, scales, adjoint_source, power, gram)
    gram = lax.all_to_all(gram, ("gx", "gy"), 0, 0, tiled=True)
    return tuple(
        call(
            functools.partial(combine_kernel, scale=math.sqrt(cells)),
            [(2, *own)] * 3,
            [(2, *own)] * 3 + [pltpu.SemaphoreType.DMA((2, 3))],
            name="combine",
            outside=pltpu.HBM,
        )(gram, adjoint_source, power, second, one, two)
    )


def solution(mesh):
    in_specs = (
        P(None, "gx", "gy", None),
        P(None, "gx", "gy", None),
        P("gx", "gy", None),
        P("gx", "gy"),
        P(),
    )
    out_specs = (P(None, "gx", "gy", None), P(None, "gx", "gy", None), P(None, "gx", "gy", None))
    return jax.shard_map(shards, mesh=mesh, in_specs=in_specs, out_specs=out_specs, check_vma=False)
```

```python
import functools
import math

import jax
import jax.numpy as jnp
from jax import lax
from jax.experimental import pallas as pl
from jax.experimental.pallas import tpu as pltpu
from jax.sharding import PartitionSpec as P

MARGIN = 4
SWEEPS = 6
SUB = 8
LANE = 128
TILE = (SUB, LANE)
RIM = MARGIN + 1
EPSILON = 1e-06
F32 = jnp.float32


def sublane():
    return lax.broadcasted_iota(jnp.int32, TILE, 0)


def lane():
    return lax.broadcasted_iota(jnp.int32, TILE, 1)


def up_y(tile):
    return pltpu.roll(tile, SUB - 1, 0)


def down_y(tile):
    return pltpu.roll(tile, 1, 0)


def half_turn(tile):
    return pltpu.roll(tile, SUB // 2, 0)


def along_z(tile, spot):
    above = jnp.where(spot == LANE - 1, 0.0, pltpu.roll(tile, LANE - 1, 1))
    below = jnp.where(spot == 0, 0.0, pltpu.roll(tile, 1, 1))
    return above + below


def along_y(own, side, row, last_up, last_down):
    own_up, own_down = up_y(own), down_y(own)
    side_up, side_down = up_y(side), down_y(side)
    own_sum = jnp.where(row == 7, side_up, own_up) + jnp.where(row == 0, side_down, own_down)
    if last_up is None:
        return own_sum, None
    side_sum = jnp.where(row == 7, own_up, jnp.where(row == 3, last_up, side_up))
    side_sum = side_sum + jnp.where(row == 0, own_down, jnp.where(row == 4, last_down, side_down))
    return own_sum, side_sum


def position(axis):
    place = lax.axis_index(axis)
    first = lax.rem(place, 2) == 0
    return first, place > 0, place < lax.axis_size(axis) - 1


def from_sides(first, even, odd):
    return jnp.where(first, odd, even), jnp.where(first, even, odd)


def lookup(table, wire):
    index = jnp.maximum(wire.astype(jnp.int32) - 1, 0)
    return jnp.where(wire > 0.0, jnp.take_along_axis(table, index, axis=1), 0.0)


def wide_tables(props_ref):
    pad = jnp.zeros((props_ref.shape[0], LANE - props_ref.shape[1]), F32)
    wide = jnp.concatenate([props_ref[...], pad], axis=1)
    return [jnp.broadcast_to(wide[k : k + 1], TILE) for k in range(3)]


def rim_rows(even_ref, odd_ref, base, tiles, rows_even, rows_odd):
    for j, (tile_ref, index) in enumerate(tiles):
        line = (base + j // SUB, pl.ds(j % SUB, 1))
        even_ref[line] = tile_ref[(*index, pl.ds(rows_even, 1))]
        odd_ref[line] = tile_ref[(*index, pl.ds(rows_odd, 1))]


def pack_y(fields, wire_ref, even_ref, odd_ref):
    first, _, _ = position("gy")
    even_low = (sublane() < 4) != first
    count, half = len(fields[0]), wire_ref.shape[0] // 2

    def put(spot, one, other):
        other = half_turn(other)
        even_ref[spot] = jnp.where(even_low, one, other)
        odd_ref[spot] = jnp.where(even_low, other, one)

    for pair in range(2):
        for i in range(count):
            put(pair * count + i, fields[2 * pair][i], fields[2 * pair + 1][i])
    for j in range(half):
        put(2 * count + j, wire_ref[j], wire_ref[j + half])
    rows_even, rows_odd = jnp.where(first, 3, 4), jnp.where(first, 4, 3)
    if 2 * half % SUB:
        last = even_ref.shape[0] - 1
        even_ref[last] = odd_ref[last] = jnp.zeros(TILE, F32)
    spots = [(wire_ref, (j,)) for j in range(2 * half)]
    rim_rows(even_ref, odd_ref, 2 * count + half, spots, rows_even, rows_odd)


def y_slab(count, ids):
    return (2 * count + ids // 2 + -(-ids // SUB), *TILE)


def unpack_fields(even_ref, odd_ref, count, i):
    first, _, _ = position("gy")
    row = sublane()
    out = []
    for pair in range(2):
        low, high = from_sides(first, even_ref[pair * count + i], odd_ref[pair * count + i])
        out.append(jnp.where(row < 4, high, low))
        out.append(half_turn(jnp.where(row < 4, low, high)))
    return out


def unpack_wire(even_ref, odd_ref, count, ids):
    first, has_low, has_high = position("gy")
    row = sublane()

    def sides(spot):
        low, high = from_sides(first, even_ref[spot], odd_ref[spot])
        return jnp.where(has_low, low, 0.0), jnp.where(has_high, high, 0.0)

    one, other = [], []
    for j in range(ids // 2):
        low, high = sides(2 * count + j)
        one.append(jnp.where(row < 4, high, low))
        other.append(half_turn(jnp.where(row < 4, low, high)))
    beyond = [sides(2 * count + ids // 2 + tile) for tile in range(-(-ids // SUB))]
    return one + other, beyond


def halo_x(even_ref, odd_ref):
    first, has_low, has_high = position("gx")
    fields = []
    for k in range(4):
        spots = pl.ds(k * MARGIN, MARGIN)
        low, high = from_sides(first, even_ref[spots], odd_ref[spots])
        fields.append([low[i] for i in range(MARGIN)] + [high[i] for i in range(MARGIN)])
    spots = pl.ds(4 * MARGIN, RIM)
    low, high = from_sides(first, even_ref[spots], odd_ref[spots])
    low = jnp.where(has_low, low, 0.0)
    high = jnp.where(has_high, high, 0.0)
    return fields, [low[i] for i in range(RIM)] + [high[i] for i in range(RIM)]


def first_pack_kernel(
    props_hbm, storage_hbm, ids_hbm, bc_hbm,
    fields_ref, wire_ref, x_even_ref, x_odd_ref, y_even_ref, y_odd_ref,
    props_ref, storage_ref, ids_ref, bc_ref, sems,
):
    places = ((ids_hbm, ids_ref), (storage_hbm, storage_ref), (props_hbm, props_ref), (bc_hbm, bc_ref))
    copies = [pltpu.make_async_copy(src, dst, sems.at[k]) for k, (src, dst) in enumerate(places)]
    for copy in copies:
        copy.start()
    rows = ids_ref.shape[0]
    spot = lane()
    for copy in copies:
        copy.wait()
    tables = wide_tables(props_ref)
    fields = [[] for _ in range(4)]
    for x in range(rows):
        wire = (ids_ref[x] + 1).astype(F32)
        wire_ref[x] = wire
        kp = lookup(tables[0], wire)
        carried = lookup(tables[2], wire)
        held = jnp.broadcast_to(bc_ref[:, x : x + 1].astype(F32), TILE)
        bound = jnp.where(spot == LANE - 1, 2.0 * kp * held, 0.0)
        press = storage_ref[0, x]
        lower = storage_ref[1, x]
        fields[0].append(press + bound)
        fields[1].append(carried * press - storage_ref[2, x])
        fields[2].append(lower)
        fields[3].append(storage_ref[3, x] - carried * lower)
        for k in range(4):
            fields_ref[k, x] = fields[k][x]
    first, _, _ = position("gx")
    high, low = rows - MARGIN, 0
    start_even = jnp.where(first, high, low)
    start_odd = jnp.where(first, low, high)
    wire_even = jnp.where(first, rows - RIM, 0)
    wire_odd = jnp.where(first, 0, rows - RIM)
    for k in range(4):
        x_even_ref[pl.ds(k * MARGIN, MARGIN)] = fields_ref[k, pl.ds(start_even, MARGIN)]
        x_odd_ref[pl.ds(k * MARGIN, MARGIN)] = fields_ref[k, pl.ds(start_odd, MARGIN)]
    x_even_ref[pl.ds(4 * MARGIN, RIM)] = wire_ref[pl.ds(wire_even, RIM)]
    x_odd_ref[pl.ds(4 * MARGIN, RIM)] = wire_ref[pl.ds(wire_odd, RIM)]
    pack_y(fields, wire_ref, y_even_ref, y_odd_ref)


def corner_pack_kernel(xe_ref, xo_ref, even_ref, odd_ref, wire_ref):
    fields, wire = halo_x(xe_ref, xo_ref)
    for j, value in enumerate(wire):
        wire_ref[j] = value
    pack_y(fields, wire_ref, even_ref, odd_ref)


def sweep_row(q_ref, t_ref, coeff, j, row, spot, rhs):
    sums = []
    for ref in (q_ref, t_ref):
        own, side = ref[j, 0], ref[j, 1]
        own_sum, side_sum = along_y(own, side, row, 0.0, 0.0)
        own_sum = own_sum + (along_z(own, spot) + (ref[j - 1, 0] + ref[j + 1, 0]))
        side_sum = side_sum + (along_z(side, spot) + (ref[j - 1, 1] + ref[j + 1, 1]))
        sums.append([own_sum, side_sum])
    if rhs is not None:
        sums[0][0] = sums[0][0] + rhs[0]
        sums[1][0] = sums[1][0] + rhs[1]
    out = []
    for tile in range(2):
        flow, heat = sums[0][tile], sums[1][tile]
        out.append(
            (
                coeff(0, j - 1, tile) * flow + coeff(1, j - 1, tile) * heat,
                coeff(2, j - 1, tile) * flow + coeff(3, j - 1, tile) * heat,
            )
        )
    return out


def subdomain_sweeps(rhs_ref, coeff, solved_ref, rims_ref, even_ref, odd_ref, buffers, rows):
    row, spot = sublane(), lane()
    wide = rows + 2 * MARGIN
    zero = jnp.zeros(TILE, F32)
    for buffer in buffers:
        for j in range(wide + 2):
            for tile in range(2):
                buffer[j, tile] = zero
    current, following = buffers[:2], buffers[2:]
    for x in range(rows):
        j = x + RIM
        flow, heat = rhs_ref[0, x], rhs_ref[1, x]
        current[0][j, 0] = coeff(0, j - 1, 0) * flow + coeff(1, j - 1, 0) * heat
        current[1][j, 0] = coeff(2, j - 1, 0) * flow + coeff(3, j - 1, 0) * heat
    first, _, _ = position("gy")
    even_low = (row < 4) != first
    for sweep in range(1, SWEEPS):
        reach = min(sweep, MARGIN)
        for x in range(-reach, rows + reach):
            j = x + RIM
            rhs = (rhs_ref[0, x], rhs_ref[1, x]) if 0 <= x < rows else None
            out = sweep_row(current[0], current[1], coeff, j, row, spot, rhs)
            if sweep < SWEEPS - 1:
                for tile in range(2):
                    following[0][j, tile] = out[tile][0]
                    following[1][j, tile] = out[tile][1]
            else:
                i = j - 1
                (own_q, own_t), (side_q, side_t) = out
                solved_ref[0, i], solved_ref[1, i] = own_q, own_t
                turned = half_turn(side_t)
                even_ref[i] = jnp.where(even_low, turned, side_q)
                odd_ref[i] = jnp.where(even_low, side_q, turned)
                for k, side in enumerate((side_q, side_t)):
                    line = (i // SUB, pl.ds(i % SUB, 1))
                    rims_ref[(2 * k, *line)] = side[7:8]
                    rims_ref[(2 * k + 1, *line)] = side[0:1]
        current, following = following, current
    rows_even, rows_odd = jnp.where(first, 7, 0), jnp.where(first, 0, 7)
    for k in range(2):
        spots = [(solved_ref, (k, i)) for i in range(wide)]
        rim_rows(even_ref, odd_ref, wide + k * (wide // SUB), spots, rows_even, rows_odd)


def getter(own_ref, own_side_ref, rest_ref, rest_side_ref):
    rows = own_ref.shape[1]

    def coeff(k, i, tile):
        ref, rest, start, count = (own_ref, rest_ref, MARGIN, rows)
        if tile:
            ref, rest, start, count = (own_side_ref, rest_side_ref, MARGIN + 1, rows - 2)
        if start <= i < start + count:
            return ref[k, i - start]
        return rest[k, i if i < start else i - count]

    return coeff


def diagonal(tiles, index, spot):
    j, last_up, last_down = index
    own_sum, side_sum = along_y(tiles(j, 0), tiles(j, 1), sublane(), last_up, last_down)
    out = []
    for tile, total in ((0, own_sum), (1, side_sum)):
        if tile == 1 and last_up is None:
            break
        centre = tiles(j, tile)
        total = total + along_z(centre, spot) + (tiles(j - 1, tile) + tiles(j + 1, tile))
        out.append(centre * total)
    return out


def block_tiles(stores, sums, scales, wire):
    press, cross, lower, heat = stores
    gp, gt = scales
    outside = jnp.where(wire > 0.0, 0.0, 1.0)
    a = press + sums[0] + outside
    d = heat + sums[1] + outside
    inverse = 1.0 / (a * d + cross * lower)
    pp, pt, tt = gp * gp * inverse, gp * gt * inverse, gt * gt * inverse
    return a, d, (pp * d, pt * cross, -(pt * lower), tt * a)


def root_tables(props_ref):
    tables = wide_tables(props_ref)
    return [jnp.sqrt(jnp.maximum(table, 0.0)) for table in tables[:2]], tables[2]


def beyond_lines(beyond_ref, g, j):
    return tuple(
        jnp.broadcast_to(beyond_ref[g, end, j // SUB, pl.ds(j % SUB, 1)], TILE) for end in (1, 0)
    )


def own_coefficients_kernel(
    props_ref, fields_ref, wire_ref, xe_ref, xo_ref, ye_ref, yo_ref, source_ref,
    own_ref, own_side_ref, image_ref, scale_ref, rhs_ref, roots_ref, roots_side_ref, beyond_ref,
):
    rows = wire_ref.shape[0]
    spot = lane()
    roots, carried = root_tables(props_ref)
    _, x_wire = halo_x(xe_ref, xo_ref)
    sides, beyond = unpack_wire(ye_ref, yo_ref, rows, rows)
    wire = x_wire[:RIM] + [wire_ref[x] for x in range(rows)] + x_wire[RIM:]
    for g in range(2):
        for j, value in enumerate(wire):
            roots_ref[g, j] = lookup(roots[g], value)
        for x in range(rows):
            roots_side_ref[g, x] = lookup(roots[g], sides[x])
        for tile, ends in enumerate(beyond):
            for end in range(2):
                beyond_ref[g, end, tile] = lookup(roots[g], ends[end])
    for x in range(rows):
        inner = 0 < x < rows - 1
        sums = []
        for g in range(2):
            tiles = lambda j, tile: roots_side_ref[g, j - RIM] if tile else roots_ref[g, j]
            lines = beyond_lines(beyond_ref, g, x) if inner else (None, None)
            sums.append(diagonal(tiles, (x + RIM, *lines), spot))
        stores = [fields_ref[k, x] for k in range(4)]
        gp, gt = (roots_ref[g, x + RIM] for g in range(2))
        a, d, coeffs = block_tiles(stores, (sums[0][0], sums[1][0]), (gp, gt), wire_ref[x])
        for k in range(4):
            own_ref[k, x] = coeffs[k]
        over_p, over_t = 1.0 / gp, 1.0 / gt
        over = over_p * over_t
        image_ref[0, x] = a * (over_p * over_p)
        image_ref[1, x] = -(stores[1] * over)
        image_ref[2, x] = stores[2] * over
        image_ref[3, x] = d * (over_t * over_t)
        for k, value in enumerate((gp, gt, over_p, over_t, lookup(carried, wire_ref[x]))):
            scale_ref[k, x] = value
        rhs_ref[0, x] = source_ref[0, x] * over_p
        rhs_ref[1, x] = source_ref[1, x] * over_t
        if inner:
            stores = unpack_fields(ye_ref, yo_ref, rows, x)
            scales = [roots_side_ref[g, x] for g in range(2)]
            _, _, coeffs = block_tiles(stores, (sums[0][1], sums[1][1]), scales, sides[x])
            for k in range(4):
                own_side_ref[k, x - 1] = coeffs[k]


def first_solve_kernel(
    props_ref, xe_ref, xo_ref, ye_ref, yo_ref, ce_ref, co_ref,
    own_ref, own_side_ref, rhs_ref, roots_ref, roots_side_ref, beyond_ref,
    rest_ref, rest_side_ref, solved_ref, rims_ref, even_ref, odd_ref,
    corner_roots_ref, corner_beyond_ref, *buffers,
):
    rows = own_ref.shape[1]
    wide = rows + 2 * MARGIN
    spot = lane()
    roots, _ = root_tables(props_ref)
    x_fields, x_wire = halo_x(xe_ref, xo_ref)
    sides, beyond = unpack_wire(ce_ref, co_ref, 2 * MARGIN, 2 * RIM)
    own_sides, _ = unpack_wire(ye_ref, yo_ref, rows, rows)
    for g in range(2):
        for j, value in enumerate(sides):
            corner_roots_ref[g, j] = lookup(roots[g], value)
        for tile, ends in enumerate(beyond):
            for end in range(2):
                corner_beyond_ref[g, end, tile] = lookup(roots[g], ends[end])
    for i in list(range(RIM)) + list(range(wide - RIM, wide)):
        j, x = i + 1, i - MARGIN
        own_row = 0 <= x < rows
        sums = []
        for g in range(2):

            def tiles(j, tile):
                if not tile:
                    return roots_ref[g, j]
                if RIM <= j < RIM + rows:
                    return roots_side_ref[g, j - RIM]
                return corner_roots_ref[g, j if j < RIM else j - rows]

            if own_row:
                lines = beyond_lines(beyond_ref, g, x)
            else:
                lines = beyond_lines(corner_beyond_ref, g, j if j < RIM else j - rows)
            sums.append((diagonal(tiles, (j, *lines), spot), tiles(j, 0), tiles(j, 1)))
        corner = i if i < MARGIN else i - rows
        if not own_row:
            stores = [x_fields[k][corner] for k in range(4)]
            scales = (sums[0][1], sums[1][1])
            spare = x_wire[j if j < RIM else j - rows]
            _, _, coeffs = block_tiles(stores, (sums[0][0][0], sums[1][0][0]), scales, spare)
            for k in range(4):
                rest_ref[k, corner] = coeffs[k]
            stores = unpack_fields(ce_ref, co_ref, 2 * MARGIN, corner)
            spare = sides[j if j < RIM else j - rows]
        else:
            stores = unpack_fields(ye_ref, yo_ref, rows, x)
            spare = own_sides[x]
        scales = (sums[0][2], sums[1][2])
        _, _, coeffs = block_tiles(stores, (sums[0][0][1], sums[1][0][1]), scales, spare)
        for k in range(4):
            rest_side_ref[k, i if i < RIM else i - (rows - 2)] = coeffs[k]
    coeff = getter(own_ref, own_side_ref, rest_ref, rest_side_ref)
    subdomain_sweeps(rhs_ref, coeff, solved_ref, rims_ref, even_ref, odd_ref, buffers, rows)


def fold_y_kernel(solved_ref, rims_ref, ye_ref, yo_ref, summed_ref, edges_ref, even_ref, odd_ref):
    wide = solved_ref.shape[1]
    row = sublane()
    first, has_low, has_high = position("gy")
    for i in range(wide):
        low, high = from_sides(first, ye_ref[i], yo_ref[i])
        low = jnp.where(has_low, low, 0.0)
        high = jnp.where(has_high, high, 0.0)
        summed_ref[0, i] = solved_ref[0, i] + jnp.where(row < 4, low, high)
        summed_ref[1, i] = solved_ref[1, i] + half_turn(jnp.where(row < 4, high, low))
    count = wide // SUB
    for k in range(2):
        for tile in range(count):
            spot = wide + k * count + tile
            low, high = from_sides(first, ye_ref[spot], yo_ref[spot])
            edges_ref[2 * k, tile] = rims_ref[2 * k, tile] + jnp.where(has_low, low, 0.0)
            edges_ref[2 * k + 1, tile] = rims_ref[2 * k + 1, tile] + jnp.where(has_high, high, 0.0)
    first, _, _ = position("gx")
    margin_even = jnp.where(first, wide - MARGIN, 0)
    margin_odd = jnp.where(first, 0, wide - MARGIN)
    rim_even = jnp.where(first, wide - MARGIN - 1, MARGIN)
    rim_odd = jnp.where(first, MARGIN, wide - MARGIN - 1)
    for k in range(2):
        base = k * (MARGIN + 2)
        for ref, margin, rim in ((even_ref, margin_even, rim_even), (odd_ref, margin_odd, rim_odd)):
            ref[pl.ds(base, MARGIN)] = summed_ref[k, pl.ds(margin, MARGIN)]
            ref[base + MARGIN] = summed_ref[k, rim]
        to_low = jnp.where(row < 4, edges_ref[2 * k, 0], half_turn(edges_ref[2 * k + 1, 0]))
        last = count - 1
        to_high = jnp.where(row < 4, half_turn(edges_ref[2 * k + 1, last]), edges_ref[2 * k, last])
        even_ref[base + MARGIN + 1] = jnp.where(first, to_high, to_low)
        odd_ref[base + MARGIN + 1] = jnp.where(first, to_low, to_high)


def fold_x(summed_ref, edges_ref, xe_ref, xo_ref, field_refs, edge_ref):
    wide = summed_ref.shape[1]
    rows = wide - 2 * MARGIN
    row = sublane()
    first, has_low, has_high = position("gx")
    for k in range(2):
        base = k * (MARGIN + 2)
        low, high = from_sides(first, xe_ref[pl.ds(base, MARGIN + 2)], xo_ref[pl.ds(base, MARGIN + 2)])
        low = jnp.where(has_low, low, 0.0)
        high = jnp.where(has_high, high, 0.0)
        for x in range(-1, rows + 1):
            value = summed_ref[k, x + MARGIN]
            if 0 <= x < MARGIN:
                value = value + low[x]
            if rows - MARGIN <= x < rows:
                value = value + high[x - (rows - MARGIN)]
            if x == -1:
                value = value + low[MARGIN]
            if x == rows:
                value = value + high[MARGIN]
            field_refs[k][x + 1] = value
        from_low, from_high = low[MARGIN + 1], high[MARGIN + 1]
        last = edge_ref.shape[1] - 1
        for end in range(2):
            for tile in range(last + 1):
                value = edges_ref[2 * k + end, tile]
                if tile == 0:
                    part = half_turn(from_low) if end == 1 else from_low
                    value = value + jnp.where(row < 4, 0.0, part)
                if tile == last:
                    part = half_turn(from_high) if end == 1 else from_high
                    value = value + jnp.where(row < 4, part, 0.0)
                edge_ref[2 * k + end, tile] = value


def image_row(field_refs, edge_ref, image_ref, x, row, spot):
    sums = []
    i = x + MARGIN
    for k, ref in enumerate(field_refs):
        own = ref[x + 1]
        down, up = (
            jnp.broadcast_to(edge_ref[2 * k + end, i // SUB, pl.ds(i % SUB, 1)], TILE) for end in range(2)
        )
        total = jnp.where(row == 7, up, up_y(own)) + jnp.where(row == 0, down, down_y(own))
        sums.append(total + along_z(own, spot) + (ref[x] + ref[x + 2]))
    flow, heat = field_refs[0][x + 1], field_refs[1][x + 1]
    return (
        image_ref[0, x] * flow + image_ref[1, x] * heat - sums[0],
        image_ref[2, x] * flow + image_ref[3, x] * heat - sums[1],
    )


def keep_direction(direction_ref, scale_ref, field_refs, x):
    heat = field_refs[1][x + 1] * scale_ref[3, x]
    direction_ref[1, x] = heat
    direction_ref[0, x] = field_refs[0][x + 1] * scale_ref[2, x] - scale_ref[4, x] * heat


def gram_rows(pairs, row, offset):
    total = jnp.zeros(TILE, F32)
    for index, value in enumerate(pairs):
        line = jnp.broadcast_to(jnp.sum(value, axis=0, keepdims=True), TILE)
        total = total + jnp.where(row == index + offset, line, 0.0)
    return total


def step_kernel(
    summed_ref, edges_ref, xe_ref, xo_ref, own_ref, own_side_ref, rest_ref, rest_side_ref, image_ref, scale_ref, source_ref,
    direction_ref, power_ref, gram_ref, solved_ref, rims_ref, even_ref, odd_ref,
    rhs_ref, q_ref, t_ref, edge_ref, *buffers,
):
    rows = source_ref.shape[1]
    row, spot = sublane(), lane()
    fields = (q_ref, t_ref)
    fold_x(summed_ref, edges_ref, xe_ref, xo_ref, fields, edge_ref)
    products = [jnp.zeros(TILE, F32) for _ in range(3)]
    for x in range(rows):
        keep_direction(direction_ref, scale_ref, fields, x)
        for k, part in enumerate(image_row(fields, edge_ref, image_ref, x, row, spot)):
            source = source_ref[k, x]
            scaled = part - source * scale_ref[2 + k, x]
            power = scaled * scale_ref[k, x]
            rhs_ref[k, x] = scaled
            power_ref[k, x] = power
            products[0] = products[0] + source * source
            products[1] = products[1] + source * power
            products[2] = products[2] + power * power
    gram_ref[...] = gram_rows(products, row, 0)
    coeff = getter(own_ref, own_side_ref, rest_ref, rest_side_ref)
    subdomain_sweeps(rhs_ref, coeff, solved_ref, rims_ref, even_ref, odd_ref, buffers, rows)


def last_kernel(
    summed_ref, edges_ref, xe_ref, xo_ref, image_ref, scale_ref, source_ref, power_ref, gram_in_ref,
    direction_ref, second_ref, gram_ref, q_ref, t_ref, edge_ref,
):
    rows = source_ref.shape[1]
    row, spot = sublane(), lane()
    fields = (q_ref, t_ref)
    fold_x(summed_ref, edges_ref, xe_ref, xo_ref, fields, edge_ref)
    products = [jnp.zeros(TILE, F32) for _ in range(3)]
    for x in range(rows):
        keep_direction(direction_ref, scale_ref, fields, x)
        for k, part in enumerate(image_row(fields, edge_ref, image_ref, x, row, spot)):
            power = power_ref[k, x]
            second = part * scale_ref[k, x] - power
            second_ref[k, x] = second
            products[0] = products[0] + source_ref[k, x] * second
            products[1] = products[1] + power * second
            products[2] = products[2] + second * second
    total = jnp.sum(gram_in_ref[...] + gram_rows(products, row, 3), axis=1, keepdims=True)
    line = jnp.sum(jnp.where(row == spot, jnp.broadcast_to(total, TILE), 0.0), axis=0, keepdims=True)
    gram_ref[...] = jnp.broadcast_to(line, gram_ref.shape)


def combine_kernel(
    gram_ref, source_ref, power_ref, second_ref, one_ref, two_ref,
    adjoint_hbm, residual_hbm, basis_hbm, adjoint_ref, residual_ref, basis_ref, sems, *, scale,
):
    sums = jnp.sum(gram_ref[...], axis=0, keepdims=True)
    spot = lax.broadcasted_iota(jnp.int32, sums.shape, 1)
    g00, g01, g11, g02, g12, g22 = (
        jnp.sum(jnp.where(spot == k, sums, 0.0), axis=1, keepdims=True) for k in range(6)
    )
    beta2 = g00 + EPSILON
    beta = jnp.sqrt(beta2)
    less = (EPSILON - g01) / beta2
    h11 = (g00 + g01) / beta2
    square = (less * less * g00 + 2.0 * less * g01 + g11) / beta2
    square = jnp.maximum(square, 0.0)
    h21 = jnp.sqrt(square + EPSILON)
    b = 1.0 / (beta * h21)
    a = less * b
    h12 = EPSILON * h11 / (beta2 * h21) + (a * g01 + b * g02) / beta
    short = EPSILON / (square + EPSILON) - (a * a * g01 + a * b * (g11 + g02) + b * b * g12)
    h22 = 1.0 - short
    c0 = a * short - h12 / beta
    c1 = a + b * short
    c2 = b
    square = c0 * (c0 * g00 + 2.0 * (c1 * g01 + c2 * g02)) + c1 * (c1 * g11 + 2.0 * c2 * g12) + c2 * c2 * g22
    h32 = jnp.sqrt(jnp.maximum(square, 0.0) + EPSILON)
    n0, n1, n2 = h21 * h32, -h11 * h32, h11 * h22 - h12 * h21
    factor = beta * n0 / (n0 * n0 + n1 * n1 + n2 * n2)
    f0, f1, f2 = factor * n0, factor * n1, factor * n2
    y2 = -f2 / h32
    y1 = (h11 * (beta - f0 - h12 * y2) - h21 * (f1 + h22 * y2)) / (h11 * h11 + h21 * h21)
    over = 1.0 / h32
    v0, v1, v2 = c0 * over, c1 * over, c2 * over
    wide = lambda value: jnp.broadcast_to(value, TILE)
    z_one, z_two = wide(y1 / beta + y2 * a), wide(y2 * b)
    r0, r1, r2 = wide(f0 / beta + f1 * a + f2 * v0), wide(f1 * b + f2 * v1), wide(f2 * v2)
    s0, s1, s2 = wide(scale * v0), wide(scale * v1), wide(scale * v2)
    copies = []
    for k in range(2):
        for x in range(source_ref.shape[1]):
            source, power, second = source_ref[k, x], power_ref[k, x], second_ref[k, x]
            adjoint_ref[k, x] = z_one * one_ref[k, x] + z_two * two_ref[k, x]
            residual_ref[k, x] = r0 * source + r1 * power + r2 * second
            basis_ref[k, x] = s0 * source + s1 * power + s2 * second
        pairs = ((adjoint_ref, adjoint_hbm), (residual_ref, residual_hbm), (basis_ref, basis_hbm))
        for index, (src, dst) in enumerate(pairs):
            copy = pltpu.make_async_copy(src.at[k], dst.at[k], sems.at[k, index])
            copy.start()
            copies.append(copy)
    for copy in copies:
        copy.wait()


def call(kernel, outs, scratch=(), name=None, inside=pltpu.VMEM, outside=pltpu.VMEM):
    def run(*args):
        return pl.pallas_call(
            kernel,
            out_shape=[jax.ShapeDtypeStruct(shape, F32) for shape in outs],
            in_specs=[pl.BlockSpec(memory_space=inside)] * len(args),
            out_specs=[pl.BlockSpec(memory_space=outside)] * len(outs),
            scratch_shapes=[pltpu.VMEM(spec, F32) if isinstance(spec, tuple) else spec for spec in scratch],
            compiler_params=pltpu.CompilerParams(vmem_limit_bytes=32 * 1024 * 1024),
            name=name,
        )(*args)

    return run


def exchange(axis, even, odd):
    n_x, n_y = lax.axis_size("gx"), lax.axis_size("gy")
    count = lax.axis_size(axis)
    pairs = [(i, i ^ 1) for i in range(count)]
    others = []
    for x in range(n_x):
        for y in range(n_y):
            place = x if axis == "gx" else y
            if 0 < place < count - 1:
                partner = ((place - 1) ^ 1) + 1
                target = (partner, y) if axis == "gx" else (x, partner)
            else:
                target = (x, y ^ 1) if axis == "gx" else (x ^ (n_x // 2), y)
            others.append((x * n_y + y, target[0] * n_y + target[1]))
    return lax.ppermute(even, axis, pairs), lax.ppermute(odd, ("gx", "gy"), others)


def shards(adjoint_source, storage, soil_ids, bc_mask, soil_props):
    rows, _, depth = soil_ids.shape
    wide = rows + 2 * MARGIN
    devices = lax.axis_size("gx") * lax.axis_size("gy")
    cells = 2.0 * rows * soil_ids.shape[1] * depth * devices
    own = (rows, *TILE)
    x_slab = (4 * MARGIN + RIM, *TILE)
    slab = y_slab(rows, rows)
    fields, wire, x_even, x_odd, y_even, y_odd = call(
        first_pack_kernel,
        [(4, *own), own, x_slab, x_slab, slab, slab],
        [soil_props.shape, (4, *own), pltpu.VMEM(own, jnp.int32), pltpu.VMEM((SUB, rows), jnp.int32)]
        + [pltpu.SemaphoreType.DMA((4,))],
        name="first_pack",
        inside=pltpu.HBM,
    )(*(pltpu.with_memory_space_constraint(x, pltpu.HBM) for x in (soil_props, storage, soil_ids, bc_mask.T)))
    xe, xo = exchange("gx", x_even, x_odd)
    ye, yo = exchange("gy", y_even, y_odd)
    slab = y_slab(2 * MARGIN, 2 * RIM)
    even, odd = call(corner_pack_kernel, [slab, slab], [(2 * RIM, *TILE)], name="corner_pack")(xe, xo)
    ce, co = exchange("gy", even, odd)
    count = wide // SUB
    own_coeff, own_side, image, scales, rhs, roots, roots_side, beyond = call(
        own_coefficients_kernel,
        [(4, *own), (4, rows - 2, *TILE), (4, *own), (5, *own), (2, *own)]
        + [(2, rows + 2 * RIM, *TILE), (2, *own), (2, 2, -(-rows // SUB), *TILE)],
        name="own_coefficients",
    )(soil_props, fields, wire, xe, xo, ye, yo, adjoint_source)
    buffers = [(wide + 2, 2, *TILE)] * 4
    slab = (wide + 2 * count, *TILE)
    solved_shapes = [(2, wide, *TILE), (4, count, *TILE), slab, slab]
    rest, rest_side, solved, edges, even, odd = call(
        first_solve_kernel,
        [(4, 2 * MARGIN, *TILE), (4, 2 * RIM, *TILE)] + solved_shapes,
        [(2, 2 * RIM, *TILE), (2, 2, -(-2 * RIM // SUB), *TILE)] + buffers,
        name="first_solve",
    )(soil_props, xe, xo, ye, yo, ce, co, own_coeff, own_side, rhs, roots, roots_side, beyond)
    coeffs = (own_coeff, own_side, rest, rest_side)

    slab = (2 * (MARGIN + 2), *TILE)
    fold_shapes = [(2, wide, *TILE), (4, count, *TILE), slab, slab]
    ye, yo = exchange("gy", even, odd)
    summed, edges, even, odd = call(fold_y_kernel, fold_shapes, name="fold_y")(solved, edges, ye, yo)
    xe, xo = exchange("gx", even, odd)
    halo = [(rows + 2, *TILE)] * 2 + [(4, count, *TILE)]
    one, power, gram, solved, edges, even, odd = call(
        step_kernel,
        [(2, *own), (2, *own), TILE] + solved_shapes,
        [(2, *own)] + halo + buffers,
        name="second_solve",
    )(summed, edges, xe, xo, *coeffs, image, scales, adjoint_source)

    ye, yo = exchange("gy", even, odd)
    summed, edges, even, odd = call(fold_y_kernel, fold_shapes, name="fold_y")(solved, edges, ye, yo)
    xe, xo = exchange("gx", even, odd)
    two, second, gram = call(
        last_kernel, [(2, *own), (2, *own), (devices, LANE)], halo, name="last_image"
    )(summed, edges, xe, xo, image, scales, adjoint_source, power, gram)
    gram = lax.all_to_all(gram, ("gx", "gy"), 0, 0, tiled=True)
    return tuple(
        call(
            functools.partial(combine_kernel, scale=math.sqrt(cells)),
            [(2, *own)] * 3,
            [(2, *own)] * 3 + [pltpu.SemaphoreType.DMA((2, 3))],
            name="combine",
            outside=pltpu.HBM,
        )(gram, adjoint_source, power, second, one, two)
    )


def solution(mesh):
    in_specs = (
        P(None, "gx", "gy", None),
        P(None, "gx", "gy", None),
        P("gx", "gy", None),
        P("gx", "gy"),
        P(),
    )
    out_specs = (P(None, "gx", "gy", None), P(None, "gx", "gy", None), P(None, "gx", "gy", None))
    return jax.shard_map(shards, mesh=mesh, in_specs=in_specs, out_specs=out_specs, check_vma=False)
```

```python
import functools
import math

import jax
import jax.numpy as jnp
from jax import lax
from jax.experimental import pallas as pl
from jax.experimental.pallas import tpu as pltpu
from jax.sharding import PartitionSpec as P

MARGIN = 4
SWEEPS = 6
SUB = 8
LANE = 128
TILE = (SUB, LANE)
RIM = MARGIN + 1
EPSILON = 1e-06
F32 = jnp.float32


def sublane():
    return lax.broadcasted_iota(jnp.int32, TILE, 0)


def lane():
    return lax.broadcasted_iota(jnp.int32, TILE, 1)


def up_y(tile):
    return pltpu.roll(tile, SUB - 1, 0)


def down_y(tile):
    return pltpu.roll(tile, 1, 0)


def half_turn(tile):
    return pltpu.roll(tile, SUB // 2, 0)


def along_z(tile, spot):
    above = jnp.where(spot == LANE - 1, 0.0, pltpu.roll(tile, LANE - 1, 1))
    below = jnp.where(spot == 0, 0.0, pltpu.roll(tile, 1, 1))
    return above + below


def along_y(own, side, row, last_up, last_down):
    own_up, own_down = up_y(own), down_y(own)
    side_up, side_down = up_y(side), down_y(side)
    own_sum = jnp.where(row == 7, side_up, own_up) + jnp.where(row == 0, side_down, own_down)
    if last_up is None:
        return own_sum, None
    side_sum = jnp.where(row == 7, own_up, jnp.where(row == 3, last_up, side_up))
    side_sum = side_sum + jnp.where(row == 0, own_down, jnp.where(row == 4, last_down, side_down))
    return own_sum, side_sum


def position(axis):
    place = lax.axis_index(axis)
    first = lax.rem(place, 2) == 0
    return first, place > 0, place < lax.axis_size(axis) - 1


def from_sides(first, even, odd):
    return jnp.where(first, odd, even), jnp.where(first, even, odd)


def lookup(table, wire):
    index = jnp.maximum(wire.astype(jnp.int32) - 1, 0)
    return jnp.where(wire > 0.0, jnp.take_along_axis(table, index, axis=1), 0.0)


def wide_tables(props_ref):
    pad = jnp.zeros((props_ref.shape[0], LANE - props_ref.shape[1]), F32)
    wide = jnp.concatenate([props_ref[...], pad], axis=1)
    return [jnp.broadcast_to(wide[k : k + 1], TILE) for k in range(3)]


def rim_rows(even_ref, odd_ref, base, tiles, rows_even, rows_odd):
    for j, (tile_ref, index) in enumerate(tiles):
        line = (base + j // SUB, pl.ds(j % SUB, 1))
        even_ref[line] = tile_ref[(*index, pl.ds(rows_even, 1))]
        odd_ref[line] = tile_ref[(*index, pl.ds(rows_odd, 1))]


def merge_far(near, far, row):
    far = jnp.where(row == 3, pltpu.roll(far, 3, 0), pltpu.roll(far, 5, 0))
    return jnp.where((row == 3) | (row == 4), far, near)


def split_far(tile, row):
    return jnp.where(row < 4, pltpu.roll(tile, 5, 0), pltpu.roll(tile, 3, 0))


def merge_halves(one, other, row):
    other = jnp.where(row < 4, pltpu.roll(other, 2, 0), pltpu.roll(other, 6, 0))
    return jnp.where((row >= 2) & (row < 6), other, one)


def split_halves(tile, row):
    return jnp.where(row < 4, pltpu.roll(tile, 6, 0), pltpu.roll(tile, 2, 0))


def condense(tiles, row):
    return [
        tiles[3],
        merge_far(tiles[2], tiles[0], row),
        tiles[4],
        merge_far(tiles[5], tiles[7], row),
        merge_halves(tiles[1], tiles[6], row),
    ]


def expand(tiles, row):
    low, low_two, high, high_two, three = tiles
    return [
        split_far(low_two, row), three, low_two, low, high, high_two, split_halves(three, row), split_far(high_two, row),
    ]


def condense_wire(tiles, row):
    four = merge_halves(tiles[1], tiles[8], row)
    low, high = merge_far(tiles[2], tiles[0], row), merge_far(tiles[7], tiles[9], row)
    return [tiles[4], tiles[3], low, four, tiles[5], tiles[6], high, four]


def expand_wire(tiles, row):
    low, low_two, low_three, four, high, high_two, high_three, _ = tiles
    return [
        split_far(low_three, row), four, low_three, low_two, low,
        high, high_two, high_three, split_halves(four, row), split_far(high_three, row),
    ]


def pack_y(fields, wire, edges, even_ref, odd_ref):
    first, _, _ = position("gy")
    even_low = (sublane() < 4) != first
    count, half = len(fields[0]), len(wire) // 2

    def put(spot, one, other):
        other = half_turn(other)
        even_ref[spot] = jnp.where(even_low, one, other)
        odd_ref[spot] = jnp.where(even_low, other, one)

    for pair in range(2):
        for i in range(count):
            put(pair * count + i, fields[2 * pair][i], fields[2 * pair + 1][i])
    for j in range(half):
        put(2 * count + j, wire[j], wire[j + half])
    rows_even, rows_odd = jnp.where(first, 3, 4), jnp.where(first, 4, 3)
    if len(edges) % SUB:
        last = even_ref.shape[0] - 1
        even_ref[last] = odd_ref[last] = jnp.zeros(TILE, F32)
    rim_rows(even_ref, odd_ref, 2 * count + half, edges, rows_even, rows_odd)


def y_slab(count, ids, edges):
    return (2 * count + ids // 2 + -(-edges // SUB), *TILE)


def unpack_fields(even_ref, odd_ref, count, i):
    first, _, _ = position("gy")
    row = sublane()
    out = []
    for pair in range(2):
        low, high = from_sides(first, even_ref[pair * count + i], odd_ref[pair * count + i])
        out.append(jnp.where(row < 4, high, low))
        out.append(half_turn(jnp.where(row < 4, low, high)))
    return out


def unpack_wire(even_ref, odd_ref, count, ids):
    first, has_low, has_high = position("gy")
    row = sublane()

    def sides(spot):
        low, high = from_sides(first, even_ref[spot], odd_ref[spot])
        return jnp.where(has_low, low, 0.0), jnp.where(has_high, high, 0.0)

    one, other = [], []
    for j in range(ids // 2):
        low, high = sides(2 * count + j)
        one.append(jnp.where(row < 4, high, low))
        other.append(half_turn(jnp.where(row < 4, low, high)))
    beyond = [sides(spot) for spot in range(2 * count + ids // 2, even_ref.shape[0])]
    return one + other, beyond


def halo_x(even_ref, odd_ref):
    first, has_low, has_high = position("gx")
    fields = []
    for k in range(4):
        spots = pl.ds(k * MARGIN, MARGIN)
        low, high = from_sides(first, even_ref[spots], odd_ref[spots])
        fields.append([low[i] for i in range(MARGIN)] + [high[i] for i in range(MARGIN)])
    spots = pl.ds(4 * MARGIN, RIM)
    low, high = from_sides(first, even_ref[spots], odd_ref[spots])
    low = jnp.where(has_low, low, 0.0)
    high = jnp.where(has_high, high, 0.0)
    return fields, [low[i] for i in range(RIM)] + [high[i] for i in range(RIM)]


def first_pack_kernel(
    props_hbm, storage_hbm, ids_hbm, bc_hbm,
    fields_ref, wire_ref, x_even_ref, x_odd_ref, y_even_ref, y_odd_ref,
    props_ref, storage_ref, ids_ref, bc_ref, sems,
):
    places = ((ids_hbm, ids_ref), (storage_hbm, storage_ref), (props_hbm, props_ref), (bc_hbm, bc_ref))
    copies = [pltpu.make_async_copy(src, dst, sems.at[k]) for k, (src, dst) in enumerate(places)]
    for copy in copies:
        copy.start()
    rows = ids_ref.shape[0]
    spot = lane()
    for copy in copies:
        copy.wait()
    tables = wide_tables(props_ref)
    fields = [[] for _ in range(4)]
    for x in range(rows):
        wire = (ids_ref[x] + 1).astype(F32)
        wire_ref[x] = wire
        kp = lookup(tables[0], wire)
        carried = lookup(tables[2], wire)
        held = jnp.broadcast_to(bc_ref[:, x : x + 1].astype(F32), TILE)
        bound = jnp.where(spot == LANE - 1, 2.0 * kp * held, 0.0)
        press = storage_ref[0, x]
        lower = storage_ref[1, x]
        fields[0].append(press + bound)
        fields[1].append(carried * press - storage_ref[2, x])
        fields[2].append(lower)
        fields[3].append(storage_ref[3, x] - carried * lower)
        for k in range(4):
            fields_ref[k, x] = fields[k][x]
    first, _, _ = position("gx")
    high, low = rows - MARGIN, 0
    start_even = jnp.where(first, high, low)
    start_odd = jnp.where(first, low, high)
    wire_even = jnp.where(first, rows - RIM, 0)
    wire_odd = jnp.where(first, 0, rows - RIM)
    for k in range(4):
        x_even_ref[pl.ds(k * MARGIN, MARGIN)] = fields_ref[k, pl.ds(start_even, MARGIN)]
        x_odd_ref[pl.ds(k * MARGIN, MARGIN)] = fields_ref[k, pl.ds(start_odd, MARGIN)]
    x_even_ref[pl.ds(4 * MARGIN, RIM)] = wire_ref[pl.ds(wire_even, RIM)]
    x_odd_ref[pl.ds(4 * MARGIN, RIM)] = wire_ref[pl.ds(wire_odd, RIM)]
    wire = [wire_ref[x] for x in range(rows)]
    pack_y(fields, wire, [(wire_ref, (x,)) for x in range(rows)], y_even_ref, y_odd_ref)


def corner_pack_kernel(xe_ref, xo_ref, even_ref, odd_ref, wire_ref):
    row = sublane()
    fields, wire = halo_x(xe_ref, xo_ref)
    fields = [condense(field, row) for field in fields]
    wire_ref[0], wire_ref[1] = wire[RIM - 1], wire[RIM]
    edges = [(wire_ref, (j,)) for j in range(2)]
    pack_y(fields, condense_wire(wire, row), edges, even_ref, odd_ref)


def sweep_row(q_ref, t_ref, coeff, j, row, spot, rhs, count):
    sums = []
    for ref in (q_ref, t_ref):
        own, side = ref[j, 0], ref[j, 1]
        own_sum, side_sum = along_y(own, side, row, *((0.0, 0.0) if count == 2 else (None, None)))
        own_sum = own_sum + (along_z(own, spot) + (ref[j - 1, 0] + ref[j + 1, 0]))
        if count == 2:
            side_sum = side_sum + (along_z(side, spot) + (ref[j - 1, 1] + ref[j + 1, 1]))
        sums.append([own_sum, side_sum])
    if rhs is not None:
        sums[0][0] = sums[0][0] + rhs[0]
        sums[1][0] = sums[1][0] + rhs[1]
    out = []
    for tile in range(count):
        flow, heat = sums[0][tile], sums[1][tile]
        out.append(
            (
                coeff(0, j - 1, tile) * flow + coeff(1, j - 1, tile) * heat,
                coeff(2, j - 1, tile) * flow + coeff(3, j - 1, tile) * heat,
            )
        )
    return out


def subdomain_sweeps(rhs_ref, coeff, solved_ref, rims_ref, even_ref, odd_ref, buffers, rows):
    row, spot = sublane(), lane()
    wide = rows + 2 * MARGIN
    zero = jnp.zeros(TILE, F32)
    for buffer in buffers:
        for j in range(wide + 2):
            for tile in range(2):
                buffer[j, tile] = zero
    current, following = buffers[:2], buffers[2:]
    for x in range(rows):
        j = x + RIM
        flow, heat = rhs_ref[0, x], rhs_ref[1, x]
        current[0][j, 0] = coeff(0, j - 1, 0) * flow + coeff(1, j - 1, 0) * heat
        current[1][j, 0] = coeff(2, j - 1, 0) * flow + coeff(3, j - 1, 0) * heat
    first, _, _ = position("gy")
    even_low = (row < 4) != first
    last = []
    for sweep in range(1, SWEEPS):
        reach = min(sweep, MARGIN)
        for x in range(-reach, rows + reach):
            j = x + RIM
            rhs = (rhs_ref[0, x], rhs_ref[1, x]) if 0 <= x < rows else None
            count = 2 if max(-x, x - rows + 1) < sweep else 1
            out = sweep_row(current[0], current[1], coeff, j, row, spot, rhs, count)
            if sweep < SWEEPS - 1:
                for tile in range(count):
                    following[0][j, tile] = out[tile][0]
                    following[1][j, tile] = out[tile][1]
            else:
                i = j - 1
                (own_q, own_t), (side_q, side_t) = out
                solved_ref[0, i], solved_ref[1, i] = own_q, own_t
                last.append((side_q, side_t))
                for k, side in enumerate((side_q, side_t)):
                    line = (i // SUB, pl.ds(i % SUB, 1))
                    rims_ref[(2 * k, *line)] = side[7:8]
                    rims_ref[(2 * k + 1, *line)] = side[0:1]
        current, following = following, current
    corners = [condense([last[i][k] for i in [*range(MARGIN), *range(rows + MARGIN, wide)]], row) for k in range(2)]
    for i, (flow, heat) in enumerate(last[MARGIN : rows + MARGIN] + list(zip(*corners))):
        heat = half_turn(heat)
        even_ref[i] = jnp.where(even_low, heat, flow)
        odd_ref[i] = jnp.where(even_low, flow, heat)
    rows_even, rows_odd = jnp.where(first, 7, 0), jnp.where(first, 0, 7)
    for k in range(2):
        spots = [(solved_ref, (k, i)) for i in range(wide)]
        rim_rows(even_ref, odd_ref, rows + 5 + k * (wide // SUB), spots, rows_even, rows_odd)


def getter(own_ref, own_side_ref, rest_ref, rest_side_ref):
    rows = own_ref.shape[1]

    def coeff(k, i, tile):
        ref, rest, start, count = (own_ref, rest_ref, MARGIN, rows)
        if tile:
            ref, rest, start, count = (own_side_ref, rest_side_ref, MARGIN + 1, rows - 2)
        if start <= i < start + count:
            return ref[k, i - start]
        return rest[k, i if i < start else i - count]

    return coeff


def diagonal(tiles, index, spot):
    j, last_up, last_down = index
    own_sum, side_sum = along_y(tiles(j, 0), tiles(j, 1), sublane(), last_up, last_down)
    out = []
    for tile, total in ((0, own_sum), (1, side_sum)):
        if tile == 1 and last_up is None:
            break
        centre = tiles(j, tile)
        total = total + along_z(centre, spot) + (tiles(j - 1, tile) + tiles(j + 1, tile))
        out.append(centre * total)
    return out


def block_tiles(stores, sums, scales, wire):
    press, cross, lower, heat = stores
    gp, gt = scales
    outside = jnp.where(wire > 0.0, 0.0, 1.0)
    a = press + sums[0] + outside
    d = heat + sums[1] + outside
    inverse = 1.0 / (a * d + cross * lower)
    pp, pt, tt = gp * gp * inverse, gp * gt * inverse, gt * gt * inverse
    return a, d, (pp * d, pt * cross, -(pt * lower), tt * a)


def root_tables(props_ref):
    tables = wide_tables(props_ref)
    return [jnp.sqrt(jnp.maximum(table, 0.0)) for table in tables[:2]], tables[2]


def beyond_lines(beyond_ref, g, j):
    return tuple(
        jnp.broadcast_to(beyond_ref[g, end, j // SUB, pl.ds(j % SUB, 1)], TILE) for end in (1, 0)
    )


def own_coefficients_kernel(
    props_ref, fields_ref, wire_ref, xe_ref, xo_ref, ye_ref, yo_ref, source_ref,
    own_ref, own_side_ref, image_ref, scale_ref, rhs_ref, roots_ref, roots_side_ref, beyond_ref,
):
    rows = wire_ref.shape[0]
    spot = lane()
    roots, carried = root_tables(props_ref)
    _, x_wire = halo_x(xe_ref, xo_ref)
    sides, beyond = unpack_wire(ye_ref, yo_ref, rows, rows)
    wire = x_wire[:RIM] + [wire_ref[x] for x in range(rows)] + x_wire[RIM:]
    for g in range(2):
        for j, value in enumerate(wire):
            roots_ref[g, j] = lookup(roots[g], value)
        for x in range(rows):
            roots_side_ref[g, x] = lookup(roots[g], sides[x])
        for tile, ends in enumerate(beyond):
            for end in range(2):
                beyond_ref[g, end, tile] = lookup(roots[g], ends[end])
    for x in range(rows):
        inner = 0 < x < rows - 1
        sums = []
        for g in range(2):
            tiles = lambda j, tile: roots_side_ref[g, j - RIM] if tile else roots_ref[g, j]
            lines = beyond_lines(beyond_ref, g, x) if inner else (None, None)
            sums.append(diagonal(tiles, (x + RIM, *lines), spot))
        stores = [fields_ref[k, x] for k in range(4)]
        gp, gt = (roots_ref[g, x + RIM] for g in range(2))
        a, d, coeffs = block_tiles(stores, (sums[0][0], sums[1][0]), (gp, gt), wire_ref[x])
        for k in range(4):
            own_ref[k, x] = coeffs[k]
        over_p, over_t = 1.0 / gp, 1.0 / gt
        over = over_p * over_t
        image_ref[0, x] = a * (over_p * over_p)
        image_ref[1, x] = -(stores[1] * over)
        image_ref[2, x] = stores[2] * over
        image_ref[3, x] = d * (over_t * over_t)
        for k, value in enumerate((gp, gt, over_p, over_t, lookup(carried, wire_ref[x]))):
            scale_ref[k, x] = value
        rhs_ref[0, x] = source_ref[0, x] * over_p
        rhs_ref[1, x] = source_ref[1, x] * over_t
        if inner:
            stores = unpack_fields(ye_ref, yo_ref, rows, x)
            scales = [roots_side_ref[g, x] for g in range(2)]
            _, _, coeffs = block_tiles(stores, (sums[0][1], sums[1][1]), scales, sides[x])
            for k in range(4):
                own_side_ref[k, x - 1] = coeffs[k]


def first_solve_kernel(
    props_ref, xe_ref, xo_ref, ye_ref, yo_ref, ce_ref, co_ref,
    own_ref, own_side_ref, rhs_ref, roots_ref, roots_side_ref, beyond_ref,
    rest_ref, rest_side_ref, solved_ref, rims_ref, even_ref, odd_ref,
    corner_roots_ref, corner_beyond_ref, *buffers,
):
    rows = own_ref.shape[1]
    wide = rows + 2 * MARGIN
    spot = lane()
    roots, _ = root_tables(props_ref)
    x_fields, x_wire = halo_x(xe_ref, xo_ref)
    row = sublane()
    sides, beyond = unpack_wire(ce_ref, co_ref, 5, 8)
    sides = expand_wire(sides, row)
    corner_stores = [unpack_fields(ce_ref, co_ref, 5, i) for i in range(5)]
    corner_stores = [expand([stores[k] for stores in corner_stores], row) for k in range(4)]
    own_sides, _ = unpack_wire(ye_ref, yo_ref, rows, rows)
    for g in range(2):
        for j, value in enumerate(sides):
            corner_roots_ref[g, j] = lookup(roots[g], value)
        for tile, ends in enumerate(beyond):
            for end in range(2):
                corner_beyond_ref[g, end, tile] = lookup(roots[g], ends[end])
    for i in list(range(RIM)) + list(range(wide - RIM, wide)):
        j, x = i + 1, i - MARGIN
        own_row = 0 <= x < rows
        sums = []
        for g in range(2):

            def tiles(j, tile):
                if not tile:
                    return roots_ref[g, j]
                if RIM <= j < RIM + rows:
                    return roots_side_ref[g, j - RIM]
                return corner_roots_ref[g, j if j < RIM else j - rows]

            if own_row:
                lines = beyond_lines(beyond_ref, g, x)
            else:
                lines = beyond_lines(corner_beyond_ref, g, 0 if j < RIM else 1)
            sums.append((diagonal(tiles, (j, *lines), spot), tiles(j, 0), tiles(j, 1)))
        corner = i if i < MARGIN else i - rows
        if not own_row:
            stores = [x_fields[k][corner] for k in range(4)]
            scales = (sums[0][1], sums[1][1])
            spare = x_wire[j if j < RIM else j - rows]
            _, _, coeffs = block_tiles(stores, (sums[0][0][0], sums[1][0][0]), scales, spare)
            for k in range(4):
                rest_ref[k, corner] = coeffs[k]
            stores = [corner_stores[k][corner] for k in range(4)]
            spare = sides[j if j < RIM else j - rows]
        else:
            stores = unpack_fields(ye_ref, yo_ref, rows, x)
            spare = own_sides[x]
        scales = (sums[0][2], sums[1][2])
        _, _, coeffs = block_tiles(stores, (sums[0][0][1], sums[1][0][1]), scales, spare)
        for k in range(4):
            rest_side_ref[k, i if i < RIM else i - (rows - 2)] = coeffs[k]
    coeff = getter(own_ref, own_side_ref, rest_ref, rest_side_ref)
    subdomain_sweeps(rhs_ref, coeff, solved_ref, rims_ref, even_ref, odd_ref, buffers, rows)


def fold_y_kernel(solved_ref, rims_ref, ye_ref, yo_ref, summed_ref, edges_ref, even_ref, odd_ref):
    wide = solved_ref.shape[1]
    row = sublane()
    first, has_low, has_high = position("gy")
    rows = wide - 2 * MARGIN
    tiles = [[], []]
    for i in range(rows + 5):
        low, high = from_sides(first, ye_ref[i], yo_ref[i])
        low = jnp.where(has_low, low, 0.0)
        high = jnp.where(has_high, high, 0.0)
        tiles[0].append(jnp.where(row < 4, low, high))
        tiles[1].append(half_turn(jnp.where(row < 4, high, low)))
    for k in range(2):
        corners = expand(tiles[k][rows:], row)
        for spot, reach in enumerate((1, 2, 3, 4, 4, 3, 2, 1)):
            if reach < 4:
                corners[spot] = jnp.where((row < reach) | (row >= SUB - reach), corners[spot], 0.0)
        for i, value in enumerate(corners[:MARGIN] + tiles[k][:rows] + corners[MARGIN:]):
            summed_ref[k, i] = solved_ref[k, i] + value
    count = wide // SUB
    for k in range(2):
        for tile in range(count):
            spot = rows + 5 + k * count + tile
            low, high = from_sides(first, ye_ref[spot], yo_ref[spot])
            edges_ref[2 * k, tile] = rims_ref[2 * k, tile] + jnp.where(has_low, low, 0.0)
            edges_ref[2 * k + 1, tile] = rims_ref[2 * k + 1, tile] + jnp.where(has_high, high, 0.0)
    first, _, _ = position("gx")
    margin_even = jnp.where(first, wide - MARGIN, 0)
    margin_odd = jnp.where(first, 0, wide - MARGIN)
    rim_even = jnp.where(first, wide - MARGIN - 1, MARGIN)
    rim_odd = jnp.where(first, MARGIN, wide - MARGIN - 1)
    for k in range(2):
        base = k * (MARGIN + 2)
        for ref, margin, rim in ((even_ref, margin_even, rim_even), (odd_ref, margin_odd, rim_odd)):
            ref[pl.ds(base, MARGIN)] = summed_ref[k, pl.ds(margin, MARGIN)]
            ref[base + MARGIN] = summed_ref[k, rim]
        to_low = jnp.where(row < 4, edges_ref[2 * k, 0], half_turn(edges_ref[2 * k + 1, 0]))
        last = count - 1
        to_high = jnp.where(row < 4, half_turn(edges_ref[2 * k + 1, last]), edges_ref[2 * k, last])
        even_ref[base + MARGIN + 1] = jnp.where(first, to_high, to_low)
        odd_ref[base + MARGIN + 1] = jnp.where(first, to_low, to_high)


def fold_x(summed_ref, edges_ref, xe_ref, xo_ref, field_refs, edge_ref):
    wide = summed_ref.shape[1]
    rows = wide - 2 * MARGIN
    row = sublane()
    first, has_low, has_high = position("gx")
    for k in range(2):
        base = k * (MARGIN + 2)
        low, high = from_sides(first, xe_ref[pl.ds(base, MARGIN + 2)], xo_ref[pl.ds(base, MARGIN + 2)])
        low = jnp.where(has_low, low, 0.0)
        high = jnp.where(has_high, high, 0.0)
        for x in range(-1, rows + 1):
            value = summed_ref[k, x + MARGIN]
            if 0 <= x < MARGIN:
                value = value + low[x]
            if rows - MARGIN <= x < rows:
                value = value + high[x - (rows - MARGIN)]
            if x == -1:
                value = value + low[MARGIN]
            if x == rows:
                value = value + high[MARGIN]
            field_refs[k][x + 1] = value
        from_low, from_high = low[MARGIN + 1], high[MARGIN + 1]
        last = edge_ref.shape[1] - 1
        for end in range(2):
            for tile in range(last + 1):
                value = edges_ref[2 * k + end, tile]
                if tile == 0:
                    part = half_turn(from_low) if end == 1 else from_low
                    value = value + jnp.where(row < 4, 0.0, part)
                if tile == last:
                    part = half_turn(from_high) if end == 1 else from_high
                    value = value + jnp.where(row < 4, part, 0.0)
                edge_ref[2 * k + end, tile] = value


def image_row(field_refs, edge_ref, image_ref, x, row, spot):
    sums = []
    i = x + MARGIN
    for k, ref in enumerate(field_refs):
        own = ref[x + 1]
        down, up = (
            jnp.broadcast_to(edge_ref[2 * k + end, i // SUB, pl.ds(i % SUB, 1)], TILE) for end in range(2)
        )
        total = jnp.where(row == 7, up, up_y(own)) + jnp.where(row == 0, down, down_y(own))
        sums.append(total + along_z(own, spot) + (ref[x] + ref[x + 2]))
    flow, heat = field_refs[0][x + 1], field_refs[1][x + 1]
    return (
        image_ref[0, x] * flow + image_ref[1, x] * heat - sums[0],
        image_ref[2, x] * flow + image_ref[3, x] * heat - sums[1],
    )


def keep_direction(direction_ref, scale_ref, field_refs, x):
    heat = field_refs[1][x + 1] * scale_ref[3, x]
    direction_ref[1, x] = heat
    direction_ref[0, x] = field_refs[0][x + 1] * scale_ref[2, x] - scale_ref[4, x] * heat


def gram_rows(pairs, row, offset):
    total = jnp.zeros(TILE, F32)
    for index, value in enumerate(pairs):
        line = jnp.broadcast_to(jnp.sum(value, axis=0, keepdims=True), TILE)
        total = total + jnp.where(row == index + offset, line, 0.0)
    return total


def step_kernel(
    summed_ref, edges_ref, xe_ref, xo_ref, own_ref, own_side_ref, rest_ref, rest_side_ref, image_ref, scale_ref, source_ref,
    direction_ref, power_ref, gram_ref, solved_ref, rims_ref, even_ref, odd_ref,
    rhs_ref, q_ref, t_ref, edge_ref, *buffers,
):
    rows = source_ref.shape[1]
    row, spot = sublane(), lane()
    fields = (q_ref, t_ref)
    fold_x(summed_ref, edges_ref, xe_ref, xo_ref, fields, edge_ref)
    products = [jnp.zeros(TILE, F32) for _ in range(3)]
    for x in range(rows):
        keep_direction(direction_ref, scale_ref, fields, x)
        for k, part in enumerate(image_row(fields, edge_ref, image_ref, x, row, spot)):
            source = source_ref[k, x]
            scaled = part - source * scale_ref[2 + k, x]
            power = scaled * scale_ref[k, x]
            rhs_ref[k, x] = scaled
            power_ref[k, x] = power
            products[0] = products[0] + source * source
            products[1] = products[1] + source * power
            products[2] = products[2] + power * power
    gram_ref[...] = gram_rows(products, row, 0)
    coeff = getter(own_ref, own_side_ref, rest_ref, rest_side_ref)
    subdomain_sweeps(rhs_ref, coeff, solved_ref, rims_ref, even_ref, odd_ref, buffers, rows)


def last_kernel(
    summed_ref, edges_ref, xe_ref, xo_ref, image_ref, scale_ref, source_ref, power_ref, gram_in_ref,
    direction_ref, second_ref, gram_ref, q_ref, t_ref, edge_ref,
):
    rows = source_ref.shape[1]
    row, spot = sublane(), lane()
    fields = (q_ref, t_ref)
    fold_x(summed_ref, edges_ref, xe_ref, xo_ref, fields, edge_ref)
    products = [jnp.zeros(TILE, F32) for _ in range(3)]
    for x in range(rows):
        keep_direction(direction_ref, scale_ref, fields, x)
        for k, part in enumerate(image_row(fields, edge_ref, image_ref, x, row, spot)):
            power = power_ref[k, x]
            second = part * scale_ref[k, x] - power
            second_ref[k, x] = second
            products[0] = products[0] + source_ref[k, x] * second
            products[1] = products[1] + power * second
            products[2] = products[2] + second * second
    total = jnp.sum(gram_in_ref[...] + gram_rows(products, row, 3), axis=1, keepdims=True)
    line = jnp.sum(jnp.where(row == spot, jnp.broadcast_to(total, TILE), 0.0), axis=0, keepdims=True)
    gram_ref[...] = jnp.broadcast_to(line, gram_ref.shape)


def combine_kernel(
    gram_ref, source_ref, power_ref, second_ref, one_ref, two_ref,
    adjoint_hbm, residual_hbm, basis_hbm, adjoint_ref, residual_ref, basis_ref, sems, *, scale,
):
    sums = jnp.sum(gram_ref[...], axis=0, keepdims=True)
    spot = lax.broadcasted_iota(jnp.int32, sums.shape, 1)
    g00, g01, g11, g02, g12, g22 = (
        jnp.sum(jnp.where(spot == k, sums, 0.0), axis=1, keepdims=True) for k in range(6)
    )
    beta2 = g00 + EPSILON
    beta = jnp.sqrt(beta2)
    less = (EPSILON - g01) / beta2
    h11 = (g00 + g01) / beta2
    square = (less * less * g00 + 2.0 * less * g01 + g11) / beta2
    square = jnp.maximum(square, 0.0)
    h21 = jnp.sqrt(square + EPSILON)
    b = 1.0 / (beta * h21)
    a = less * b
    h12 = EPSILON * h11 / (beta2 * h21) + (a * g01 + b * g02) / beta
    short = EPSILON / (square + EPSILON) - (a * a * g01 + a * b * (g11 + g02) + b * b * g12)
    h22 = 1.0 - short
    c0 = a * short - h12 / beta
    c1 = a + b * short
    c2 = b
    square = c0 * (c0 * g00 + 2.0 * (c1 * g01 + c2 * g02)) + c1 * (c1 * g11 + 2.0 * c2 * g12) + c2 * c2 * g22
    h32 = jnp.sqrt(jnp.maximum(square, 0.0) + EPSILON)
    n0, n1, n2 = h21 * h32, -h11 * h32, h11 * h22 - h12 * h21
    factor = beta * n0 / (n0 * n0 + n1 * n1 + n2 * n2)
    f0, f1, f2 = factor * n0, factor * n1, factor * n2
    y2 = -f2 / h32
    y1 = (h11 * (beta - f0 - h12 * y2) - h21 * (f1 + h22 * y2)) / (h11 * h11 + h21 * h21)
    over = 1.0 / h32
    v0, v1, v2 = c0 * over, c1 * over, c2 * over
    wide = lambda value: jnp.broadcast_to(value, TILE)
    z_one, z_two = wide(y1 / beta + y2 * a), wide(y2 * b)
    r0, r1, r2 = wide(f0 / beta + f1 * a + f2 * v0), wide(f1 * b + f2 * v1), wide(f2 * v2)
    s0, s1, s2 = wide(scale * v0), wide(scale * v1), wide(scale * v2)
    copies = []
    for k in range(2):
        for x in range(source_ref.shape[1]):
            source, power, second = source_ref[k, x], power_ref[k, x], second_ref[k, x]
            adjoint_ref[k, x] = z_one * one_ref[k, x] + z_two * two_ref[k, x]
            residual_ref[k, x] = r0 * source + r1 * power + r2 * second
            basis_ref[k, x] = s0 * source + s1 * power + s2 * second
        pairs = ((adjoint_ref, adjoint_hbm), (residual_ref, residual_hbm), (basis_ref, basis_hbm))
        for index, (src, dst) in enumerate(pairs):
            copy = pltpu.make_async_copy(src.at[k], dst.at[k], sems.at[k, index])
            copy.start()
            copies.append(copy)
    for copy in copies:
        copy.wait()


def call(kernel, outs, scratch=(), name=None, inside=pltpu.VMEM, outside=pltpu.VMEM, cost=None):
    def run(*args):
        return pl.pallas_call(
            kernel,
            out_shape=[jax.ShapeDtypeStruct(shape, F32) for shape in outs],
            in_specs=[pl.BlockSpec(memory_space=inside)] * len(args),
            out_specs=[pl.BlockSpec(memory_space=outside)] * len(outs),
            scratch_shapes=[pltpu.VMEM(spec, F32) if isinstance(spec, tuple) else spec for spec in scratch],
            compiler_params=pltpu.CompilerParams(vmem_limit_bytes=32 * 1024 * 1024),
            name=name,
            cost_estimate=cost,
        )(*args)

    return run


def exchange(axis, even, odd):
    n_x, n_y = lax.axis_size("gx"), lax.axis_size("gy")
    count = lax.axis_size(axis)
    pairs = [(i, i ^ 1) for i in range(count)]
    others = []
    for x in range(n_x):
        for y in range(n_y):
            place = x if axis == "gx" else y
            if 0 < place < count - 1:
                partner = ((place - 1) ^ 1) + 1
                target = (partner, y) if axis == "gx" else (x, partner)
            else:
                target = (x, y ^ 1) if axis == "gx" else (x ^ (n_x // 2), y)
            others.append((x * n_y + y, target[0] * n_y + target[1]))
    return lax.ppermute(even, axis, pairs), lax.ppermute(odd, ("gx", "gy"), others)


def shards(adjoint_source, storage, soil_ids, bc_mask, soil_props):
    rows, _, depth = soil_ids.shape
    wide = rows + 2 * MARGIN
    devices = lax.axis_size("gx") * lax.axis_size("gy")
    cells = 2.0 * rows * soil_ids.shape[1] * depth * devices
    own = (rows, *TILE)
    x_slab = (4 * MARGIN + RIM, *TILE)
    slab = y_slab(rows, rows, rows)
    fields, wire, x_even, x_odd, y_even, y_odd = call(
        first_pack_kernel,
        [(4, *own), own, x_slab, x_slab, slab, slab],
        [soil_props.shape, (4, *own), pltpu.VMEM(own, jnp.int32), pltpu.VMEM((SUB, rows), jnp.int32)]
        + [pltpu.SemaphoreType.DMA((4,))],
        name="first_pack",
        inside=pltpu.HBM,
    )(*(pltpu.with_memory_space_constraint(x, pltpu.HBM) for x in (soil_props, storage, soil_ids, bc_mask.T)))
    xe, xo = exchange("gx", x_even, x_odd)
    ye, yo = exchange("gy", y_even, y_odd)
    slab = y_slab(5, 8, 2)
    weight = pl.CostEstimate(flops=10**11, bytes_accessed=10**9, transcendentals=0)
    even, odd = call(corner_pack_kernel, [slab, slab], [(2, *TILE)], name="corner_pack", cost=weight)(xe, xo)
    ce, co = exchange("gy", even, odd)
    count = wide // SUB
    own_coeff, own_side, image, scales, rhs, roots, roots_side, beyond = call(
        own_coefficients_kernel,
        [(4, *own), (4, rows - 2, *TILE), (4, *own), (5, *own), (2, *own)]
        + [(2, rows + 2 * RIM, *TILE), (2, *own), (2, 2, -(-rows // SUB), *TILE)],
        name="own_coefficients",
    )(soil_props, fields, wire, xe, xo, ye, yo, adjoint_source)
    buffers = [(wide + 2, 2, *TILE)] * 4
    slab = (rows + 5 + 2 * count, *TILE)
    solved_shapes = [(2, wide, *TILE), (4, count, *TILE), slab, slab]
    rest, rest_side, solved, edges, even, odd = call(
        first_solve_kernel,
        [(4, 2 * MARGIN, *TILE), (4, 2 * RIM, *TILE)] + solved_shapes,
        [(2, 2 * RIM, *TILE), (2, 2, 1, *TILE)] + buffers,
        name="first_solve",
    )(soil_props, xe, xo, ye, yo, ce, co, own_coeff, own_side, rhs, roots, roots_side, beyond)
    coeffs = (own_coeff, own_side, rest, rest_side)

    slab = (2 * (MARGIN + 2), *TILE)
    fold_shapes = [(2, wide, *TILE), (4, count, *TILE), slab, slab]
    ye, yo = exchange("gy", even, odd)
    summed, edges, even, odd = call(fold_y_kernel, fold_shapes, name="fold_y")(solved, edges, ye, yo)
    xe, xo = exchange("gx", even, odd)
    halo = [(rows + 2, *TILE)] * 2 + [(4, count, *TILE)]
    one, power, gram, solved, edges, even, odd = call(
        step_kernel,
        [(2, *own), (2, *own), TILE] + solved_shapes,
        [(2, *own)] + halo + buffers,
        name="second_solve",
    )(summed, edges, xe, xo, *coeffs, image, scales, adjoint_source)

    ye, yo = exchange("gy", even, odd)
    summed, edges, even, odd = call(fold_y_kernel, fold_shapes, name="fold_y")(solved, edges, ye, yo)
    xe, xo = exchange("gx", even, odd)
    two, second, gram = call(
        last_kernel, [(2, *own), (2, *own), (devices, LANE)], halo, name="last_image"
    )(summed, edges, xe, xo, image, scales, adjoint_source, power, gram)
    gram = lax.all_to_all(gram, ("gx", "gy"), 0, 0, tiled=True)
    return tuple(
        call(
            functools.partial(combine_kernel, scale=math.sqrt(cells)),
            [(2, *own)] * 3,
            [(2, *own)] * 3 + [pltpu.SemaphoreType.DMA((2, 3))],
            name="combine",
            outside=pltpu.HBM,
        )(gram, adjoint_source, power, second, one, two)
    )


def solution(mesh):
    in_specs = (
        P(None, "gx", "gy", None),
        P(None, "gx", "gy", None),
        P("gx", "gy", None),
        P("gx", "gy"),
        P(),
    )
    out_specs = (P(None, "gx", "gy", None), P(None, "gx", "gy", None), P(None, "gx", "gy", None))
    return jax.shard_map(shards, mesh=mesh, in_specs=in_specs, out_specs=out_specs, check_vma=False)
```

```python
import functools
import math

import jax
import jax.numpy as jnp
from jax import lax
from jax.experimental import pallas as pl
from jax.experimental.pallas import tpu as pltpu
from jax.sharding import PartitionSpec as P

MARGIN = 4
SWEEPS = 6
SUB = 8
LANE = 128
TILE = (SUB, LANE)
RIM = MARGIN + 1
EPSILON = 1e-06
F32 = jnp.float32


def sublane():
    return lax.broadcasted_iota(jnp.int32, TILE, 0)


def lane():
    return lax.broadcasted_iota(jnp.int32, TILE, 1)


def up_y(tile):
    return pltpu.roll(tile, SUB - 1, 0)


def down_y(tile):
    return pltpu.roll(tile, 1, 0)


def half_turn(tile):
    return pltpu.roll(tile, SUB // 2, 0)


def along_z(tile, spot):
    above = jnp.where(spot == LANE - 1, 0.0, pltpu.roll(tile, LANE - 1, 1))
    below = jnp.where(spot == 0, 0.0, pltpu.roll(tile, 1, 1))
    return above + below


def along_y(own, side, row, last_up, last_down):
    own_up, own_down = up_y(own), down_y(own)
    side_up, side_down = up_y(side), down_y(side)
    own_sum = jnp.where(row == 7, side_up, own_up) + jnp.where(row == 0, side_down, own_down)
    if last_up is None:
        return own_sum, None
    side_sum = jnp.where(row == 7, own_up, jnp.where(row == 3, last_up, side_up))
    side_sum = side_sum + jnp.where(row == 0, own_down, jnp.where(row == 4, last_down, side_down))
    return own_sum, side_sum


def position(axis):
    place = lax.axis_index(axis)
    first = lax.rem(place, 2) == 0
    return first, place > 0, place < lax.axis_size(axis) - 1


def from_sides(first, even, odd):
    return jnp.where(first, odd, even), jnp.where(first, even, odd)


def lookup(table, wire):
    index = jnp.maximum(wire.astype(jnp.int32) - 1, 0)
    return jnp.where(wire > 0.0, jnp.take_along_axis(table, index, axis=1), 0.0)


def wide_tables(props_ref):
    pad = jnp.zeros((props_ref.shape[0], LANE - props_ref.shape[1]), F32)
    wide = jnp.concatenate([props_ref[...], pad], axis=1)
    return [jnp.broadcast_to(wide[k : k + 1], TILE) for k in range(3)]


def rim_rows(even_ref, odd_ref, base, tiles, rows_even, rows_odd):
    for j, (tile_ref, index) in enumerate(tiles):
        line = (base + j // SUB, pl.ds(j % SUB, 1))
        even_ref[line] = tile_ref[(*index, pl.ds(rows_even, 1))]
        odd_ref[line] = tile_ref[(*index, pl.ds(rows_odd, 1))]


def merge_far(near, far, row):
    far = jnp.where(row == 3, pltpu.roll(far, 3, 0), pltpu.roll(far, 5, 0))
    return jnp.where((row == 3) | (row == 4), far, near)


def split_far(tile, row):
    return jnp.where(row < 4, pltpu.roll(tile, 5, 0), pltpu.roll(tile, 3, 0))


def merge_halves(one, other, row):
    other = jnp.where(row < 4, pltpu.roll(other, 2, 0), pltpu.roll(other, 6, 0))
    return jnp.where((row >= 2) & (row < 6), other, one)


def split_halves(tile, row):
    return jnp.where(row < 4, pltpu.roll(tile, 6, 0), pltpu.roll(tile, 2, 0))


def condense(tiles, row):
    return [
        tiles[3],
        merge_far(tiles[2], tiles[0], row),
        tiles[4],
        merge_far(tiles[5], tiles[7], row),
        merge_halves(tiles[1], tiles[6], row),
    ]


def expand(tiles, row):
    low, low_two, high, high_two, three = tiles
    return [
        split_far(low_two, row), three, low_two, low, high, high_two, split_halves(three, row), split_far(high_two, row),
    ]


def condense_wire(tiles, row):
    four = merge_halves(tiles[1], tiles[8], row)
    low, high = merge_far(tiles[2], tiles[0], row), merge_far(tiles[7], tiles[9], row)
    return [tiles[4], tiles[3], low, four, tiles[5], tiles[6], high, four]


def expand_wire(tiles, row):
    low, low_two, low_three, four, high, high_two, high_three, _ = tiles
    return [
        split_far(low_three, row), four, low_three, low_two, low,
        high, high_two, high_three, split_halves(four, row), split_far(high_three, row),
    ]


def pack_y(fields, wire, edges, even_ref, odd_ref):
    first, _, _ = position("gy")
    even_low = (sublane() < 4) != first
    count, half = len(fields[0]), len(wire) // 2

    def put(spot, one, other):
        other = half_turn(other)
        even_ref[spot] = jnp.where(even_low, one, other)
        odd_ref[spot] = jnp.where(even_low, other, one)

    for pair in range(2):
        for i in range(count):
            put(pair * count + i, fields[2 * pair][i], fields[2 * pair + 1][i])
    for j in range(half):
        put(2 * count + j, wire[j], wire[j + half])
    rows_even, rows_odd = jnp.where(first, 3, 4), jnp.where(first, 4, 3)
    if len(edges) % SUB:
        last = even_ref.shape[0] - 1
        even_ref[last] = odd_ref[last] = jnp.zeros(TILE, F32)
    rim_rows(even_ref, odd_ref, 2 * count + half, edges, rows_even, rows_odd)


def y_slab(count, ids, edges):
    return (2 * count + ids // 2 + -(-edges // SUB), *TILE)


def unpack_fields(even_ref, odd_ref, count, i):
    first, _, _ = position("gy")
    row = sublane()
    out = []
    for pair in range(2):
        low, high = from_sides(first, even_ref[pair * count + i], odd_ref[pair * count + i])
        out.append(jnp.where(row < 4, high, low))
        out.append(half_turn(jnp.where(row < 4, low, high)))
    return out


def unpack_wire(even_ref, odd_ref, count, ids):
    first, has_low, has_high = position("gy")
    row = sublane()

    def sides(spot):
        low, high = from_sides(first, even_ref[spot], odd_ref[spot])
        return jnp.where(has_low, low, 0.0), jnp.where(has_high, high, 0.0)

    one, other = [], []
    for j in range(ids // 2):
        low, high = sides(2 * count + j)
        one.append(jnp.where(row < 4, high, low))
        other.append(half_turn(jnp.where(row < 4, low, high)))
    beyond = [sides(spot) for spot in range(2 * count + ids // 2, even_ref.shape[0])]
    return one + other, beyond


def halo_x(even_ref, odd_ref):
    first, has_low, has_high = position("gx")
    fields = []
    for k in range(4):
        spots = pl.ds(k * MARGIN, MARGIN)
        low, high = from_sides(first, even_ref[spots], odd_ref[spots])
        fields.append([low[i] for i in range(MARGIN)] + [high[i] for i in range(MARGIN)])
    spots = pl.ds(4 * MARGIN, RIM)
    low, high = from_sides(first, even_ref[spots], odd_ref[spots])
    low = jnp.where(has_low, low, 0.0)
    high = jnp.where(has_high, high, 0.0)
    return fields, [low[i] for i in range(RIM)] + [high[i] for i in range(RIM)]


def first_pack_kernel(
    props_hbm, storage_hbm, ids_hbm, bc_hbm,
    fields_ref, wire_ref, x_even_ref, x_odd_ref, y_even_ref, y_odd_ref,
    props_ref, storage_ref, ids_ref, bc_ref, sems,
):
    places = [(ids_hbm, ids_ref), (props_hbm, props_ref), (bc_hbm, bc_ref)]
    places += [(storage_hbm.at[k], storage_ref.at[k]) for k in range(4)]
    copies = [pltpu.make_async_copy(src, dst, sems.at[k]) for k, (src, dst) in enumerate(places)]
    for copy in copies:
        copy.start()
    rows = ids_ref.shape[0]
    spot = lane()
    for copy in copies:
        copy.wait()
    tables = wide_tables(props_ref)
    fields = [[] for _ in range(4)]
    for x in range(rows):
        wire = (ids_ref[x] + 1).astype(F32)
        wire_ref[x] = wire
        kp = lookup(tables[0], wire)
        carried = lookup(tables[2], wire)
        held = jnp.broadcast_to(bc_ref[:, x : x + 1].astype(F32), TILE)
        bound = jnp.where(spot == LANE - 1, 2.0 * kp * held, 0.0)
        press = storage_ref[0, x]
        lower = storage_ref[1, x]
        fields[0].append(press + bound)
        fields[1].append(carried * press - storage_ref[2, x])
        fields[2].append(lower)
        fields[3].append(storage_ref[3, x] - carried * lower)
        for k in range(4):
            fields_ref[k, x] = fields[k][x]
    first, _, _ = position("gx")
    high, low = rows - MARGIN, 0
    start_even = jnp.where(first, high, low)
    start_odd = jnp.where(first, low, high)
    wire_even = jnp.where(first, rows - RIM, 0)
    wire_odd = jnp.where(first, 0, rows - RIM)
    for k in range(4):
        x_even_ref[pl.ds(k * MARGIN, MARGIN)] = fields_ref[k, pl.ds(start_even, MARGIN)]
        x_odd_ref[pl.ds(k * MARGIN, MARGIN)] = fields_ref[k, pl.ds(start_odd, MARGIN)]
    x_even_ref[pl.ds(4 * MARGIN, RIM)] = wire_ref[pl.ds(wire_even, RIM)]
    x_odd_ref[pl.ds(4 * MARGIN, RIM)] = wire_ref[pl.ds(wire_odd, RIM)]
    wire = [wire_ref[x] for x in range(rows)]
    pack_y(fields, wire, [(wire_ref, (x,)) for x in range(rows)], y_even_ref, y_odd_ref)


def corner_pack_kernel(xe_ref, xo_ref, even_ref, odd_ref, wire_ref):
    row = sublane()
    fields, wire = halo_x(xe_ref, xo_ref)
    fields = [condense(field, row) for field in fields]
    wire_ref[0], wire_ref[1] = wire[RIM - 1], wire[RIM]
    edges = [(wire_ref, (j,)) for j in range(2)]
    pack_y(fields, condense_wire(wire, row), edges, even_ref, odd_ref)


def sweep_row(load, coeff, j, row, spot, rhs, count):
    sums = []
    for k in range(2):
        own, side = load(k, j, 0), load(k, j, 1)
        own_sum, side_sum = along_y(own, side, row, *((0.0, 0.0) if count == 2 else (None, None)))
        own_sum = own_sum + (along_z(own, spot) + (load(k, j - 1, 0) + load(k, j + 1, 0)))
        if count == 2:
            side_sum = side_sum + (along_z(side, spot) + (load(k, j - 1, 1) + load(k, j + 1, 1)))
        sums.append([own_sum, side_sum])
    if rhs is not None:
        sums[0][0] = sums[0][0] + rhs[0]
        sums[1][0] = sums[1][0] + rhs[1]
    out = []
    for tile in range(count):
        flow, heat = sums[0][tile], sums[1][tile]
        out.append(
            (
                coeff(0, j - 1, tile) * flow + coeff(1, j - 1, tile) * heat,
                coeff(2, j - 1, tile) * flow + coeff(3, j - 1, tile) * heat,
            )
        )
    return out


def reach_of(sweep, rows):
    reach = min(sweep, MARGIN)
    return [(x, 2 if max(-x, x - rows + 1) < sweep else 1) for x in range(-reach, rows + reach)]


def read_first(rows):
    written = [{(x + RIM, 0) for x in range(rows)}, set()]
    missing = []
    for sweep in range(1, SWEEPS):
        half = (sweep - 1) % 2
        reads = set()
        for x, count in reach_of(sweep, rows):
            j = x + RIM
            reads |= {(j, 0), (j, 1), (j - 1, 0), (j + 1, 0)}
            if count == 2:
                reads |= {(j - 1, 1), (j + 1, 1)}
        missing += [(half, *spot) for spot in sorted(reads - written[half])]
        written[half] |= reads
        written[1 - half] |= {(x + RIM, tile) for x, count in reach_of(sweep, rows) for tile in range(count)}
    return missing


def subdomain_sweeps(rhs_ref, coeff, solved_ref, rims_ref, even_ref, odd_ref, buffers, rows):
    row, spot = sublane(), lane()
    wide = rows + 2 * MARGIN
    zero = jnp.zeros(TILE, F32)
    for half, j, tile in read_first(rows):
        for k in range(2):
            buffers[2 * half + k][j, tile] = zero
    current, following = buffers[:2], buffers[2:]
    for x in range(rows):
        j = x + RIM
        flow, heat = rhs_ref[0, x], rhs_ref[1, x]
        current[0][j, 0] = coeff(0, j - 1, 0) * flow + coeff(1, j - 1, 0) * heat
        current[1][j, 0] = coeff(2, j - 1, 0) * flow + coeff(3, j - 1, 0) * heat
    first, _, _ = position("gy")
    even_low = (row < 4) != first
    last = []
    for sweep in range(1, SWEEPS):
        load = functools.cache(functools.partial(lambda pair, k, j, tile: pair[k][j, tile], current))
        for x, count in reach_of(sweep, rows):
            j = x + RIM
            rhs = (rhs_ref[0, x], rhs_ref[1, x]) if 0 <= x < rows else None
            out = sweep_row(load, coeff, j, row, spot, rhs, count)
            if sweep < SWEEPS - 1:
                for tile in range(count):
                    following[0][j, tile] = out[tile][0]
                    following[1][j, tile] = out[tile][1]
            else:
                i = j - 1
                (own_q, own_t), (side_q, side_t) = out
                solved_ref[0, i], solved_ref[1, i] = own_q, own_t
                last.append((side_q, side_t))
                for k, side in enumerate((side_q, side_t)):
                    line = (i // SUB, pl.ds(i % SUB, 1))
                    rims_ref[(2 * k, *line)] = side[7:8]
                    rims_ref[(2 * k + 1, *line)] = side[0:1]
        current, following = following, current
    corners = [condense([last[i][k] for i in [*range(MARGIN), *range(rows + MARGIN, wide)]], row) for k in range(2)]
    for i, (flow, heat) in enumerate(last[MARGIN : rows + MARGIN] + list(zip(*corners))):
        heat = half_turn(heat)
        even_ref[i] = jnp.where(even_low, heat, flow)
        odd_ref[i] = jnp.where(even_low, flow, heat)
    rows_even, rows_odd = jnp.where(first, 7, 0), jnp.where(first, 0, 7)
    for k in range(2):
        spots = [(solved_ref, (k, i)) for i in range(wide)]
        rim_rows(even_ref, odd_ref, rows + 5 + k * (wide // SUB), spots, rows_even, rows_odd)


def getter(own_ref, own_side_ref, rest_ref, rest_side_ref):
    rows = own_ref.shape[1]

    def coeff(k, i, tile):
        ref, rest, start, count = (own_ref, rest_ref, MARGIN, rows)
        if tile:
            ref, rest, start, count = (own_side_ref, rest_side_ref, MARGIN + 1, rows - 2)
        if start <= i < start + count:
            return ref[k, i - start]
        return rest[k, i if i < start else i - count]

    return coeff


def diagonal(tiles, index, spot):
    j, last_up, last_down = index
    own_sum, side_sum = along_y(tiles(j, 0), tiles(j, 1), sublane(), last_up, last_down)
    out = []
    for tile, total in ((0, own_sum), (1, side_sum)):
        if tile == 1 and last_up is None:
            break
        centre = tiles(j, tile)
        total = total + along_z(centre, spot) + (tiles(j - 1, tile) + tiles(j + 1, tile))
        out.append(centre * total)
    return out


def block_tiles(stores, sums, scales, wire):
    press, cross, lower, heat = stores
    gp, gt = scales
    outside = jnp.where(wire > 0.0, 0.0, 1.0)
    a = press + sums[0] + outside
    d = heat + sums[1] + outside
    inverse = 1.0 / (a * d + cross * lower)
    pp, pt, tt = gp * gp * inverse, gp * gt * inverse, gt * gt * inverse
    return a, d, (pp * d, pt * cross, -(pt * lower), tt * a)


def root_tables(props_ref):
    tables = wide_tables(props_ref)
    return [jnp.sqrt(jnp.maximum(table, 0.0)) for table in tables[:2]], tables[2]


def beyond_lines(beyond_ref, g, j):
    return tuple(
        jnp.broadcast_to(beyond_ref[g, end, j // SUB, pl.ds(j % SUB, 1)], TILE) for end in (1, 0)
    )


def own_coefficients_kernel(
    props_ref, fields_ref, wire_ref, xe_ref, xo_ref, ye_ref, yo_ref, source_ref,
    own_ref, own_side_ref, image_ref, scale_ref, rhs_ref, roots_ref, roots_side_ref, beyond_ref,
):
    rows = wire_ref.shape[0]
    spot = lane()
    roots, carried = root_tables(props_ref)
    _, x_wire = halo_x(xe_ref, xo_ref)
    sides, beyond = unpack_wire(ye_ref, yo_ref, rows, rows)
    wire = x_wire[:RIM] + [wire_ref[x] for x in range(rows)] + x_wire[RIM:]
    for g in range(2):
        for j, value in enumerate(wire):
            roots_ref[g, j] = lookup(roots[g], value)
        for x in range(rows):
            roots_side_ref[g, x] = lookup(roots[g], sides[x])
        for tile, ends in enumerate(beyond):
            for end in range(2):
                beyond_ref[g, end, tile] = lookup(roots[g], ends[end])
    for x in range(rows):
        inner = 0 < x < rows - 1
        sums = []
        for g in range(2):
            tiles = lambda j, tile: roots_side_ref[g, j - RIM] if tile else roots_ref[g, j]
            lines = beyond_lines(beyond_ref, g, x) if inner else (None, None)
            sums.append(diagonal(tiles, (x + RIM, *lines), spot))
        stores = [fields_ref[k, x] for k in range(4)]
        gp, gt = (roots_ref[g, x + RIM] for g in range(2))
        a, d, coeffs = block_tiles(stores, (sums[0][0], sums[1][0]), (gp, gt), wire_ref[x])
        for k in range(4):
            own_ref[k, x] = coeffs[k]
        over_p, over_t = 1.0 / gp, 1.0 / gt
        over = over_p * over_t
        image_ref[0, x] = a * (over_p * over_p)
        image_ref[1, x] = -(stores[1] * over)
        image_ref[2, x] = stores[2] * over
        image_ref[3, x] = d * (over_t * over_t)
        for k, value in enumerate((gp, gt, over_p, over_t, lookup(carried, wire_ref[x]))):
            scale_ref[k, x] = value
        rhs_ref[0, x] = source_ref[0, x] * over_p
        rhs_ref[1, x] = source_ref[1, x] * over_t
        if inner:
            stores = unpack_fields(ye_ref, yo_ref, rows, x)
            scales = [roots_side_ref[g, x] for g in range(2)]
            _, _, coeffs = block_tiles(stores, (sums[0][1], sums[1][1]), scales, sides[x])
            for k in range(4):
                own_side_ref[k, x - 1] = coeffs[k]


def first_solve_kernel(
    props_ref, xe_ref, xo_ref, ye_ref, yo_ref, ce_ref, co_ref,
    own_ref, own_side_ref, rhs_ref, roots_ref, roots_side_ref, beyond_ref,
    rest_ref, rest_side_ref, solved_ref, rims_ref, even_ref, odd_ref,
    corner_roots_ref, corner_beyond_ref, *buffers,
):
    rows = own_ref.shape[1]
    wide = rows + 2 * MARGIN
    spot = lane()
    roots, _ = root_tables(props_ref)
    x_fields, x_wire = halo_x(xe_ref, xo_ref)
    row = sublane()
    sides, beyond = unpack_wire(ce_ref, co_ref, 5, 8)
    sides = expand_wire(sides, row)
    corner_stores = [unpack_fields(ce_ref, co_ref, 5, i) for i in range(5)]
    corner_stores = [expand([stores[k] for stores in corner_stores], row) for k in range(4)]
    own_sides, _ = unpack_wire(ye_ref, yo_ref, rows, rows)
    for g in range(2):
        for j, value in enumerate(sides):
            corner_roots_ref[g, j] = lookup(roots[g], value)
        for tile, ends in enumerate(beyond):
            for end in range(2):
                corner_beyond_ref[g, end, tile] = lookup(roots[g], ends[end])
    for i in list(range(RIM)) + list(range(wide - RIM, wide)):
        j, x = i + 1, i - MARGIN
        own_row = 0 <= x < rows
        sums = []
        for g in range(2):

            def tiles(j, tile):
                if not tile:
                    return roots_ref[g, j]
                if RIM <= j < RIM + rows:
                    return roots_side_ref[g, j - RIM]
                return corner_roots_ref[g, j if j < RIM else j - rows]

            if own_row:
                lines = beyond_lines(beyond_ref, g, x)
            else:
                lines = beyond_lines(corner_beyond_ref, g, 0 if j < RIM else 1)
            sums.append((diagonal(tiles, (j, *lines), spot), tiles(j, 0), tiles(j, 1)))
        corner = i if i < MARGIN else i - rows
        if not own_row:
            stores = [x_fields[k][corner] for k in range(4)]
            scales = (sums[0][1], sums[1][1])
            spare = x_wire[j if j < RIM else j - rows]
            _, _, coeffs = block_tiles(stores, (sums[0][0][0], sums[1][0][0]), scales, spare)
            for k in range(4):
                rest_ref[k, corner] = coeffs[k]
            stores = [corner_stores[k][corner] for k in range(4)]
            spare = sides[j if j < RIM else j - rows]
        else:
            stores = unpack_fields(ye_ref, yo_ref, rows, x)
            spare = own_sides[x]
        scales = (sums[0][2], sums[1][2])
        _, _, coeffs = block_tiles(stores, (sums[0][0][1], sums[1][0][1]), scales, spare)
        for k in range(4):
            rest_side_ref[k, i if i < RIM else i - (rows - 2)] = coeffs[k]
    coeff = getter(own_ref, own_side_ref, rest_ref, rest_side_ref)
    subdomain_sweeps(rhs_ref, coeff, solved_ref, rims_ref, even_ref, odd_ref, buffers, rows)


def fold_y_kernel(solved_ref, rims_ref, ye_ref, yo_ref, summed_ref, edges_ref, even_ref, odd_ref):
    wide = solved_ref.shape[1]
    row = sublane()
    first, has_low, has_high = position("gy")
    rows = wide - 2 * MARGIN
    tiles = [[], []]
    for i in range(rows + 5):
        low, high = from_sides(first, ye_ref[i], yo_ref[i])
        low = jnp.where(has_low, low, 0.0)
        high = jnp.where(has_high, high, 0.0)
        tiles[0].append(jnp.where(row < 4, low, high))
        tiles[1].append(half_turn(jnp.where(row < 4, high, low)))
    for k in range(2):
        corners = expand(tiles[k][rows:], row)
        for spot, reach in enumerate((1, 2, 3, 4, 4, 3, 2, 1)):
            if reach < 4:
                corners[spot] = jnp.where((row < reach) | (row >= SUB - reach), corners[spot], 0.0)
        for i, value in enumerate(corners[:MARGIN] + tiles[k][:rows] + corners[MARGIN:]):
            summed_ref[k, i] = solved_ref[k, i] + value
    count = wide // SUB
    for k in range(2):
        for tile in range(count):
            spot = rows + 5 + k * count + tile
            low, high = from_sides(first, ye_ref[spot], yo_ref[spot])
            edges_ref[2 * k, tile] = rims_ref[2 * k, tile] + jnp.where(has_low, low, 0.0)
            edges_ref[2 * k + 1, tile] = rims_ref[2 * k + 1, tile] + jnp.where(has_high, high, 0.0)
    first, _, _ = position("gx")
    margin_even = jnp.where(first, wide - MARGIN, 0)
    margin_odd = jnp.where(first, 0, wide - MARGIN)
    rim_even = jnp.where(first, wide - MARGIN - 1, MARGIN)
    rim_odd = jnp.where(first, MARGIN, wide - MARGIN - 1)
    for k in range(2):
        base = k * (MARGIN + 2)
        for ref, margin, rim in ((even_ref, margin_even, rim_even), (odd_ref, margin_odd, rim_odd)):
            ref[pl.ds(base, MARGIN)] = summed_ref[k, pl.ds(margin, MARGIN)]
            ref[base + MARGIN] = summed_ref[k, rim]
        to_low = jnp.where(row < 4, edges_ref[2 * k, 0], half_turn(edges_ref[2 * k + 1, 0]))
        last = count - 1
        to_high = jnp.where(row < 4, half_turn(edges_ref[2 * k + 1, last]), edges_ref[2 * k, last])
        even_ref[base + MARGIN + 1] = jnp.where(first, to_high, to_low)
        odd_ref[base + MARGIN + 1] = jnp.where(first, to_low, to_high)


def fold_x(summed_ref, edges_ref, xe_ref, xo_ref, field_refs, edge_ref):
    wide = summed_ref.shape[1]
    rows = wide - 2 * MARGIN
    row = sublane()
    first, has_low, has_high = position("gx")
    for k in range(2):
        base = k * (MARGIN + 2)
        low, high = from_sides(first, xe_ref[pl.ds(base, MARGIN + 2)], xo_ref[pl.ds(base, MARGIN + 2)])
        low = jnp.where(has_low, low, 0.0)
        high = jnp.where(has_high, high, 0.0)
        for x in range(-1, rows + 1):
            value = summed_ref[k, x + MARGIN]
            if 0 <= x < MARGIN:
                value = value + low[x]
            if rows - MARGIN <= x < rows:
                value = value + high[x - (rows - MARGIN)]
            if x == -1:
                value = value + low[MARGIN]
            if x == rows:
                value = value + high[MARGIN]
            field_refs[k][x + 1] = value
        from_low, from_high = low[MARGIN + 1], high[MARGIN + 1]
        last = edge_ref.shape[1] - 1
        for end in range(2):
            for tile in range(last + 1):
                value = edges_ref[2 * k + end, tile]
                if tile == 0:
                    part = half_turn(from_low) if end == 1 else from_low
                    value = value + jnp.where(row < 4, 0.0, part)
                if tile == last:
                    part = half_turn(from_high) if end == 1 else from_high
                    value = value + jnp.where(row < 4, part, 0.0)
                edge_ref[2 * k + end, tile] = value


def image_row(field_refs, edge_ref, image_ref, x, row, spot):
    sums = []
    i = x + MARGIN
    for k, ref in enumerate(field_refs):
        own = ref[x + 1]
        down, up = (
            jnp.broadcast_to(edge_ref[2 * k + end, i // SUB, pl.ds(i % SUB, 1)], TILE) for end in range(2)
        )
        total = jnp.where(row == 7, up, up_y(own)) + jnp.where(row == 0, down, down_y(own))
        sums.append(total + along_z(own, spot) + (ref[x] + ref[x + 2]))
    flow, heat = field_refs[0][x + 1], field_refs[1][x + 1]
    return (
        image_ref[0, x] * flow + image_ref[1, x] * heat - sums[0],
        image_ref[2, x] * flow + image_ref[3, x] * heat - sums[1],
    )


def keep_direction(direction_ref, scale_ref, field_refs, x):
    heat = field_refs[1][x + 1] * scale_ref[3, x]
    direction_ref[1, x] = heat
    direction_ref[0, x] = field_refs[0][x + 1] * scale_ref[2, x] - scale_ref[4, x] * heat


def gram_rows(pairs, row, offset):
    total = jnp.zeros(TILE, F32)
    for index, value in enumerate(pairs):
        line = jnp.broadcast_to(jnp.sum(value, axis=0, keepdims=True), TILE)
        total = total + jnp.where(row == index + offset, line, 0.0)
    return total


def step_kernel(
    summed_ref, edges_ref, xe_ref, xo_ref, own_ref, own_side_ref, rest_ref, rest_side_ref, image_ref, scale_ref, source_ref,
    rhs_ref, q_ref, t_ref, solved_ref, rims_ref, even_ref, odd_ref, edge_ref, *buffers,
):
    rows = source_ref.shape[1]
    row, spot = sublane(), lane()
    fields = (q_ref, t_ref)
    fold_x(summed_ref, edges_ref, xe_ref, xo_ref, fields, edge_ref)
    for x in range(rows):
        for k, part in enumerate(image_row(fields, edge_ref, image_ref, x, row, spot)):
            rhs_ref[k, x] = part - source_ref[k, x] * scale_ref[2 + k, x]
    coeff = getter(own_ref, own_side_ref, rest_ref, rest_side_ref)
    subdomain_sweeps(rhs_ref, coeff, solved_ref, rims_ref, even_ref, odd_ref, buffers, rows)


def power_kernel(
    rhs_ref, q_ref, t_ref, scale_ref, source_ref, direction_ref, power_ref, shifted_ref, shift_ref, gram_ref
):
    rows = source_ref.shape[1]
    row, spot = sublane(), lane()
    square = along = jnp.zeros(TILE, F32)
    for x in range(rows):
        keep_direction(direction_ref, scale_ref, (q_ref, t_ref), x)
        for k in range(2):
            source = source_ref[k, x]
            power = rhs_ref[k, x] * scale_ref[k, x]
            power_ref[k, x] = power
            square = square + source * source
            along = along + source * power
    square_sum, along_sum = (
        jnp.sum(jnp.sum(value, axis=0, keepdims=True), axis=1, keepdims=True) for value in (square, along)
    )
    shift = jnp.broadcast_to(along_sum / jnp.maximum(square_sum, 1e-30), TILE)
    shift_ref[...] = shift
    products = [square, jnp.zeros(TILE, F32), jnp.zeros(TILE, F32)]
    for x in range(rows):
        for k in range(2):
            source = source_ref[k, x]
            shifted = power_ref[k, x] - shift * source
            shifted_ref[k, x] = shifted
            products[1] = products[1] + source * shifted
            products[2] = products[2] + shifted * shifted
    gram_ref[...] = gram_rows(products, row, 0) + jnp.where((row == 6) & (spot == 0), shift, 0.0)


def last_kernel(
    summed_ref, edges_ref, xe_ref, xo_ref, image_ref, scale_ref,
    source_ref, power_ref, shifted_in_ref, shift_ref, gram_in_ref,
    direction_ref, second_ref, gram_ref, q_ref, t_ref, edge_ref,
):
    rows = source_ref.shape[1]
    row, spot = sublane(), lane()
    fields = (q_ref, t_ref)
    fold_x(summed_ref, edges_ref, xe_ref, xo_ref, fields, edge_ref)
    products = [jnp.zeros(TILE, F32) for _ in range(3)]
    for x in range(rows):
        keep_direction(direction_ref, scale_ref, fields, x)
        for k, part in enumerate(image_row(fields, edge_ref, image_ref, x, row, spot)):
            power = power_ref[k, x]
            second = part * scale_ref[k, x] - power
            second_ref[k, x] = second
            shifted = second - shift_ref[...] * power
            products[0] = products[0] + source_ref[k, x] * shifted
            products[1] = products[1] + shifted_in_ref[k, x] * shifted
            products[2] = products[2] + shifted * shifted
    total = jnp.sum(gram_in_ref[...] + gram_rows(products, row, 3), axis=1, keepdims=True)
    line = jnp.sum(jnp.where(row == spot, jnp.broadcast_to(total, TILE), 0.0), axis=0, keepdims=True)
    gram_ref[...] = jnp.broadcast_to(line, gram_ref.shape)


def combine_kernel(
    gram_ref, source_ref, power_ref, second_ref, one_ref, two_ref,
    adjoint_hbm, residual_hbm, basis_hbm, adjoint_ref, residual_ref, basis_ref, sems, *, scale,
):
    parts = gram_ref[...]
    spot = lax.broadcasted_iota(jnp.int32, parts.shape, 1)
    p00, p01, p11, p02, p12, p22, shift_of = (
        jnp.sum(jnp.where(spot == k, parts, 0.0), axis=1, keepdims=True) for k in range(7)
    )
    total = lambda value: jnp.sum(value, axis=0, keepdims=True)
    g00 = total(p00)
    shift = total(shift_of * p00) / jnp.maximum(g00, 1e-30)
    e = shift_of - shift
    f = e * shift_of
    mixed = p02 + e * p01 + f * p00
    g01 = total(p01 + e * p00)
    g11 = total(p11 + e * (2.0 * p01 + e * p00))
    g02 = total(mixed)
    g12 = total(p12 + e * p11 + f * p01 + e * mixed)
    g22 = total(p22 + 2.0 * (e * p12 + f * p02 + e * f * p01) + e * e * p11 + f * f * p00)
    grown = 1.0 + shift
    beta2 = g00 + EPSILON
    beta = jnp.sqrt(beta2)
    less = (grown * EPSILON - g01) / beta2
    h11 = (grown * g00 + g01) / beta2
    square = (less * less * g00 + 2.0 * less * g01 + g11) / beta2
    square = jnp.maximum(square, 0.0)
    h21 = jnp.sqrt(square + EPSILON)
    b = 1.0 / (beta * h21)
    a = less * b
    c = a - shift * b
    along_r, along_p = c * g01 + b * g02, c * g11 + b * g12
    h12 = grown * EPSILON * h11 * b / beta + along_r / beta
    d2 = a * along_r + b * along_p
    unit = 1.0 / (square + EPSILON)
    short = grown * EPSILON * unit - d2
    h22 = grown * square * unit + d2
    c0 = a * short - h12 / beta
    c1 = b * short + c
    c2 = b
    square = c0 * (c0 * g00 + 2.0 * (c1 * g01 + c2 * g02)) + c1 * (c1 * g11 + 2.0 * c2 * g12) + c2 * c2 * g22
    h32 = jnp.sqrt(jnp.maximum(square, 0.0) + EPSILON)
    a = c
    c0, c1 = c0 - shift * c1, c1 - shift * c2
    n0, n1, n2 = h21 * h32, -h11 * h32, h11 * h22 - h12 * h21
    factor = beta * n0 / (n0 * n0 + n1 * n1 + n2 * n2)
    f0, f1, f2 = factor * n0, factor * n1, factor * n2
    y2 = -f2 / h32
    y1 = (h11 * (beta - f0 - h12 * y2) - h21 * (f1 + h22 * y2)) / (h11 * h11 + h21 * h21)
    over = 1.0 / h32
    v0, v1, v2 = c0 * over, c1 * over, c2 * over
    wide = lambda value: jnp.broadcast_to(value, TILE)
    z_one, z_two = wide(y1 / beta + y2 * a), wide(y2 * b)
    r0, r1, r2 = wide(f0 / beta + f1 * a + f2 * v0), wide(f1 * b + f2 * v1), wide(f2 * v2)
    s0, s1, s2 = wide(scale * v0), wide(scale * v1), wide(scale * v2)
    copies = []
    for k in range(2):
        for x in range(source_ref.shape[1]):
            source, power, second = source_ref[k, x], power_ref[k, x], second_ref[k, x]
            adjoint_ref[k, x] = z_one * one_ref[k, x] + z_two * two_ref[k, x]
            residual_ref[k, x] = r0 * source + r1 * power + r2 * second
            basis_ref[k, x] = s0 * source + s1 * power + s2 * second
        pairs = ((adjoint_ref, adjoint_hbm), (residual_ref, residual_hbm), (basis_ref, basis_hbm))
        for index, (src, dst) in enumerate(pairs):
            copy = pltpu.make_async_copy(src.at[k], dst.at[k], sems.at[k, index])
            copy.start()
            copies.append(copy)
    for copy in copies:
        copy.wait()


def call(kernel, outs, scratch=(), name=None, inside=pltpu.VMEM, outside=pltpu.VMEM, cost=None):
    def run(*args):
        return pl.pallas_call(
            kernel,
            out_shape=[jax.ShapeDtypeStruct(shape, F32) for shape in outs],
            in_specs=[pl.BlockSpec(memory_space=inside)] * len(args),
            out_specs=[pl.BlockSpec(memory_space=outside)] * len(outs),
            scratch_shapes=[pltpu.VMEM(spec, F32) if isinstance(spec, tuple) else spec for spec in scratch],
            compiler_params=pltpu.CompilerParams(vmem_limit_bytes=32 * 1024 * 1024),
            name=name,
            cost_estimate=cost,
        )(*args)

    return run


def exchange(axis, even, odd):
    n_x, n_y = lax.axis_size("gx"), lax.axis_size("gy")
    count = lax.axis_size(axis)
    pairs = [(i, i ^ 1) for i in range(count)]
    others = []
    for x in range(n_x):
        for y in range(n_y):
            place = x if axis == "gx" else y
            if 0 < place < count - 1:
                partner = ((place - 1) ^ 1) + 1
                target = (partner, y) if axis == "gx" else (x, partner)
            else:
                target = (x, y ^ 1) if axis == "gx" else (x ^ (n_x // 2), y)
            others.append((x * n_y + y, target[0] * n_y + target[1]))
    return lax.ppermute(even, axis, pairs), lax.ppermute(odd, ("gx", "gy"), others)


def shards(adjoint_source, storage, soil_ids, bc_mask, soil_props):
    rows, _, depth = soil_ids.shape
    wide = rows + 2 * MARGIN
    devices = lax.axis_size("gx") * lax.axis_size("gy")
    cells = 2.0 * rows * soil_ids.shape[1] * depth * devices
    own = (rows, *TILE)
    x_slab = (4 * MARGIN + RIM, *TILE)
    slab = y_slab(rows, rows, rows)
    fields, wire, x_even, x_odd, y_even, y_odd = call(
        first_pack_kernel,
        [(4, *own), own, x_slab, x_slab, slab, slab],
        [soil_props.shape, (4, *own), pltpu.VMEM(own, jnp.int32), pltpu.VMEM((SUB, rows), jnp.int32)]
        + [pltpu.SemaphoreType.DMA((7,))],
        name="first_pack",
        inside=pltpu.HBM,
    )(*(pltpu.with_memory_space_constraint(x, pltpu.HBM) for x in (soil_props, storage, soil_ids, bc_mask.T)))
    xe, xo = exchange("gx", x_even, x_odd)
    ye, yo = exchange("gy", y_even, y_odd)
    slab = y_slab(5, 8, 2)
    weight = pl.CostEstimate(flops=10**11, bytes_accessed=10**9, transcendentals=0)
    even, odd = call(corner_pack_kernel, [slab, slab], [(2, *TILE)], name="corner_pack", cost=weight)(xe, xo)
    ce, co = exchange("gy", even, odd)
    count = wide // SUB
    own_coeff, own_side, image, scales, rhs, roots, roots_side, beyond = call(
        own_coefficients_kernel,
        [(4, *own), (4, rows - 2, *TILE), (4, *own), (5, *own), (2, *own)]
        + [(2, rows + 2 * RIM, *TILE), (2, *own), (2, 2, -(-rows // SUB), *TILE)],
        name="own_coefficients",
    )(soil_props, fields, wire, xe, xo, ye, yo, adjoint_source)
    buffers = [(wide + 2, 2, *TILE)] * 4
    slab = (rows + 5 + 2 * count, *TILE)
    solved_shapes = [(2, wide, *TILE), (4, count, *TILE), slab, slab]
    rest, rest_side, solved, edges, even, odd = call(
        first_solve_kernel,
        [(4, 2 * MARGIN, *TILE), (4, 2 * RIM, *TILE)] + solved_shapes,
        [(2, 2 * RIM, *TILE), (2, 2, 1, *TILE)] + buffers,
        name="first_solve",
    )(soil_props, xe, xo, ye, yo, ce, co, own_coeff, own_side, rhs, roots, roots_side, beyond)
    coeffs = (own_coeff, own_side, rest, rest_side)

    slab = (2 * (MARGIN + 2), *TILE)
    fold_shapes = [(2, wide, *TILE), (4, count, *TILE), slab, slab]
    ye, yo = exchange("gy", even, odd)
    summed, edges, even, odd = call(fold_y_kernel, fold_shapes, name="fold_y")(solved, edges, ye, yo)
    xe, xo = exchange("gx", even, odd)
    halo = [(rows + 2, *TILE)] * 2 + [(4, count, *TILE)]
    rhs, q, t, solved, edges, even, odd = call(
        step_kernel,
        [(2, *own), halo[0], halo[0]] + solved_shapes,
        halo[2:] + buffers,
        name="second_solve",
    )(summed, edges, xe, xo, *coeffs, image, scales, adjoint_source)
    one, power, shifted, shift, gram = call(power_kernel, [(2, *own)] * 3 + [TILE, TILE], name="first_power")(
        rhs, q, t, scales, adjoint_source
    )

    ye, yo = exchange("gy", even, odd)
    summed, edges, even, odd = call(fold_y_kernel, fold_shapes, name="fold_y")(solved, edges, ye, yo)
    xe, xo = exchange("gx", even, odd)
    two, second, gram = call(
        last_kernel, [(2, *own), (2, *own), (devices, LANE)], halo, name="last_image"
    )(summed, edges, xe, xo, image, scales, adjoint_source, power, shifted, shift, gram)
    gram = lax.all_to_all(gram, ("gx", "gy"), 0, 0, tiled=True)
    return tuple(
        call(
            functools.partial(combine_kernel, scale=math.sqrt(cells)),
            [(2, *own)] * 3,
            [(2, *own)] * 3 + [pltpu.SemaphoreType.DMA((2, 3))],
            name="combine",
            outside=pltpu.HBM,
        )(gram, adjoint_source, power, second, one, two)
    )


def solution(mesh):
    in_specs = (
        P(None, "gx", "gy", None),
        P(None, "gx", "gy", None),
        P("gx", "gy", None),
        P("gx", "gy"),
        P(),
    )
    out_specs = (P(None, "gx", "gy", None), P(None, "gx", "gy", None), P(None, "gx", "gy", None))
    return jax.shard_map(shards, mesh=mesh, in_specs=in_specs, out_specs=out_specs, check_vma=False)
```

```python
import functools
import math

import jax
import jax.numpy as jnp
from jax import lax
from jax.experimental import pallas as pl
from jax.experimental.pallas import tpu as pltpu
from jax.sharding import PartitionSpec as P

MARGIN = 4
SWEEPS = 6
SUB = 8
LANE = 128
TILE = (SUB, LANE)
RIM = MARGIN + 1
EPSILON = 1e-06
F32 = jnp.float32


def sublane():
    return lax.broadcasted_iota(jnp.int32, TILE, 0)


def lane():
    return lax.broadcasted_iota(jnp.int32, TILE, 1)


def up_y(tile):
    return pltpu.roll(tile, SUB - 1, 0)


def down_y(tile):
    return pltpu.roll(tile, 1, 0)


def half_turn(tile):
    return pltpu.roll(tile, SUB // 2, 0)


def along_z(tile, spot):
    above = jnp.where(spot == LANE - 1, 0.0, pltpu.roll(tile, LANE - 1, 1))
    below = jnp.where(spot == 0, 0.0, pltpu.roll(tile, 1, 1))
    return above + below


def along_y(own, side, row, last_up, last_down):
    own_up, own_down = up_y(own), down_y(own)
    side_up, side_down = up_y(side), down_y(side)
    own_sum = jnp.where(row == 7, side_up, own_up) + jnp.where(row == 0, side_down, own_down)
    if last_up is None:
        return own_sum, None
    side_sum = jnp.where(row == 7, own_up, jnp.where(row == 3, last_up, side_up))
    side_sum = side_sum + jnp.where(row == 0, own_down, jnp.where(row == 4, last_down, side_down))
    return own_sum, side_sum


def position(axis):
    place = lax.axis_index(axis)
    first = lax.rem(place, 2) == 0
    return first, place > 0, place < lax.axis_size(axis) - 1


def from_sides(first, even, odd):
    return jnp.where(first, odd, even), jnp.where(first, even, odd)


def lookup(table, wire):
    index = jnp.maximum(wire.astype(jnp.int32) - 1, 0)
    return jnp.where(wire > 0.0, jnp.take_along_axis(table, index, axis=1), 0.0)


def wide_tables(props_ref):
    pad = jnp.zeros((props_ref.shape[0], LANE - props_ref.shape[1]), F32)
    wide = jnp.concatenate([props_ref[...], pad], axis=1)
    return [jnp.broadcast_to(wide[k : k + 1], TILE) for k in range(3)]


def rim_rows(even_ref, odd_ref, base, tiles, rows_even, rows_odd):
    for j, (tile_ref, index) in enumerate(tiles):
        line = (base + j // SUB, pl.ds(j % SUB, 1))
        even_ref[line] = tile_ref[(*index, pl.ds(rows_even, 1))]
        odd_ref[line] = tile_ref[(*index, pl.ds(rows_odd, 1))]


def merge_far(near, far, row):
    far = jnp.where(row == 3, pltpu.roll(far, 3, 0), pltpu.roll(far, 5, 0))
    return jnp.where((row == 3) | (row == 4), far, near)


def split_far(tile, row):
    return jnp.where(row < 4, pltpu.roll(tile, 5, 0), pltpu.roll(tile, 3, 0))


def merge_halves(one, other, row):
    other = jnp.where(row < 4, pltpu.roll(other, 2, 0), pltpu.roll(other, 6, 0))
    return jnp.where((row >= 2) & (row < 6), other, one)


def split_halves(tile, row):
    return jnp.where(row < 4, pltpu.roll(tile, 6, 0), pltpu.roll(tile, 2, 0))


def condense(tiles, row):
    return [
        tiles[3],
        merge_far(tiles[2], tiles[0], row),
        tiles[4],
        merge_far(tiles[5], tiles[7], row),
        merge_halves(tiles[1], tiles[6], row),
    ]


def expand(tiles, row):
    low, low_two, high, high_two, three = tiles
    return [
        split_far(low_two, row), three, low_two, low, high, high_two, split_halves(three, row), split_far(high_two, row),
    ]


def condense_wire(tiles, row):
    four = merge_halves(tiles[1], tiles[8], row)
    low, high = merge_far(tiles[2], tiles[0], row), merge_far(tiles[7], tiles[9], row)
    return [tiles[4], tiles[3], low, four, tiles[5], tiles[6], high, four]


def expand_wire(tiles, row):
    low, low_two, low_three, four, high, high_two, high_three, _ = tiles
    return [
        split_far(low_three, row), four, low_three, low_two, low,
        high, high_two, high_three, split_halves(four, row), split_far(high_three, row),
    ]


def pack_y(fields, wire, edges, even_ref, odd_ref):
    first, _, _ = position("gy")
    even_low = (sublane() < 4) != first
    count, half = len(fields[0]), len(wire) // 2

    def put(spot, one, other):
        other = half_turn(other)
        even_ref[spot] = jnp.where(even_low, one, other)
        odd_ref[spot] = jnp.where(even_low, other, one)

    for pair in range(2):
        for i in range(count):
            put(pair * count + i, fields[2 * pair][i], fields[2 * pair + 1][i])
    for j in range(half):
        put(2 * count + j, wire[j], wire[j + half])
    rows_even, rows_odd = jnp.where(first, 3, 4), jnp.where(first, 4, 3)
    if len(edges) % SUB:
        last = even_ref.shape[0] - 1
        even_ref[last] = odd_ref[last] = jnp.zeros(TILE, F32)
    rim_rows(even_ref, odd_ref, 2 * count + half, edges, rows_even, rows_odd)


def y_slab(count, ids, edges):
    return (2 * count + ids // 2 + -(-edges // SUB), *TILE)


def unpack_fields(even_ref, odd_ref, count, i):
    first, _, _ = position("gy")
    row = sublane()
    out = []
    for pair in range(2):
        low, high = from_sides(first, even_ref[pair * count + i], odd_ref[pair * count + i])
        out.append(jnp.where(row < 4, high, low))
        out.append(half_turn(jnp.where(row < 4, low, high)))
    return out


def unpack_wire(even_ref, odd_ref, count, ids):
    first, has_low, has_high = position("gy")
    row = sublane()

    def sides(spot):
        low, high = from_sides(first, even_ref[spot], odd_ref[spot])
        return jnp.where(has_low, low, 0.0), jnp.where(has_high, high, 0.0)

    one, other = [], []
    for j in range(ids // 2):
        low, high = sides(2 * count + j)
        one.append(jnp.where(row < 4, high, low))
        other.append(half_turn(jnp.where(row < 4, low, high)))
    beyond = [sides(spot) for spot in range(2 * count + ids // 2, even_ref.shape[0])]
    return one + other, beyond


def halo_x(even_ref, odd_ref):
    first, has_low, has_high = position("gx")
    groups = []
    for k in range(5):
        spots = pl.ds(k * MARGIN, MARGIN)
        low, high = from_sides(first, even_ref[spots], odd_ref[spots])
        if k == 4:
            low = jnp.where(has_low, low, 0.0)
            high = jnp.where(has_high, high, 0.0)
        groups.append([low[i] for i in range(MARGIN)] + [high[i] for i in range(MARGIN)])
    empty = jnp.zeros(TILE, F32)
    return groups[:4], [empty, *groups[4], empty]


def own_row(tables, storage_ref, ids_ref, bc_ref, x, spot):
    wire = (ids_ref[x] + 1).astype(F32)
    kp = lookup(tables[0], wire)
    carried = lookup(tables[2], wire)
    held = jnp.broadcast_to(bc_ref[:, x : x + 1].astype(F32), TILE)
    bound = jnp.where(spot == LANE - 1, 2.0 * kp * held, 0.0)
    press = storage_ref[0, x]
    lower = storage_ref[1, x]
    fields = (press + bound, carried * press - storage_ref[2, x], lower, storage_ref[3, x] - carried * lower)
    return fields, wire


def first_pack_kernel(
    props_hbm, storage_hbm, ids_hbm, bc_hbm,
    props_ref, storage_ref, ids_ref, bc_ref, even_ref, odd_ref, sems,
):
    places = ((ids_hbm, ids_ref), (storage_hbm, storage_ref), (props_hbm, props_ref), (bc_hbm, bc_ref))
    copies = [pltpu.make_async_copy(src, dst, sems.at[k]) for k, (src, dst) in enumerate(places)]
    for copy in copies:
        copy.start()
    rows = ids_ref.shape[0]
    spot = lane()
    first, _, _ = position("gx")
    for copy in copies:
        copy.wait()
    tables = wide_tables(props_ref)

    ends = []
    for start, inner, beyond in ((0, MARGIN - 1, MARGIN), (rows - MARGIN, 0, -1)):
        values, wires = zip(*(own_row(tables, storage_ref, ids_ref, bc_ref, start + i, spot) for i in range(MARGIN)))
        fields = [[value[k] for value in values] for k in range(4)]
        next_wire = (ids_ref[start + beyond] + 1).astype(F32)
        for k, table in ((0, tables[0]), (3, tables[1])):
            face = jnp.sqrt(lookup(table, wires[inner]) * lookup(table, next_wire))
            fields[k][inner] = fields[k][inner] + face
        ends.append([tile for group in (*fields, wires) for tile in group])
    for place, (low, high) in enumerate(zip(*ends)):
        even_ref[place] = jnp.where(first, high, low)
        odd_ref[place] = jnp.where(first, low, high)


def own_pack_kernel(
    props_ref, storage_ref, ids_ref, bc_ref, fields_ref, wire_ref, even_ref, odd_ref,
):
    rows = ids_ref.shape[0]
    spot = lane()
    tables = wide_tables(props_ref)
    fields = [[] for _ in range(4)]
    wires = []
    for x in range(rows):
        values, wire = own_row(tables, storage_ref, ids_ref, bc_ref, x, spot)
        wire_ref[x] = wire
        wires.append(wire)
        for k in range(4):
            fields_ref[k, x] = values[k]
            fields[k].append(values[k])
    pack_y(fields, wires, [(wire_ref, (x,)) for x in range(rows)], even_ref, odd_ref)


def corner_pack_kernel(xe_ref, xo_ref, even_ref, odd_ref, wire_ref):
    row = sublane()
    fields, wire = halo_x(xe_ref, xo_ref)
    fields = [condense(field, row) for field in fields]
    wire_ref[0], wire_ref[1] = wire[RIM - 1], wire[RIM]
    edges = [(wire_ref, (j,)) for j in range(2)]
    pack_y(fields, condense_wire(wire, row), edges, even_ref, odd_ref)


def sweep_row(load, coeff, j, row, spot, rhs, count):
    sums = []
    for k in range(2):
        own, side = load(k, j, 0), load(k, j, 1)
        own_sum, side_sum = along_y(own, side, row, *((0.0, 0.0) if count == 2 else (None, None)))
        own_sum = own_sum + (along_z(own, spot) + (load(k, j - 1, 0) + load(k, j + 1, 0)))
        if count == 2:
            side_sum = side_sum + (along_z(side, spot) + (load(k, j - 1, 1) + load(k, j + 1, 1)))
        sums.append([own_sum, side_sum])
    if rhs is not None:
        sums[0][0] = sums[0][0] + rhs[0]
        sums[1][0] = sums[1][0] + rhs[1]
    out = []
    for tile in range(count):
        flow, heat = sums[0][tile], sums[1][tile]
        out.append(
            (
                coeff(0, j - 1, tile) * flow + coeff(1, j - 1, tile) * heat,
                coeff(2, j - 1, tile) * flow + coeff(3, j - 1, tile) * heat,
            )
        )
    return out


def reach_of(sweep, rows):
    reach = min(sweep, MARGIN)
    return [(x, 2 if max(-x, x - rows + 1) < sweep else 1) for x in range(-reach, rows + reach)]


def read_first(rows):
    written = [{(x + RIM, 0) for x in range(rows)}, set()]
    missing = []
    for sweep in range(1, SWEEPS):
        half = (sweep - 1) % 2
        reads = set()
        for x, count in reach_of(sweep, rows):
            j = x + RIM
            reads |= {(j, 0), (j, 1), (j - 1, 0), (j + 1, 0)}
            if count == 2:
                reads |= {(j - 1, 1), (j + 1, 1)}
        missing += [(half, *spot) for spot in sorted(reads - written[half])]
        written[half] |= reads
        written[1 - half] |= {(x + RIM, tile) for x, count in reach_of(sweep, rows) for tile in range(count)}
    return missing


def subdomain_sweeps(rhs_ref, coeff, solved_ref, rims_ref, even_ref, odd_ref, buffers, rows):
    row, spot = sublane(), lane()
    wide = rows + 2 * MARGIN
    zero = jnp.zeros(TILE, F32)
    for half, j, tile in read_first(rows):
        for k in range(2):
            buffers[2 * half + k][j, tile] = zero
    current, following = buffers[:2], buffers[2:]
    for x in range(rows):
        j = x + RIM
        flow, heat = rhs_ref[0, x], rhs_ref[1, x]
        current[0][j, 0] = coeff(0, j - 1, 0) * flow + coeff(1, j - 1, 0) * heat
        current[1][j, 0] = coeff(2, j - 1, 0) * flow + coeff(3, j - 1, 0) * heat
    first, _, _ = position("gy")
    even_low = (row < 4) != first
    last = []
    for sweep in range(1, SWEEPS):
        load = functools.cache(functools.partial(lambda pair, k, j, tile: pair[k][j, tile], current))
        for x, count in reach_of(sweep, rows):
            j = x + RIM
            rhs = (rhs_ref[0, x], rhs_ref[1, x]) if 0 <= x < rows else None
            out = sweep_row(load, coeff, j, row, spot, rhs, count)
            if sweep < SWEEPS - 1:
                for tile in range(count):
                    following[0][j, tile] = out[tile][0]
                    following[1][j, tile] = out[tile][1]
            else:
                i = j - 1
                (own_q, own_t), (side_q, side_t) = out
                solved_ref[0, i], solved_ref[1, i] = own_q, own_t
                last.append((side_q, side_t))
                for k, side in enumerate((side_q, side_t)):
                    line = (i // SUB, pl.ds(i % SUB, 1))
                    rims_ref[(2 * k, *line)] = side[7:8]
                    rims_ref[(2 * k + 1, *line)] = side[0:1]
        current, following = following, current
    corners = [condense([last[i][k] for i in [*range(MARGIN), *range(rows + MARGIN, wide)]], row) for k in range(2)]
    for i, (flow, heat) in enumerate(last[MARGIN : rows + MARGIN] + list(zip(*corners))):
        heat = half_turn(heat)
        even_ref[i] = jnp.where(even_low, heat, flow)
        odd_ref[i] = jnp.where(even_low, flow, heat)
    rows_even, rows_odd = jnp.where(first, 7, 0), jnp.where(first, 0, 7)
    for k in range(2):
        spots = [(solved_ref, (k, i)) for i in range(wide)]
        rim_rows(even_ref, odd_ref, rows + 5 + k * (wide // SUB), spots, rows_even, rows_odd)


def getter(own_ref, own_side_ref, rest_ref, rest_side_ref):
    rows = own_ref.shape[1]

    def coeff(k, i, tile):
        ref, rest, start, count = (own_ref, rest_ref, MARGIN, rows)
        if tile:
            ref, rest, start, count = (own_side_ref, rest_side_ref, MARGIN + 1, rows - 2)
        if start <= i < start + count:
            return ref[k, i - start]
        return rest[k, i if i < start else i - count]

    return coeff


def diagonal(tiles, index, spot):
    j, last_up, last_down = index
    own_sum, side_sum = along_y(tiles(j, 0), tiles(j, 1), sublane(), last_up, last_down)
    out = []
    for tile, total in ((0, own_sum), (1, side_sum)):
        if tile == 1 and last_up is None:
            break
        centre = tiles(j, tile)
        total = total + along_z(centre, spot) + (tiles(j - 1, tile) + tiles(j + 1, tile))
        out.append(centre * total)
    return out


def block_tiles(stores, sums, scales, wire):
    press, cross, lower, heat = stores
    gp, gt = scales
    outside = jnp.where(wire > 0.0, 0.0, 1.0)
    a = press + sums[0] + outside
    d = heat + sums[1] + outside
    inverse = 1.0 / (a * d + cross * lower)
    pp, pt, tt = gp * gp * inverse, gp * gt * inverse, gt * gt * inverse
    return a, d, (pp * d, pt * cross, -(pt * lower), tt * a)


def root_tables(props_ref):
    tables = wide_tables(props_ref)
    return [jnp.sqrt(jnp.maximum(table, 0.0)) for table in tables[:2]], tables[2]


def beyond_lines(beyond_ref, g, j):
    return tuple(
        jnp.broadcast_to(beyond_ref[g, end, j // SUB, pl.ds(j % SUB, 1)], TILE) for end in (1, 0)
    )


def own_coefficients_kernel(
    props_ref, fields_ref, wire_ref, xe_ref, xo_ref, ye_ref, yo_ref, source_ref,
    own_ref, own_side_ref, image_ref, scale_ref, rhs_ref, roots_ref, roots_side_ref, beyond_ref,
):
    rows = wire_ref.shape[0]
    spot = lane()
    roots, carried = root_tables(props_ref)
    _, x_wire = halo_x(xe_ref, xo_ref)
    sides, beyond = unpack_wire(ye_ref, yo_ref, rows, rows)
    wire = x_wire[:RIM] + [wire_ref[x] for x in range(rows)] + x_wire[RIM:]
    for g in range(2):
        for j, value in enumerate(wire):
            roots_ref[g, j] = lookup(roots[g], value)
        for x in range(rows):
            roots_side_ref[g, x] = lookup(roots[g], sides[x])
        for tile, ends in enumerate(beyond):
            for end in range(2):
                beyond_ref[g, end, tile] = lookup(roots[g], ends[end])
    for x in range(rows):
        inner = 0 < x < rows - 1
        sums = []
        for g in range(2):
            tiles = lambda j, tile: roots_side_ref[g, j - RIM] if tile else roots_ref[g, j]
            lines = beyond_lines(beyond_ref, g, x) if inner else (None, None)
            sums.append(diagonal(tiles, (x + RIM, *lines), spot))
        stores = [fields_ref[k, x] for k in range(4)]
        gp, gt = (roots_ref[g, x + RIM] for g in range(2))
        a, d, coeffs = block_tiles(stores, (sums[0][0], sums[1][0]), (gp, gt), wire_ref[x])
        for k in range(4):
            own_ref[k, x] = coeffs[k]
        over_p, over_t = 1.0 / gp, 1.0 / gt
        over = over_p * over_t
        image_ref[0, x] = a * (over_p * over_p)
        image_ref[1, x] = -(stores[1] * over)
        image_ref[2, x] = stores[2] * over
        image_ref[3, x] = d * (over_t * over_t)
        for k, value in enumerate((gp, gt, over_p, over_t, lookup(carried, wire_ref[x]))):
            scale_ref[k, x] = value
        rhs_ref[0, x] = source_ref[0, x] * over_p
        rhs_ref[1, x] = source_ref[1, x] * over_t
        if inner:
            stores = unpack_fields(ye_ref, yo_ref, rows, x)
            scales = [roots_side_ref[g, x] for g in range(2)]
            _, _, coeffs = block_tiles(stores, (sums[0][1], sums[1][1]), scales, sides[x])
            for k in range(4):
                own_side_ref[k, x - 1] = coeffs[k]


def first_solve_kernel(
    props_ref, xe_ref, xo_ref, ye_ref, yo_ref, ce_ref, co_ref,
    own_ref, own_side_ref, rhs_ref, roots_ref, roots_side_ref, beyond_ref,
    rest_ref, rest_side_ref, solved_ref, rims_ref, even_ref, odd_ref,
    corner_roots_ref, corner_beyond_ref, *buffers,
):
    rows = own_ref.shape[1]
    wide = rows + 2 * MARGIN
    spot = lane()
    roots, _ = root_tables(props_ref)
    x_fields, x_wire = halo_x(xe_ref, xo_ref)
    row = sublane()
    sides, beyond = unpack_wire(ce_ref, co_ref, 5, 8)
    sides = expand_wire(sides, row)
    corner_stores = [unpack_fields(ce_ref, co_ref, 5, i) for i in range(5)]
    corner_stores = [expand([stores[k] for stores in corner_stores], row) for k in range(4)]
    own_sides, _ = unpack_wire(ye_ref, yo_ref, rows, rows)
    for g in range(2):
        for j, value in enumerate(sides):
            corner_roots_ref[g, j] = lookup(roots[g], value)
        for tile, ends in enumerate(beyond):
            for end in range(2):
                corner_beyond_ref[g, end, tile] = lookup(roots[g], ends[end])
    for i in list(range(RIM)) + list(range(wide - RIM, wide)):
        j, x = i + 1, i - MARGIN
        own_row = 0 <= x < rows
        sums = []
        for g in range(2):

            def tiles(j, tile):
                if not tile:
                    return roots_ref[g, j]
                if RIM <= j < RIM + rows:
                    return roots_side_ref[g, j - RIM]
                return corner_roots_ref[g, j if j < RIM else j - rows]

            if own_row:
                lines = beyond_lines(beyond_ref, g, x)
            else:
                lines = beyond_lines(corner_beyond_ref, g, 0 if j < RIM else 1)
            sums.append((diagonal(tiles, (j, *lines), spot), tiles(j, 0), tiles(j, 1)))
        corner = i if i < MARGIN else i - rows
        if not own_row:
            stores = [x_fields[k][corner] for k in range(4)]
            scales = (sums[0][1], sums[1][1])
            spare = x_wire[j if j < RIM else j - rows]
            _, _, coeffs = block_tiles(stores, (sums[0][0][0], sums[1][0][0]), scales, spare)
            for k in range(4):
                rest_ref[k, corner] = coeffs[k]
            stores = [corner_stores[k][corner] for k in range(4)]
            spare = sides[j if j < RIM else j - rows]
        else:
            stores = unpack_fields(ye_ref, yo_ref, rows, x)
            spare = own_sides[x]
        scales = (sums[0][2], sums[1][2])
        _, _, coeffs = block_tiles(stores, (sums[0][0][1], sums[1][0][1]), scales, spare)
        for k in range(4):
            rest_side_ref[k, i if i < RIM else i - (rows - 2)] = coeffs[k]
    coeff = getter(own_ref, own_side_ref, rest_ref, rest_side_ref)
    subdomain_sweeps(rhs_ref, coeff, solved_ref, rims_ref, even_ref, odd_ref, buffers, rows)


def fold_y_kernel(solved_ref, rims_ref, ye_ref, yo_ref, summed_ref, edges_ref, even_ref, odd_ref):
    wide = solved_ref.shape[1]
    row = sublane()
    first, has_low, has_high = position("gy")
    rows = wide - 2 * MARGIN
    tiles = [[], []]
    for i in range(rows + 5):
        low, high = from_sides(first, ye_ref[i], yo_ref[i])
        low = jnp.where(has_low, low, 0.0)
        high = jnp.where(has_high, high, 0.0)
        tiles[0].append(jnp.where(row < 4, low, high))
        tiles[1].append(half_turn(jnp.where(row < 4, high, low)))
    for k in range(2):
        corners = expand(tiles[k][rows:], row)
        for spot, reach in enumerate((1, 2, 3, 4, 4, 3, 2, 1)):
            if reach < 4:
                corners[spot] = jnp.where((row < reach) | (row >= SUB - reach), corners[spot], 0.0)
        for i, value in enumerate(corners[:MARGIN] + tiles[k][:rows] + corners[MARGIN:]):
            summed_ref[k, i] = solved_ref[k, i] + value
    count = wide // SUB
    for k in range(2):
        for tile in range(count):
            spot = rows + 5 + k * count + tile
            low, high = from_sides(first, ye_ref[spot], yo_ref[spot])
            edges_ref[2 * k, tile] = rims_ref[2 * k, tile] + jnp.where(has_low, low, 0.0)
            edges_ref[2 * k + 1, tile] = rims_ref[2 * k + 1, tile] + jnp.where(has_high, high, 0.0)
    first, _, _ = position("gx")
    margin_even = jnp.where(first, wide - MARGIN, 0)
    margin_odd = jnp.where(first, 0, wide - MARGIN)
    rim_even = jnp.where(first, wide - MARGIN - 1, MARGIN)
    rim_odd = jnp.where(first, MARGIN, wide - MARGIN - 1)
    for k in range(2):
        base = k * (MARGIN + 2)
        for ref, margin, rim in ((even_ref, margin_even, rim_even), (odd_ref, margin_odd, rim_odd)):
            ref[pl.ds(base, MARGIN)] = summed_ref[k, pl.ds(margin, MARGIN)]
            ref[base + MARGIN] = summed_ref[k, rim]
        to_low = jnp.where(row < 4, edges_ref[2 * k, 0], half_turn(edges_ref[2 * k + 1, 0]))
        last = count - 1
        to_high = jnp.where(row < 4, half_turn(edges_ref[2 * k + 1, last]), edges_ref[2 * k, last])
        even_ref[base + MARGIN + 1] = jnp.where(first, to_high, to_low)
        odd_ref[base + MARGIN + 1] = jnp.where(first, to_low, to_high)


def fold_x(summed_ref, edges_ref, xe_ref, xo_ref, field_refs, edge_ref):
    wide = summed_ref.shape[1]
    rows = wide - 2 * MARGIN
    row = sublane()
    first, has_low, has_high = position("gx")
    for k in range(2):
        base = k * (MARGIN + 2)
        low, high = from_sides(first, xe_ref[pl.ds(base, MARGIN + 2)], xo_ref[pl.ds(base, MARGIN + 2)])
        low = jnp.where(has_low, low, 0.0)
        high = jnp.where(has_high, high, 0.0)
        for x in range(-1, rows + 1):
            value = summed_ref[k, x + MARGIN]
            if 0 <= x < MARGIN:
                value = value + low[x]
            if rows - MARGIN <= x < rows:
                value = value + high[x - (rows - MARGIN)]
            if x == -1:
                value = value + low[MARGIN]
            if x == rows:
                value = value + high[MARGIN]
            field_refs[k][x + 1] = value
        from_low, from_high = low[MARGIN + 1], high[MARGIN + 1]
        last = edge_ref.shape[1] - 1
        for end in range(2):
            for tile in range(last + 1):
                value = edges_ref[2 * k + end, tile]
                if tile == 0:
                    part = half_turn(from_low) if end == 1 else from_low
                    value = value + jnp.where(row < 4, 0.0, part)
                if tile == last:
                    part = half_turn(from_high) if end == 1 else from_high
                    value = value + jnp.where(row < 4, part, 0.0)
                edge_ref[2 * k + end, tile] = value


def image_row(field_refs, edge_ref, image_ref, x, row, spot):
    sums = []
    i = x + MARGIN
    for k, ref in enumerate(field_refs):
        own = ref[x + 1]
        down, up = (
            jnp.broadcast_to(edge_ref[2 * k + end, i // SUB, pl.ds(i % SUB, 1)], TILE) for end in range(2)
        )
        total = jnp.where(row == 7, up, up_y(own)) + jnp.where(row == 0, down, down_y(own))
        sums.append(total + along_z(own, spot) + (ref[x] + ref[x + 2]))
    flow, heat = field_refs[0][x + 1], field_refs[1][x + 1]
    return (
        image_ref[0, x] * flow + image_ref[1, x] * heat - sums[0],
        image_ref[2, x] * flow + image_ref[3, x] * heat - sums[1],
    )


def keep_direction(direction_ref, scale_ref, field_refs, x):
    heat = field_refs[1][x + 1] * scale_ref[3, x]
    direction_ref[1, x] = heat
    direction_ref[0, x] = field_refs[0][x + 1] * scale_ref[2, x] - scale_ref[4, x] * heat


def gram_rows(pairs, row, offset):
    total = jnp.zeros(TILE, F32)
    for index, value in enumerate(pairs):
        line = jnp.broadcast_to(jnp.sum(value, axis=0, keepdims=True), TILE)
        total = total + jnp.where(row == index + offset, line, 0.0)
    return total


def step_kernel(
    summed_ref, edges_ref, xe_ref, xo_ref, own_ref, own_side_ref, rest_ref, rest_side_ref, image_ref, scale_ref, source_ref,
    rhs_ref, q_ref, t_ref, solved_ref, rims_ref, even_ref, odd_ref, edge_ref, *buffers,
):
    rows = source_ref.shape[1]
    row, spot = sublane(), lane()
    fields = (q_ref, t_ref)
    fold_x(summed_ref, edges_ref, xe_ref, xo_ref, fields, edge_ref)
    for x in range(rows):
        for k, part in enumerate(image_row(fields, edge_ref, image_ref, x, row, spot)):
            rhs_ref[k, x] = part - source_ref[k, x] * scale_ref[2 + k, x]
    coeff = getter(own_ref, own_side_ref, rest_ref, rest_side_ref)
    subdomain_sweeps(rhs_ref, coeff, solved_ref, rims_ref, even_ref, odd_ref, buffers, rows)


def power_kernel(
    rhs_ref, q_ref, t_ref, scale_ref, source_ref, direction_ref, power_ref, shifted_ref, shift_ref, gram_ref
):
    rows = source_ref.shape[1]
    row, spot = sublane(), lane()
    square = along = jnp.zeros(TILE, F32)
    for x in range(rows):
        keep_direction(direction_ref, scale_ref, (q_ref, t_ref), x)
        for k in range(2):
            source = source_ref[k, x]
            power = rhs_ref[k, x] * scale_ref[k, x]
            power_ref[k, x] = power
            square = square + source * source
            along = along + source * power
    square_sum, along_sum = (
        jnp.sum(jnp.sum(value, axis=0, keepdims=True), axis=1, keepdims=True) for value in (square, along)
    )
    shift = jnp.broadcast_to(along_sum / jnp.maximum(square_sum, 1e-30), TILE)
    shift_ref[...] = shift
    products = [square, jnp.zeros(TILE, F32), jnp.zeros(TILE, F32)]
    for x in range(rows):
        for k in range(2):
            source = source_ref[k, x]
            shifted = power_ref[k, x] - shift * source
            shifted_ref[k, x] = shifted
            products[1] = products[1] + source * shifted
            products[2] = products[2] + shifted * shifted
    gram_ref[...] = gram_rows(products, row, 0) + jnp.where((row == 6) & (spot == 0), shift, 0.0)


def last_kernel(
    summed_ref, edges_ref, xe_ref, xo_ref, image_ref, scale_ref,
    source_ref, power_ref, shifted_in_ref, shift_ref, gram_in_ref,
    direction_ref, second_ref, gram_ref, q_ref, t_ref, edge_ref,
):
    rows = source_ref.shape[1]
    row, spot = sublane(), lane()
    fields = (q_ref, t_ref)
    fold_x(summed_ref, edges_ref, xe_ref, xo_ref, fields, edge_ref)
    products = [jnp.zeros(TILE, F32) for _ in range(3)]
    for x in range(rows):
        keep_direction(direction_ref, scale_ref, fields, x)
        for k, part in enumerate(image_row(fields, edge_ref, image_ref, x, row, spot)):
            power = power_ref[k, x]
            second = part * scale_ref[k, x] - power
            second_ref[k, x] = second
            shifted = second - shift_ref[...] * power
            products[0] = products[0] + source_ref[k, x] * shifted
            products[1] = products[1] + shifted_in_ref[k, x] * shifted
            products[2] = products[2] + shifted * shifted
    total = jnp.sum(gram_in_ref[...] + gram_rows(products, row, 3), axis=1, keepdims=True)
    line = jnp.sum(jnp.where(row == spot, jnp.broadcast_to(total, TILE), 0.0), axis=0, keepdims=True)
    gram_ref[...] = jnp.broadcast_to(line, gram_ref.shape)


def combine_kernel(
    gram_ref, source_ref, power_ref, second_ref, one_ref, two_ref,
    adjoint_hbm, residual_hbm, basis_hbm, adjoint_ref, residual_ref, basis_ref, sems, *, scale,
):
    parts = gram_ref[...]
    spot = lax.broadcasted_iota(jnp.int32, parts.shape, 1)
    p00, p01, p11, p02, p12, p22, shift_of = (
        jnp.sum(jnp.where(spot == k, parts, 0.0), axis=1, keepdims=True) for k in range(7)
    )
    total = lambda value: jnp.sum(value, axis=0, keepdims=True)
    g00 = total(p00)
    shift = total(shift_of * p00) / jnp.maximum(g00, 1e-30)
    e = shift_of - shift
    f = e * shift_of
    mixed = p02 + e * p01 + f * p00
    g01 = total(p01 + e * p00)
    g11 = total(p11 + e * (2.0 * p01 + e * p00))
    g02 = total(mixed)
    g12 = total(p12 + e * p11 + f * p01 + e * mixed)
    g22 = total(p22 + 2.0 * (e * p12 + f * p02 + e * f * p01) + e * e * p11 + f * f * p00)
    grown = 1.0 + shift
    beta2 = g00 + EPSILON
    beta = jnp.sqrt(beta2)
    less = (grown * EPSILON - g01) / beta2
    h11 = (grown * g00 + g01) / beta2
    square = (less * less * g00 + 2.0 * less * g01 + g11) / beta2
    square = jnp.maximum(square, 0.0)
    h21 = jnp.sqrt(square + EPSILON)
    b = 1.0 / (beta * h21)
    a = less * b
    c = a - shift * b
    along_r, along_p = c * g01 + b * g02, c * g11 + b * g12
    h12 = grown * EPSILON * h11 * b / beta + along_r / beta
    d2 = a * along_r + b * along_p
    unit = 1.0 / (square + EPSILON)
    short = grown * EPSILON * unit - d2
    h22 = grown * square * unit + d2
    c0 = a * short - h12 / beta
    c1 = b * short + c
    c2 = b
    square = c0 * (c0 * g00 + 2.0 * (c1 * g01 + c2 * g02)) + c1 * (c1 * g11 + 2.0 * c2 * g12) + c2 * c2 * g22
    h32 = jnp.sqrt(jnp.maximum(square, 0.0) + EPSILON)
    a = c
    c0, c1 = c0 - shift * c1, c1 - shift * c2
    n0, n1, n2 = h21 * h32, -h11 * h32, h11 * h22 - h12 * h21
    factor = beta * n0 / (n0 * n0 + n1 * n1 + n2 * n2)
    f0, f1, f2 = factor * n0, factor * n1, factor * n2
    y2 = -f2 / h32
    y1 = (h11 * (beta - f0 - h12 * y2) - h21 * (f1 + h22 * y2)) / (h11 * h11 + h21 * h21)
    over = 1.0 / h32
    v0, v1, v2 = c0 * over, c1 * over, c2 * over
    wide = lambda value: jnp.broadcast_to(value, TILE)
    z_one, z_two = wide(y1 / beta + y2 * a), wide(y2 * b)
    r0, r1, r2 = wide(f0 / beta + f1 * a + f2 * v0), wide(f1 * b + f2 * v1), wide(f2 * v2)
    s0, s1, s2 = wide(scale * v0), wide(scale * v1), wide(scale * v2)
    copies = []
    for k in range(2):
        for x in range(source_ref.shape[1]):
            source, power, second = source_ref[k, x], power_ref[k, x], second_ref[k, x]
            adjoint_ref[k, x] = z_one * one_ref[k, x] + z_two * two_ref[k, x]
            residual_ref[k, x] = r0 * source + r1 * power + r2 * second
            basis_ref[k, x] = s0 * source + s1 * power + s2 * second
        pairs = ((adjoint_ref, adjoint_hbm), (residual_ref, residual_hbm), (basis_ref, basis_hbm))
        for index, (src, dst) in enumerate(pairs):
            copy = pltpu.make_async_copy(src.at[k], dst.at[k], sems.at[k, index])
            copy.start()
            copies.append(copy)
    for copy in copies:
        copy.wait()


def call(kernel, outs, scratch=(), name=None, inside=pltpu.VMEM, outside=pltpu.VMEM, cost=None):
    def run(*args):
        return pl.pallas_call(
            kernel,
            out_shape=[
                jax.ShapeDtypeStruct(*(spec if isinstance(spec[0], tuple) else (spec, F32))) for spec in outs
            ],
            in_specs=[pl.BlockSpec(memory_space=inside)] * len(args),
            out_specs=[pl.BlockSpec(memory_space=outside)] * len(outs),
            scratch_shapes=[pltpu.VMEM(spec, F32) if isinstance(spec, tuple) else spec for spec in scratch],
            compiler_params=pltpu.CompilerParams(vmem_limit_bytes=32 * 1024 * 1024),
            name=name,
            cost_estimate=cost,
        )(*args)

    return run


def exchange(axis, even, odd):
    n_x, n_y = lax.axis_size("gx"), lax.axis_size("gy")
    count = lax.axis_size(axis)
    pairs = [(i, i ^ 1) for i in range(count)]
    others = []
    for x in range(n_x):
        for y in range(n_y):
            place = x if axis == "gx" else y
            if 0 < place < count - 1:
                partner = ((place - 1) ^ 1) + 1
                target = (partner, y) if axis == "gx" else (x, partner)
            else:
                target = (x, y ^ 1) if axis == "gx" else (x ^ (n_x // 2), y)
            others.append((x * n_y + y, target[0] * n_y + target[1]))
    return lax.ppermute(even, axis, pairs), lax.ppermute(odd, ("gx", "gy"), others)


def shards(adjoint_source, storage, soil_ids, bc_mask, soil_props):
    rows, _, depth = soil_ids.shape
    wide = rows + 2 * MARGIN
    devices = lax.axis_size("gx") * lax.axis_size("gy")
    cells = 2.0 * rows * soil_ids.shape[1] * depth * devices
    own = (rows, *TILE)
    x_slab = (5 * MARGIN, *TILE)
    held = (SUB, rows)
    *raw, x_even, x_odd = call(
        first_pack_kernel,
        [soil_props.shape, (4, *own), (own, jnp.int32), (held, jnp.int32), x_slab, x_slab],
        [pltpu.SemaphoreType.DMA((4,))],
        name="first_pack",
        inside=pltpu.HBM,
    )(*(pltpu.with_memory_space_constraint(x, pltpu.HBM) for x in (soil_props, storage, soil_ids, bc_mask.T)))
    xe, xo = exchange("gx", x_even, x_odd)
    slab = y_slab(rows, rows, rows)
    fields, wire, y_even, y_odd = call(own_pack_kernel, [(4, *own), own, slab, slab], name="own_pack")(*raw)
    ye, yo = exchange("gy", y_even, y_odd)
    slab = y_slab(5, 8, 2)
    weight = pl.CostEstimate(flops=10**11, bytes_accessed=10**9, transcendentals=0)
    even, odd = call(corner_pack_kernel, [slab, slab], [(2, *TILE)], name="corner_pack", cost=weight)(xe, xo)
    ce, co = exchange("gy", even, odd)
    count = wide // SUB
    own_coeff, own_side, image, scales, rhs, roots, roots_side, beyond = call(
        own_coefficients_kernel,
        [(4, *own), (4, rows - 2, *TILE), (4, *own), (5, *own), (2, *own)]
        + [(2, rows + 2 * RIM, *TILE), (2, *own), (2, 2, -(-rows // SUB), *TILE)],
        name="own_coefficients",
    )(soil_props, fields, wire, xe, xo, ye, yo, adjoint_source)
    buffers = [(wide + 2, 2, *TILE)] * 4
    slab = (rows + 5 + 2 * count, *TILE)
    solved_shapes = [(2, wide, *TILE), (4, count, *TILE), slab, slab]
    rest, rest_side, solved, edges, even, odd = call(
        first_solve_kernel,
        [(4, 2 * MARGIN, *TILE), (4, 2 * RIM, *TILE)] + solved_shapes,
        [(2, 2 * RIM, *TILE), (2, 2, 1, *TILE)] + buffers,
        name="first_solve",
    )(soil_props, xe, xo, ye, yo, ce, co, own_coeff, own_side, rhs, roots, roots_side, beyond)
    coeffs = (own_coeff, own_side, rest, rest_side)

    slab = (2 * (MARGIN + 2), *TILE)
    fold_shapes = [(2, wide, *TILE), (4, count, *TILE), slab, slab]
    ye, yo = exchange("gy", even, odd)
    summed, edges, even, odd = call(fold_y_kernel, fold_shapes, name="fold_y")(solved, edges, ye, yo)
    xe, xo = exchange("gx", even, odd)
    halo = [(rows + 2, *TILE)] * 2 + [(4, count, *TILE)]
    rhs, q, t, solved, edges, even, odd = call(
        step_kernel,
        [(2, *own), halo[0], halo[0]] + solved_shapes,
        halo[2:] + buffers,
        name="second_solve",
    )(summed, edges, xe, xo, *coeffs, image, scales, adjoint_source)
    one, power, shifted, shift, gram = call(power_kernel, [(2, *own)] * 3 + [TILE, TILE], name="first_power")(
        rhs, q, t, scales, adjoint_source
    )

    ye, yo = exchange("gy", even, odd)
    summed, edges, even, odd = call(fold_y_kernel, fold_shapes, name="fold_y")(solved, edges, ye, yo)
    xe, xo = exchange("gx", even, odd)
    two, second, gram = call(
        last_kernel, [(2, *own), (2, *own), (devices, LANE)], halo, name="last_image"
    )(summed, edges, xe, xo, image, scales, adjoint_source, power, shifted, shift, gram)
    gram = lax.all_to_all(gram, ("gx", "gy"), 0, 0, tiled=True)
    return tuple(
        call(
            functools.partial(combine_kernel, scale=math.sqrt(cells)),
            [(2, *own)] * 3,
            [(2, *own)] * 3 + [pltpu.SemaphoreType.DMA((2, 3))],
            name="combine",
            outside=pltpu.HBM,
        )(gram, adjoint_source, power, second, one, two)
    )


def solution(mesh):
    in_specs = (
        P(None, "gx", "gy", None),
        P(None, "gx", "gy", None),
        P("gx", "gy", None),
        P("gx", "gy"),
        P(),
    )
    out_specs = (P(None, "gx", "gy", None), P(None, "gx", "gy", None), P(None, "gx", "gy", None))
    return jax.shard_map(shards, mesh=mesh, in_specs=in_specs, out_specs=out_specs, check_vma=False)
```

```python
import functools
import math

import jax
import jax.numpy as jnp
from jax import lax
from jax.experimental import pallas as pl
from jax.experimental.pallas import tpu as pltpu
from jax.sharding import PartitionSpec as P

MARGIN = 4
SWEEPS = 6
SUB = 8
LANE = 128
TILE = (SUB, LANE)
RIM = MARGIN + 1
EPSILON = 1e-06
F32 = jnp.float32


def sublane():
    return lax.broadcasted_iota(jnp.int32, TILE, 0)


def lane():
    return lax.broadcasted_iota(jnp.int32, TILE, 1)


def up_y(tile):
    return pltpu.roll(tile, SUB - 1, 0)


def down_y(tile):
    return pltpu.roll(tile, 1, 0)


def half_turn(tile):
    return pltpu.roll(tile, SUB // 2, 0)


def along_z(tile, spot):
    above = jnp.where(spot == LANE - 1, 0.0, pltpu.roll(tile, LANE - 1, 1))
    below = jnp.where(spot == 0, 0.0, pltpu.roll(tile, 1, 1))
    return above + below


def along_y(own, side, row, last_up, last_down):
    own_up, own_down = up_y(own), down_y(own)
    side_up, side_down = up_y(side), down_y(side)
    own_sum = jnp.where(row == 7, side_up, own_up) + jnp.where(row == 0, side_down, own_down)
    if last_up is None:
        return own_sum, None
    side_sum = jnp.where(row == 7, own_up, jnp.where(row == 3, last_up, side_up))
    side_sum = side_sum + jnp.where(row == 0, own_down, jnp.where(row == 4, last_down, side_down))
    return own_sum, side_sum


def position(axis):
    place = lax.axis_index(axis)
    first = lax.rem(place, 2) == 0
    return first, place > 0, place < lax.axis_size(axis) - 1


def from_sides(first, even, odd):
    return jnp.where(first, odd, even), jnp.where(first, even, odd)


def lookup(table, wire):
    index = jnp.maximum(wire.astype(jnp.int32) - 1, 0)
    return jnp.where(wire > 0.0, jnp.take_along_axis(table, index, axis=1), 0.0)


def wide_tables(props_ref):
    pad = jnp.zeros((props_ref.shape[0], LANE - props_ref.shape[1]), F32)
    wide = jnp.concatenate([props_ref[...], pad], axis=1)
    return [jnp.broadcast_to(wide[k : k + 1], TILE) for k in range(3)]


def rim_rows(even_ref, odd_ref, base, tiles, rows_even, rows_odd):
    for j, (tile_ref, index) in enumerate(tiles):
        line = (base + j // SUB, pl.ds(j % SUB, 1))
        even_ref[line] = tile_ref[(*index, pl.ds(rows_even, 1))]
        odd_ref[line] = tile_ref[(*index, pl.ds(rows_odd, 1))]


def merge_far(near, far, row):
    far = jnp.where(row == 3, pltpu.roll(far, 3, 0), pltpu.roll(far, 5, 0))
    return jnp.where((row == 3) | (row == 4), far, near)


def split_far(tile, row):
    return jnp.where(row < 4, pltpu.roll(tile, 5, 0), pltpu.roll(tile, 3, 0))


def merge_halves(one, other, row):
    other = jnp.where(row < 4, pltpu.roll(other, 2, 0), pltpu.roll(other, 6, 0))
    return jnp.where((row >= 2) & (row < 6), other, one)


def split_halves(tile, row):
    return jnp.where(row < 4, pltpu.roll(tile, 6, 0), pltpu.roll(tile, 2, 0))


def condense(tiles, row):
    return [
        tiles[3],
        merge_far(tiles[2], tiles[0], row),
        tiles[4],
        merge_far(tiles[5], tiles[7], row),
        merge_halves(tiles[1], tiles[6], row),
    ]


def expand(tiles, row):
    low, low_two, high, high_two, three = tiles
    return [
        split_far(low_two, row), three, low_two, low, high, high_two, split_halves(three, row), split_far(high_two, row),
    ]


def condense_wire(tiles, row):
    four = merge_halves(tiles[1], tiles[8], row)
    low, high = merge_far(tiles[2], tiles[0], row), merge_far(tiles[7], tiles[9], row)
    return [tiles[4], tiles[3], low, four, tiles[5], tiles[6], high, four]


def expand_wire(tiles, row):
    low, low_two, low_three, four, high, high_two, high_three, _ = tiles
    return [
        split_far(low_three, row), four, low_three, low_two, low,
        high, high_two, high_three, split_halves(four, row), split_far(high_three, row),
    ]


def pack_y(fields, wire, even_ref, odd_ref):
    first, _, _ = position("gy")
    even_low = (sublane() < 4) != first
    count, half = len(fields[0]), len(wire) // 2

    def put(spot, one, other):
        other = half_turn(other)
        even_ref[spot] = jnp.where(even_low, one, other)
        odd_ref[spot] = jnp.where(even_low, other, one)

    for pair in range(2):
        for i in range(count):
            put(pair * count + i, fields[2 * pair][i], fields[2 * pair + 1][i])
    for j in range(half):
        put(2 * count + j, wire[j], wire[j + half])


def fold_beyond(fields, wire, tables, row):
    out = list(fields)
    for k, table in ((0, tables[0]), (3, tables[1])):
        value = lookup(table, wire)
        face = jnp.sqrt(value * jnp.where(row == 3, up_y(value), down_y(value)))
        out[k] = out[k] + jnp.where((row == 3) | (row == 4), face, 0.0)
    return out


def y_slab(count, ids):
    return (2 * count + ids // 2, *TILE)


def unpack_fields(even_ref, odd_ref, count, i):
    first, _, _ = position("gy")
    row = sublane()
    out = []
    for pair in range(2):
        low, high = from_sides(first, even_ref[pair * count + i], odd_ref[pair * count + i])
        out.append(jnp.where(row < 4, high, low))
        out.append(half_turn(jnp.where(row < 4, low, high)))
    return out


def unpack_wire(even_ref, odd_ref, count, ids):
    first, has_low, has_high = position("gy")
    row = sublane()

    def sides(spot):
        low, high = from_sides(first, even_ref[spot], odd_ref[spot])
        return jnp.where(has_low, low, 0.0), jnp.where(has_high, high, 0.0)

    one, other = [], []
    for j in range(ids // 2):
        low, high = sides(2 * count + j)
        one.append(jnp.where(row < 4, high, low))
        other.append(half_turn(jnp.where(row < 4, low, high)))
    return one + other


def halo_x(even_ref, odd_ref):
    first, has_low, has_high = position("gx")
    groups = []
    for k in range(5):
        spots = pl.ds(k * MARGIN, MARGIN)
        low, high = from_sides(first, even_ref[spots], odd_ref[spots])
        if k == 4:
            low = jnp.where(has_low, low, 0.0)
            high = jnp.where(has_high, high, 0.0)
        groups.append([low[i] for i in range(MARGIN)] + [high[i] for i in range(MARGIN)])
    empty = jnp.zeros(TILE, F32)
    return groups[:4], [empty, *groups[4], empty]


def own_row(tables, storage_ref, ids_ref, bc_ref, x, spot):
    wire = (ids_ref[x] + 1).astype(F32)
    kp = lookup(tables[0], wire)
    carried = lookup(tables[2], wire)
    held = jnp.broadcast_to(bc_ref[:, x : x + 1].astype(F32), TILE)
    bound = jnp.where(spot == LANE - 1, 2.0 * kp * held, 0.0)
    press = storage_ref[0, x]
    lower = storage_ref[1, x]
    fields = (press + bound, carried * press - storage_ref[2, x], lower, storage_ref[3, x] - carried * lower)
    return fields, wire


def first_pack_kernel(
    props_hbm, storage_hbm, ids_hbm, bc_hbm,
    props_ref, storage_ref, ids_ref, bc_ref, even_ref, odd_ref, sems,
):
    places = ((ids_hbm, ids_ref), (storage_hbm, storage_ref), (props_hbm, props_ref), (bc_hbm, bc_ref))
    copies = [pltpu.make_async_copy(src, dst, sems.at[k]) for k, (src, dst) in enumerate(places)]
    for copy in copies:
        copy.start()
    rows = ids_ref.shape[0]
    spot = lane()
    first, _, _ = position("gx")
    for copy in copies:
        copy.wait()
    tables = wide_tables(props_ref)

    ends = []
    for start, inner, beyond in ((0, MARGIN - 1, MARGIN), (rows - MARGIN, 0, -1)):
        values, wires = zip(*(own_row(tables, storage_ref, ids_ref, bc_ref, start + i, spot) for i in range(MARGIN)))
        fields = [[value[k] for value in values] for k in range(4)]
        next_wire = (ids_ref[start + beyond] + 1).astype(F32)
        for k, table in ((0, tables[0]), (3, tables[1])):
            face = jnp.sqrt(lookup(table, wires[inner]) * lookup(table, next_wire))
            fields[k][inner] = fields[k][inner] + face
        ends.append([tile for group in (*fields, wires) for tile in group])
    for place, (low, high) in enumerate(zip(*ends)):
        even_ref[place] = jnp.where(first, high, low)
        odd_ref[place] = jnp.where(first, low, high)


def own_pack_kernel(
    props_ref, storage_ref, ids_ref, bc_ref, fields_ref, wire_ref, even_ref, odd_ref,
):
    rows = ids_ref.shape[0]
    spot = lane()
    tables = wide_tables(props_ref)
    fields = [[] for _ in range(4)]
    wires = []
    for x in range(rows):
        values, wire = own_row(tables, storage_ref, ids_ref, bc_ref, x, spot)
        wire_ref[x] = wire
        wires.append(wire)
        for k in range(4):
            fields_ref[k, x] = values[k]
        for k, value in enumerate(fold_beyond(values, wire, tables, sublane())):
            fields[k].append(value)
    pack_y(fields, wires, even_ref, odd_ref)


def corner_pack_kernel(props_ref, xe_ref, xo_ref, even_ref, odd_ref):
    row = sublane()
    tables = wide_tables(props_ref)
    fields, wire = halo_x(xe_ref, xo_ref)
    for i in (MARGIN - 1, MARGIN):
        for k, value in enumerate(fold_beyond([field[i] for field in fields], wire[i + 1], tables, row)):
            fields[k][i] = value
    fields = [condense(field, row) for field in fields]
    pack_y(fields, condense_wire(wire, row), even_ref, odd_ref)


def sweep_row(load, coeff, j, row, spot, rhs, count):
    sums = []
    for k in range(2):
        own, side = load(k, j, 0), load(k, j, 1)
        own_sum, side_sum = along_y(own, side, row, *((0.0, 0.0) if count == 2 else (None, None)))
        own_sum = own_sum + (along_z(own, spot) + (load(k, j - 1, 0) + load(k, j + 1, 0)))
        if count == 2:
            side_sum = side_sum + (along_z(side, spot) + (load(k, j - 1, 1) + load(k, j + 1, 1)))
        sums.append([own_sum, side_sum])
    if rhs is not None:
        sums[0][0] = sums[0][0] + rhs[0]
        sums[1][0] = sums[1][0] + rhs[1]
    out = []
    for tile in range(count):
        flow, heat = sums[0][tile], sums[1][tile]
        out.append(
            (
                coeff(0, j - 1, tile) * flow + coeff(1, j - 1, tile) * heat,
                coeff(2, j - 1, tile) * flow + coeff(3, j - 1, tile) * heat,
            )
        )
    return out


def reach_of(sweep, rows):
    reach = min(sweep, MARGIN)
    return [(x, 2 if max(-x, x - rows + 1) < sweep else 1) for x in range(-reach, rows + reach)]


def read_first(rows):
    written = [{(x + RIM, 0) for x in range(rows)}, set()]
    missing = []
    for sweep in range(1, SWEEPS):
        half = (sweep - 1) % 2
        reads = set()
        for x, count in reach_of(sweep, rows):
            j = x + RIM
            reads |= {(j, 0), (j, 1), (j - 1, 0), (j + 1, 0)}
            if count == 2:
                reads |= {(j - 1, 1), (j + 1, 1)}
        missing += [(half, *spot) for spot in sorted(reads - written[half])]
        written[half] |= reads
        written[1 - half] |= {(x + RIM, tile) for x, count in reach_of(sweep, rows) for tile in range(count)}
    return missing


def subdomain_sweeps(rhs_ref, coeff, solved_ref, rims_ref, even_ref, odd_ref, buffers, rows):
    row, spot = sublane(), lane()
    wide = rows + 2 * MARGIN
    zero = jnp.zeros(TILE, F32)
    for half, j, tile in read_first(rows):
        for k in range(2):
            buffers[2 * half + k][j, tile] = zero
    current, following = buffers[:2], buffers[2:]
    for x in range(rows):
        j = x + RIM
        flow, heat = rhs_ref[0, x], rhs_ref[1, x]
        current[0][j, 0] = coeff(0, j - 1, 0) * flow + coeff(1, j - 1, 0) * heat
        current[1][j, 0] = coeff(2, j - 1, 0) * flow + coeff(3, j - 1, 0) * heat
    first, _, _ = position("gy")
    even_low = (row < 4) != first
    last = []
    for sweep in range(1, SWEEPS):
        load = functools.cache(functools.partial(lambda pair, k, j, tile: pair[k][j, tile], current))
        for x, count in reach_of(sweep, rows):
            j = x + RIM
            rhs = (rhs_ref[0, x], rhs_ref[1, x]) if 0 <= x < rows else None
            out = sweep_row(load, coeff, j, row, spot, rhs, count)
            if sweep < SWEEPS - 1:
                for tile in range(count):
                    following[0][j, tile] = out[tile][0]
                    following[1][j, tile] = out[tile][1]
            else:
                i = j - 1
                (own_q, own_t), (side_q, side_t) = out
                solved_ref[0, i], solved_ref[1, i] = own_q, own_t
                last.append((side_q, side_t))
                for k, side in enumerate((side_q, side_t)):
                    line = (i // SUB, pl.ds(i % SUB, 1))
                    rims_ref[(2 * k, *line)] = side[7:8]
                    rims_ref[(2 * k + 1, *line)] = side[0:1]
        current, following = following, current
    corners = [condense([last[i][k] for i in [*range(MARGIN), *range(rows + MARGIN, wide)]], row) for k in range(2)]
    for i, (flow, heat) in enumerate(last[MARGIN : rows + MARGIN] + list(zip(*corners))):
        heat = half_turn(heat)
        even_ref[i] = jnp.where(even_low, heat, flow)
        odd_ref[i] = jnp.where(even_low, flow, heat)
    rows_even, rows_odd = jnp.where(first, 7, 0), jnp.where(first, 0, 7)
    for k in range(2):
        spots = [(solved_ref, (k, i)) for i in range(wide)]
        rim_rows(even_ref, odd_ref, rows + 5 + k * (wide // SUB), spots, rows_even, rows_odd)


def getter(own_ref, own_side_ref, rest_ref, rest_side_ref):
    rows = own_ref.shape[1]

    def coeff(k, i, tile):
        ref, rest, start, count = (own_ref, rest_ref, MARGIN, rows)
        if tile:
            ref, rest, start, count = (own_side_ref, rest_side_ref, MARGIN + 1, rows - 2)
        if start <= i < start + count:
            return ref[k, i - start]
        return rest[k, i if i < start else i - count]

    return coeff


def diagonal(tiles, index, spot):
    j, last_up, last_down = index
    own_sum, side_sum = along_y(tiles(j, 0), tiles(j, 1), sublane(), last_up, last_down)
    out = []
    for tile, total in ((0, own_sum), (1, side_sum)):
        if tile == 1 and last_up is None:
            break
        centre = tiles(j, tile)
        total = total + along_z(centre, spot) + (tiles(j - 1, tile) + tiles(j + 1, tile))
        out.append(centre * total)
    return out


def block_tiles(stores, sums, scales, wire):
    press, cross, lower, heat = stores
    gp, gt = scales
    outside = jnp.where(wire > 0.0, 0.0, 1.0)
    a = press + sums[0] + outside
    d = heat + sums[1] + outside
    inverse = 1.0 / (a * d + cross * lower)
    pp, pt, tt = gp * gp * inverse, gp * gt * inverse, gt * gt * inverse
    return a, d, (pp * d, pt * cross, -(pt * lower), tt * a)


def root_tables(props_ref):
    tables = wide_tables(props_ref)
    return [jnp.sqrt(jnp.maximum(table, 0.0)) for table in tables[:2]], tables[2]


def own_coefficients_kernel(
    props_ref, fields_ref, wire_ref, xe_ref, xo_ref, ye_ref, yo_ref, source_ref,
    own_ref, own_side_ref, image_ref, scale_ref, rhs_ref, roots_ref, roots_side_ref,
):
    rows = wire_ref.shape[0]
    spot = lane()
    roots, carried = root_tables(props_ref)
    _, x_wire = halo_x(xe_ref, xo_ref)
    sides = unpack_wire(ye_ref, yo_ref, rows, rows)
    wire = x_wire[:RIM] + [wire_ref[x] for x in range(rows)] + x_wire[RIM:]
    for g in range(2):
        for j, value in enumerate(wire):
            roots_ref[g, j] = lookup(roots[g], value)
        for x in range(rows):
            roots_side_ref[g, x] = lookup(roots[g], sides[x])
    for x in range(rows):
        inner = 0 < x < rows - 1
        sums = []
        for g in range(2):
            tiles = lambda j, tile: roots_side_ref[g, j - RIM] if tile else roots_ref[g, j]
            lines = (0.0, 0.0) if inner else (None, None)
            sums.append(diagonal(tiles, (x + RIM, *lines), spot))
        stores = [fields_ref[k, x] for k in range(4)]
        gp, gt = (roots_ref[g, x + RIM] for g in range(2))
        a, d, coeffs = block_tiles(stores, (sums[0][0], sums[1][0]), (gp, gt), wire_ref[x])
        for k in range(4):
            own_ref[k, x] = coeffs[k]
        over_p, over_t = 1.0 / gp, 1.0 / gt
        over = over_p * over_t
        image_ref[0, x] = a * (over_p * over_p)
        image_ref[1, x] = -(stores[1] * over)
        image_ref[2, x] = stores[2] * over
        image_ref[3, x] = d * (over_t * over_t)
        for k, value in enumerate((gp, gt, over_p, over_t, lookup(carried, wire_ref[x]))):
            scale_ref[k, x] = value
        rhs_ref[0, x] = source_ref[0, x] * over_p
        rhs_ref[1, x] = source_ref[1, x] * over_t
        if inner:
            stores = unpack_fields(ye_ref, yo_ref, rows, x)
            scales = [roots_side_ref[g, x] for g in range(2)]
            _, _, coeffs = block_tiles(stores, (sums[0][1], sums[1][1]), scales, sides[x])
            for k in range(4):
                own_side_ref[k, x - 1] = coeffs[k]


def first_solve_kernel(
    props_ref, xe_ref, xo_ref, ye_ref, yo_ref, ce_ref, co_ref,
    own_ref, own_side_ref, rhs_ref, roots_ref, roots_side_ref,
    rest_ref, rest_side_ref, solved_ref, rims_ref, even_ref, odd_ref,
    corner_roots_ref, *buffers,
):
    rows = own_ref.shape[1]
    wide = rows + 2 * MARGIN
    spot = lane()
    roots, _ = root_tables(props_ref)
    x_fields, x_wire = halo_x(xe_ref, xo_ref)
    row = sublane()
    sides = unpack_wire(ce_ref, co_ref, 5, 8)
    sides = expand_wire(sides, row)
    corner_stores = [unpack_fields(ce_ref, co_ref, 5, i) for i in range(5)]
    corner_stores = [expand([stores[k] for stores in corner_stores], row) for k in range(4)]
    own_sides = unpack_wire(ye_ref, yo_ref, rows, rows)
    for g in range(2):
        for j, value in enumerate(sides):
            corner_roots_ref[g, j] = lookup(roots[g], value)
    for i in list(range(RIM)) + list(range(wide - RIM, wide)):
        j, x = i + 1, i - MARGIN
        own_row = 0 <= x < rows
        sums = []
        for g in range(2):

            def tiles(j, tile):
                if not tile:
                    return roots_ref[g, j]
                if RIM <= j < RIM + rows:
                    return roots_side_ref[g, j - RIM]
                return corner_roots_ref[g, j if j < RIM else j - rows]

            sums.append((diagonal(tiles, (j, 0.0, 0.0), spot), tiles(j, 0), tiles(j, 1)))
        corner = i if i < MARGIN else i - rows
        if not own_row:
            stores = [x_fields[k][corner] for k in range(4)]
            scales = (sums[0][1], sums[1][1])
            spare = x_wire[j if j < RIM else j - rows]
            _, _, coeffs = block_tiles(stores, (sums[0][0][0], sums[1][0][0]), scales, spare)
            for k in range(4):
                rest_ref[k, corner] = coeffs[k]
            stores = [corner_stores[k][corner] for k in range(4)]
            spare = sides[j if j < RIM else j - rows]
        else:
            stores = unpack_fields(ye_ref, yo_ref, rows, x)
            spare = own_sides[x]
        scales = (sums[0][2], sums[1][2])
        _, _, coeffs = block_tiles(stores, (sums[0][0][1], sums[1][0][1]), scales, spare)
        for k in range(4):
            rest_side_ref[k, i if i < RIM else i - (rows - 2)] = coeffs[k]
    coeff = getter(own_ref, own_side_ref, rest_ref, rest_side_ref)
    subdomain_sweeps(rhs_ref, coeff, solved_ref, rims_ref, even_ref, odd_ref, buffers, rows)


def fold_y_kernel(solved_ref, rims_ref, ye_ref, yo_ref, summed_ref, edges_ref, even_ref, odd_ref):
    wide = solved_ref.shape[1]
    row = sublane()
    first, has_low, has_high = position("gy")
    rows = wide - 2 * MARGIN
    tiles = [[], []]
    for i in range(rows + 5):
        low, high = from_sides(first, ye_ref[i], yo_ref[i])
        low = jnp.where(has_low, low, 0.0)
        high = jnp.where(has_high, high, 0.0)
        tiles[0].append(jnp.where(row < 4, low, high))
        tiles[1].append(half_turn(jnp.where(row < 4, high, low)))
    for k in range(2):
        corners = expand(tiles[k][rows:], row)
        for spot, reach in enumerate((1, 2, 3, 4, 4, 3, 2, 1)):
            if reach < 4:
                corners[spot] = jnp.where((row < reach) | (row >= SUB - reach), corners[spot], 0.0)
        for i, value in enumerate(corners[:MARGIN] + tiles[k][:rows] + corners[MARGIN:]):
            summed_ref[k, i] = solved_ref[k, i] + value
    count = wide // SUB
    for k in range(2):
        for tile in range(count):
            spot = rows + 5 + k * count + tile
            low, high = from_sides(first, ye_ref[spot], yo_ref[spot])
            edges_ref[2 * k, tile] = rims_ref[2 * k, tile] + jnp.where(has_low, low, 0.0)
            edges_ref[2 * k + 1, tile] = rims_ref[2 * k + 1, tile] + jnp.where(has_high, high, 0.0)
    first, _, _ = position("gx")
    margin_even = jnp.where(first, wide - MARGIN, 0)
    margin_odd = jnp.where(first, 0, wide - MARGIN)
    rim_even = jnp.where(first, wide - MARGIN - 1, MARGIN)
    rim_odd = jnp.where(first, MARGIN, wide - MARGIN - 1)
    for k in range(2):
        base = k * (MARGIN + 2)
        for ref, margin, rim in ((even_ref, margin_even, rim_even), (odd_ref, margin_odd, rim_odd)):
            ref[pl.ds(base, MARGIN)] = summed_ref[k, pl.ds(margin, MARGIN)]
            ref[base + MARGIN] = summed_ref[k, rim]
        to_low = jnp.where(row < 4, edges_ref[2 * k, 0], half_turn(edges_ref[2 * k + 1, 0]))
        last = count - 1
        to_high = jnp.where(row < 4, half_turn(edges_ref[2 * k + 1, last]), edges_ref[2 * k, last])
        even_ref[base + MARGIN + 1] = jnp.where(first, to_high, to_low)
        odd_ref[base + MARGIN + 1] = jnp.where(first, to_low, to_high)


def fold_x(summed_ref, edges_ref, xe_ref, xo_ref, field_refs, edge_ref):
    wide = summed_ref.shape[1]
    rows = wide - 2 * MARGIN
    row = sublane()
    first, has_low, has_high = position("gx")
    for k in range(2):
        base = k * (MARGIN + 2)
        low, high = from_sides(first, xe_ref[pl.ds(base, MARGIN + 2)], xo_ref[pl.ds(base, MARGIN + 2)])
        low = jnp.where(has_low, low, 0.0)
        high = jnp.where(has_high, high, 0.0)
        for x in range(-1, rows + 1):
            value = summed_ref[k, x + MARGIN]
            if 0 <= x < MARGIN:
                value = value + low[x]
            if rows - MARGIN <= x < rows:
                value = value + high[x - (rows - MARGIN)]
            if x == -1:
                value = value + low[MARGIN]
            if x == rows:
                value = value + high[MARGIN]
            field_refs[k][x + 1] = value
        from_low, from_high = low[MARGIN + 1], high[MARGIN + 1]
        last = edge_ref.shape[1] - 1
        for end in range(2):
            for tile in range(last + 1):
                value = edges_ref[2 * k + end, tile]
                if tile == 0:
                    part = half_turn(from_low) if end == 1 else from_low
                    value = value + jnp.where(row < 4, 0.0, part)
                if tile == last:
                    part = half_turn(from_high) if end == 1 else from_high
                    value = value + jnp.where(row < 4, part, 0.0)
                edge_ref[2 * k + end, tile] = value


def image_row(field_refs, edge_ref, image_ref, x, row, spot):
    sums = []
    i = x + MARGIN
    for k, ref in enumerate(field_refs):
        own = ref[x + 1]
        down, up = (
            jnp.broadcast_to(edge_ref[2 * k + end, i // SUB, pl.ds(i % SUB, 1)], TILE) for end in range(2)
        )
        total = jnp.where(row == 7, up, up_y(own)) + jnp.where(row == 0, down, down_y(own))
        sums.append(total + along_z(own, spot) + (ref[x] + ref[x + 2]))
    flow, heat = field_refs[0][x + 1], field_refs[1][x + 1]
    return (
        image_ref[0, x] * flow + image_ref[1, x] * heat - sums[0],
        image_ref[2, x] * flow + image_ref[3, x] * heat - sums[1],
    )


def keep_direction(direction_ref, scale_ref, field_refs, x):
    heat = field_refs[1][x + 1] * scale_ref[3, x]
    direction_ref[1, x] = heat
    direction_ref[0, x] = field_refs[0][x + 1] * scale_ref[2, x] - scale_ref[4, x] * heat


def gram_rows(pairs, row, offset):
    total = jnp.zeros(TILE, F32)
    for index, value in enumerate(pairs):
        line = jnp.broadcast_to(jnp.sum(value, axis=0, keepdims=True), TILE)
        total = total + jnp.where(row == index + offset, line, 0.0)
    return total


def step_kernel(
    summed_ref, edges_ref, xe_ref, xo_ref, own_ref, own_side_ref, rest_ref, rest_side_ref, image_ref, scale_ref, source_ref,
    rhs_ref, q_ref, t_ref, solved_ref, rims_ref, even_ref, odd_ref, edge_ref, *buffers,
):
    rows = source_ref.shape[1]
    row, spot = sublane(), lane()
    fields = (q_ref, t_ref)
    fold_x(summed_ref, edges_ref, xe_ref, xo_ref, fields, edge_ref)
    for x in range(rows):
        for k, part in enumerate(image_row(fields, edge_ref, image_ref, x, row, spot)):
            rhs_ref[k, x] = part - source_ref[k, x] * scale_ref[2 + k, x]
    coeff = getter(own_ref, own_side_ref, rest_ref, rest_side_ref)
    subdomain_sweeps(rhs_ref, coeff, solved_ref, rims_ref, even_ref, odd_ref, buffers, rows)


def power_kernel(
    rhs_ref, q_ref, t_ref, scale_ref, source_ref, direction_ref, power_ref, shifted_ref, shift_ref, gram_ref
):
    rows = source_ref.shape[1]
    row, spot = sublane(), lane()
    square = along = jnp.zeros(TILE, F32)
    for x in range(rows):
        keep_direction(direction_ref, scale_ref, (q_ref, t_ref), x)
        for k in range(2):
            source = source_ref[k, x]
            power = rhs_ref[k, x] * scale_ref[k, x]
            power_ref[k, x] = power
            square = square + source * source
            along = along + source * power
    square_sum, along_sum = (
        jnp.sum(jnp.sum(value, axis=0, keepdims=True), axis=1, keepdims=True) for value in (square, along)
    )
    shift = jnp.broadcast_to(along_sum / jnp.maximum(square_sum, 1e-30), TILE)
    shift_ref[...] = shift
    products = [square, jnp.zeros(TILE, F32), jnp.zeros(TILE, F32)]
    for x in range(rows):
        for k in range(2):
            source = source_ref[k, x]
            shifted = power_ref[k, x] - shift * source
            shifted_ref[k, x] = shifted
            products[1] = products[1] + source * shifted
            products[2] = products[2] + shifted * shifted
    gram_ref[...] = gram_rows(products, row, 0) + jnp.where((row == 6) & (spot == 0), shift, 0.0)


def last_kernel(
    summed_ref, edges_ref, xe_ref, xo_ref, image_ref, scale_ref,
    source_ref, power_ref, shifted_in_ref, shift_ref, gram_in_ref,
    direction_ref, second_ref, gram_ref, q_ref, t_ref, edge_ref,
):
    rows = source_ref.shape[1]
    row, spot = sublane(), lane()
    fields = (q_ref, t_ref)
    fold_x(summed_ref, edges_ref, xe_ref, xo_ref, fields, edge_ref)
    products = [jnp.zeros(TILE, F32) for _ in range(3)]
    for x in range(rows):
        keep_direction(direction_ref, scale_ref, fields, x)
        for k, part in enumerate(image_row(fields, edge_ref, image_ref, x, row, spot)):
            power = power_ref[k, x]
            second = part * scale_ref[k, x] - power
            second_ref[k, x] = second
            shifted = second - shift_ref[...] * power
            products[0] = products[0] + source_ref[k, x] * shifted
            products[1] = products[1] + shifted_in_ref[k, x] * shifted
            products[2] = products[2] + shifted * shifted
    total = jnp.sum(gram_in_ref[...] + gram_rows(products, row, 3), axis=1, keepdims=True)
    line = jnp.sum(jnp.where(row == spot, jnp.broadcast_to(total, TILE), 0.0), axis=0, keepdims=True)
    gram_ref[...] = jnp.broadcast_to(line, gram_ref.shape)


def combine_kernel(
    gram_ref, source_ref, power_ref, second_ref, one_ref, two_ref,
    adjoint_hbm, residual_hbm, basis_hbm, adjoint_ref, residual_ref, basis_ref, sems, *, scale,
):
    parts = gram_ref[...]
    spot = lax.broadcasted_iota(jnp.int32, parts.shape, 1)
    p00, p01, p11, p02, p12, p22, shift_of = (
        jnp.sum(jnp.where(spot == k, parts, 0.0), axis=1, keepdims=True) for k in range(7)
    )
    total = lambda value: jnp.sum(value, axis=0, keepdims=True)
    g00 = total(p00)
    shift = total(shift_of * p00) / jnp.maximum(g00, 1e-30)
    e = shift_of - shift
    f = e * shift_of
    mixed = p02 + e * p01 + f * p00
    g01 = total(p01 + e * p00)
    g11 = total(p11 + e * (2.0 * p01 + e * p00))
    g02 = total(mixed)
    g12 = total(p12 + e * p11 + f * p01 + e * mixed)
    g22 = total(p22 + 2.0 * (e * p12 + f * p02 + e * f * p01) + e * e * p11 + f * f * p00)
    grown = 1.0 + shift
    beta2 = g00 + EPSILON
    beta = jnp.sqrt(beta2)
    less = (grown * EPSILON - g01) / beta2
    h11 = (grown * g00 + g01) / beta2
    square = (less * less * g00 + 2.0 * less * g01 + g11) / beta2
    square = jnp.maximum(square, 0.0)
    h21 = jnp.sqrt(square + EPSILON)
    b = 1.0 / (beta * h21)
    a = less * b
    c = a - shift * b
    along_r, along_p = c * g01 + b * g02, c * g11 + b * g12
    h12 = grown * EPSILON * h11 * b / beta + along_r / beta
    d2 = a * along_r + b * along_p
    unit = 1.0 / (square + EPSILON)
    short = grown * EPSILON * unit - d2
    h22 = grown * square * unit + d2
    c0 = a * short - h12 / beta
    c1 = b * short + c
    c2 = b
    square = c0 * (c0 * g00 + 2.0 * (c1 * g01 + c2 * g02)) + c1 * (c1 * g11 + 2.0 * c2 * g12) + c2 * c2 * g22
    h32 = jnp.sqrt(jnp.maximum(square, 0.0) + EPSILON)
    a = c
    c0, c1 = c0 - shift * c1, c1 - shift * c2
    n0, n1, n2 = h21 * h32, -h11 * h32, h11 * h22 - h12 * h21
    factor = beta * n0 / (n0 * n0 + n1 * n1 + n2 * n2)
    f0, f1, f2 = factor * n0, factor * n1, factor * n2
    y2 = -f2 / h32
    y1 = (h11 * (beta - f0 - h12 * y2) - h21 * (f1 + h22 * y2)) / (h11 * h11 + h21 * h21)
    over = 1.0 / h32
    v0, v1, v2 = c0 * over, c1 * over, c2 * over
    wide = lambda value: jnp.broadcast_to(value, TILE)
    z_one, z_two = wide(y1 / beta + y2 * a), wide(y2 * b)
    r0, r1, r2 = wide(f0 / beta + f1 * a + f2 * v0), wide(f1 * b + f2 * v1), wide(f2 * v2)
    s0, s1, s2 = wide(scale * v0), wide(scale * v1), wide(scale * v2)
    copies = []
    for k in range(2):
        for x in range(source_ref.shape[1]):
            source, power, second = source_ref[k, x], power_ref[k, x], second_ref[k, x]
            adjoint_ref[k, x] = z_one * one_ref[k, x] + z_two * two_ref[k, x]
            residual_ref[k, x] = r0 * source + r1 * power + r2 * second
            basis_ref[k, x] = s0 * source + s1 * power + s2 * second
        pairs = ((adjoint_ref, adjoint_hbm), (residual_ref, residual_hbm), (basis_ref, basis_hbm))
        for index, (src, dst) in enumerate(pairs):
            copy = pltpu.make_async_copy(src.at[k], dst.at[k], sems.at[k, index])
            copy.start()
            copies.append(copy)
    for copy in copies:
        copy.wait()


def call(kernel, outs, scratch=(), name=None, inside=pltpu.VMEM, outside=pltpu.VMEM, cost=None):
    def run(*args):
        return pl.pallas_call(
            kernel,
            out_shape=[
                jax.ShapeDtypeStruct(*(spec if isinstance(spec[0], tuple) else (spec, F32))) for spec in outs
            ],
            in_specs=[pl.BlockSpec(memory_space=inside)] * len(args),
            out_specs=[pl.BlockSpec(memory_space=outside)] * len(outs),
            scratch_shapes=[pltpu.VMEM(spec, F32) if isinstance(spec, tuple) else spec for spec in scratch],
            compiler_params=pltpu.CompilerParams(vmem_limit_bytes=32 * 1024 * 1024),
            name=name,
            cost_estimate=cost,
        )(*args)

    return run


def exchange(axis, even, odd):
    n_x, n_y = lax.axis_size("gx"), lax.axis_size("gy")
    count = lax.axis_size(axis)
    pairs = [(i, i ^ 1) for i in range(count)]
    others = []
    for x in range(n_x):
        for y in range(n_y):
            place = x if axis == "gx" else y
            if 0 < place < count - 1:
                partner = ((place - 1) ^ 1) + 1
                target = (partner, y) if axis == "gx" else (x, partner)
            else:
                target = (x, y ^ 1) if axis == "gx" else (x ^ (n_x // 2), y)
            others.append((x * n_y + y, target[0] * n_y + target[1]))
    return lax.ppermute(even, axis, pairs), lax.ppermute(odd, ("gx", "gy"), others)


def shards(adjoint_source, storage, soil_ids, bc_mask, soil_props):
    rows, _, depth = soil_ids.shape
    wide = rows + 2 * MARGIN
    devices = lax.axis_size("gx") * lax.axis_size("gy")
    cells = 2.0 * rows * soil_ids.shape[1] * depth * devices
    own = (rows, *TILE)
    x_slab = (5 * MARGIN, *TILE)
    held = (SUB, rows)
    *raw, x_even, x_odd = call(
        first_pack_kernel,
        [soil_props.shape, (4, *own), (own, jnp.int32), (held, jnp.int32), x_slab, x_slab],
        [pltpu.SemaphoreType.DMA((4,))],
        name="first_pack",
        inside=pltpu.HBM,
    )(*(pltpu.with_memory_space_constraint(x, pltpu.HBM) for x in (soil_props, storage, soil_ids, bc_mask.T)))
    xe, xo = exchange("gx", x_even, x_odd)
    slab = y_slab(rows, rows)
    fields, wire, y_even, y_odd = call(own_pack_kernel, [(4, *own), own, slab, slab], name="own_pack")(*raw)
    ye, yo = exchange("gy", y_even, y_odd)
    slab = y_slab(5, 8)
    weight = pl.CostEstimate(flops=10**11, bytes_accessed=10**9, transcendentals=0)
    even, odd = call(corner_pack_kernel, [slab, slab], name="corner_pack", cost=weight)(soil_props, xe, xo)
    ce, co = exchange("gy", even, odd)
    count = wide // SUB
    own_coeff, own_side, image, scales, rhs, roots, roots_side = call(
        own_coefficients_kernel,
        [(4, *own), (4, rows - 2, *TILE), (4, *own), (5, *own), (2, *own)]
        + [(2, rows + 2 * RIM, *TILE), (2, *own)],
        name="own_coefficients",
    )(soil_props, fields, wire, xe, xo, ye, yo, adjoint_source)
    buffers = [(wide + 2, 2, *TILE)] * 4
    slab = (rows + 5 + 2 * count, *TILE)
    solved_shapes = [(2, wide, *TILE), (4, count, *TILE), slab, slab]
    rest, rest_side, solved, edges, even, odd = call(
        first_solve_kernel,
        [(4, 2 * MARGIN, *TILE), (4, 2 * RIM, *TILE)] + solved_shapes,
        [(2, 2 * RIM, *TILE)] + buffers,
        name="first_solve",
    )(soil_props, xe, xo, ye, yo, ce, co, own_coeff, own_side, rhs, roots, roots_side)
    coeffs = (own_coeff, own_side, rest, rest_side)

    slab = (2 * (MARGIN + 2), *TILE)
    fold_shapes = [(2, wide, *TILE), (4, count, *TILE), slab, slab]
    ye, yo = exchange("gy", even, odd)
    summed, edges, even, odd = call(fold_y_kernel, fold_shapes, name="fold_y")(solved, edges, ye, yo)
    xe, xo = exchange("gx", even, odd)
    halo = [(rows + 2, *TILE)] * 2 + [(4, count, *TILE)]
    rhs, q, t, solved, edges, even, odd = call(
        step_kernel,
        [(2, *own), halo[0], halo[0]] + solved_shapes,
        halo[2:] + buffers,
        name="second_solve",
    )(summed, edges, xe, xo, *coeffs, image, scales, adjoint_source)
    one, power, shifted, shift, gram = call(power_kernel, [(2, *own)] * 3 + [TILE, TILE], name="first_power")(
        rhs, q, t, scales, adjoint_source
    )

    ye, yo = exchange("gy", even, odd)
    summed, edges, even, odd = call(fold_y_kernel, fold_shapes, name="fold_y")(solved, edges, ye, yo)
    xe, xo = exchange("gx", even, odd)
    two, second, gram = call(
        last_kernel, [(2, *own), (2, *own), (devices, LANE)], halo, name="last_image"
    )(summed, edges, xe, xo, image, scales, adjoint_source, power, shifted, shift, gram)
    gram = lax.all_to_all(gram, ("gx", "gy"), 0, 0, tiled=True)
    return tuple(
        call(
            functools.partial(combine_kernel, scale=math.sqrt(cells)),
            [(2, *own)] * 3,
            [(2, *own)] * 3 + [pltpu.SemaphoreType.DMA((2, 3))],
            name="combine",
            outside=pltpu.HBM,
        )(gram, adjoint_source, power, second, one, two)
    )


def solution(mesh):
    in_specs = (
        P(None, "gx", "gy", None),
        P(None, "gx", "gy", None),
        P("gx", "gy", None),
        P("gx", "gy"),
        P(),
    )
    out_specs = (P(None, "gx", "gy", None), P(None, "gx", "gy", None), P(None, "gx", "gy", None))
    return jax.shard_map(shards, mesh=mesh, in_specs=in_specs, out_specs=out_specs, check_vma=False)
```

```python
import functools
import math

import jax
import jax.numpy as jnp
from jax import lax
from jax.experimental import pallas as pl
from jax.experimental.pallas import tpu as pltpu
from jax.sharding import PartitionSpec as P

MARGIN = 4
SWEEPS = 6
SUB = 8
LANE = 128
TILE = (SUB, LANE)
RIM = MARGIN + 1
EPSILON = 1e-06
F32 = jnp.float32


def sublane():
    return lax.broadcasted_iota(jnp.int32, TILE, 0)


def lane():
    return lax.broadcasted_iota(jnp.int32, TILE, 1)


def up_y(tile):
    return pltpu.roll(tile, SUB - 1, 0)


def down_y(tile):
    return pltpu.roll(tile, 1, 0)


def half_turn(tile):
    return pltpu.roll(tile, SUB // 2, 0)


def along_z(tile, spot):
    above = jnp.where(spot == LANE - 1, 0.0, pltpu.roll(tile, LANE - 1, 1))
    below = jnp.where(spot == 0, 0.0, pltpu.roll(tile, 1, 1))
    return above + below


def along_y(own, side, row, last_up, last_down):
    own_up, own_down = up_y(own), down_y(own)
    side_up, side_down = up_y(side), down_y(side)
    own_sum = jnp.where(row == 7, side_up, own_up) + jnp.where(row == 0, side_down, own_down)
    if last_up is None:
        return own_sum, None
    side_sum = jnp.where(row == 7, own_up, jnp.where(row == 3, last_up, side_up))
    side_sum = side_sum + jnp.where(row == 0, own_down, jnp.where(row == 4, last_down, side_down))
    return own_sum, side_sum


def position(axis):
    place = lax.axis_index(axis)
    first = lax.rem(place, 2) == 0
    return first, place > 0, place < lax.axis_size(axis) - 1


def from_sides(first, even, odd):
    return jnp.where(first, odd, even), jnp.where(first, even, odd)


def lookup(table, wire):
    index = jnp.maximum(wire.astype(jnp.int32) - 1, 0)
    return jnp.where(wire > 0.0, jnp.take_along_axis(table, index, axis=1), 0.0)


def wide_tables(props_ref):
    pad = jnp.zeros((props_ref.shape[0], LANE - props_ref.shape[1]), F32)
    wide = jnp.concatenate([props_ref[...], pad], axis=1)
    return [jnp.broadcast_to(wide[k : k + 1], TILE) for k in range(3)]


def rim_rows(even_ref, odd_ref, base, tiles, rows_even, rows_odd):
    for j, (tile_ref, index) in enumerate(tiles):
        line = (base + j // SUB, pl.ds(j % SUB, 1))
        even_ref[line] = tile_ref[(*index, pl.ds(rows_even, 1))]
        odd_ref[line] = tile_ref[(*index, pl.ds(rows_odd, 1))]


def merge_far(near, far, row):
    far = jnp.where(row == 3, pltpu.roll(far, 3, 0), pltpu.roll(far, 5, 0))
    return jnp.where((row == 3) | (row == 4), far, near)


def split_far(tile, row):
    return jnp.where(row < 4, pltpu.roll(tile, 5, 0), pltpu.roll(tile, 3, 0))


def merge_halves(one, other, row):
    other = jnp.where(row < 4, pltpu.roll(other, 2, 0), pltpu.roll(other, 6, 0))
    return jnp.where((row >= 2) & (row < 6), other, one)


def split_halves(tile, row):
    return jnp.where(row < 4, pltpu.roll(tile, 6, 0), pltpu.roll(tile, 2, 0))


def condense(tiles, row):
    return [
        tiles[3],
        merge_far(tiles[2], tiles[0], row),
        tiles[4],
        merge_far(tiles[5], tiles[7], row),
        merge_halves(tiles[1], tiles[6], row),
    ]


def expand(tiles, row):
    low, low_two, high, high_two, three = tiles
    return [
        split_far(low_two, row), three, low_two, low, high, high_two, split_halves(three, row), split_far(high_two, row),
    ]


def condense_wire(tiles, row):
    four = merge_halves(tiles[1], tiles[8], row)
    low, high = merge_far(tiles[2], tiles[0], row), merge_far(tiles[7], tiles[9], row)
    return [tiles[4], tiles[3], low, four, tiles[5], tiles[6], high, four]


def expand_wire(tiles, row):
    low, low_two, low_three, four, high, high_two, high_three, _ = tiles
    return [
        split_far(low_three, row), four, low_three, low_two, low,
        high, high_two, high_three, split_halves(four, row), split_far(high_three, row),
    ]


def pack_y(fields, wire, even_ref, odd_ref):
    first, _, _ = position("gy")
    even_low = (sublane() < 4) != first
    count, half = len(fields[0]), len(wire) // 2

    def put(spot, one, other):
        other = half_turn(other)
        even_ref[spot] = jnp.where(even_low, one, other)
        odd_ref[spot] = jnp.where(even_low, other, one)

    for pair in range(2):
        for i in range(count):
            put(pair * count + i, fields[2 * pair][i], fields[2 * pair + 1][i])
    for j in range(half):
        put(2 * count + j, wire[j], wire[j + half])


def fold_beyond(fields, wire, tables, row):
    out = list(fields)
    for k, table in ((0, tables[0]), (3, tables[1])):
        value = lookup(table, wire)
        face = jnp.sqrt(value * jnp.where(row == 3, up_y(value), down_y(value)))
        out[k] = out[k] + jnp.where((row == 3) | (row == 4), face, 0.0)
    return out


def y_slab(count, ids):
    return (2 * count + ids // 2, *TILE)


def unpack_fields(even_ref, odd_ref, count, i):
    first, _, _ = position("gy")
    row = sublane()
    out = []
    for pair in range(2):
        low, high = from_sides(first, even_ref[pair * count + i], odd_ref[pair * count + i])
        out.append(jnp.where(row < 4, high, low))
        out.append(half_turn(jnp.where(row < 4, low, high)))
    return out


def unpack_wire(even_ref, odd_ref, count, ids):
    first, has_low, has_high = position("gy")
    row = sublane()

    def sides(spot):
        low, high = from_sides(first, even_ref[spot], odd_ref[spot])
        return jnp.where(has_low, low, 0.0), jnp.where(has_high, high, 0.0)

    one, other = [], []
    for j in range(ids // 2):
        low, high = sides(2 * count + j)
        one.append(jnp.where(row < 4, high, low))
        other.append(half_turn(jnp.where(row < 4, low, high)))
    return one + other


def halo_x(even_ref, odd_ref):
    first, has_low, has_high = position("gx")
    groups = []
    for k in range(5):
        spots = pl.ds(k * MARGIN, MARGIN)
        low, high = from_sides(first, even_ref[spots], odd_ref[spots])
        if k == 4:
            low = jnp.where(has_low, low, 0.0)
            high = jnp.where(has_high, high, 0.0)
        groups.append([low[i] for i in range(MARGIN)] + [high[i] for i in range(MARGIN)])
    empty = jnp.zeros(TILE, F32)
    return groups[:4], [empty, *groups[4], empty]


def own_row(tables, storage_ref, ids_ref, bc_ref, x, spot):
    wire = (ids_ref[x] + 1).astype(F32)
    kp = lookup(tables[0], wire)
    carried = lookup(tables[2], wire)
    held = jnp.broadcast_to(bc_ref[:, x : x + 1].astype(F32), TILE)
    bound = jnp.where(spot == LANE - 1, 2.0 * kp * held, 0.0)
    press = storage_ref[0, x]
    lower = storage_ref[1, x]
    fields = (press + bound, carried * press - storage_ref[2, x], lower, storage_ref[3, x] - carried * lower)
    return fields, wire


def first_pack_kernel(
    props_hbm, storage_hbm, ids_hbm, bc_hbm,
    props_ref, storage_ref, ids_ref, bc_ref, even_ref, odd_ref, sems,
):
    places = ((ids_hbm, ids_ref), (storage_hbm, storage_ref), (props_hbm, props_ref), (bc_hbm, bc_ref))
    copies = [pltpu.make_async_copy(src, dst, sems.at[k]) for k, (src, dst) in enumerate(places)]
    for copy in copies:
        copy.start()
    rows = ids_ref.shape[0]
    spot = lane()
    first, _, _ = position("gx")
    for copy in copies:
        copy.wait()
    tables = wide_tables(props_ref)

    ends = []
    for start, inner, beyond in ((0, MARGIN - 1, MARGIN), (rows - MARGIN, 0, -1)):
        values, wires = zip(*(own_row(tables, storage_ref, ids_ref, bc_ref, start + i, spot) for i in range(MARGIN)))
        fields = [[value[k] for value in values] for k in range(4)]
        next_wire = (ids_ref[start + beyond] + 1).astype(F32)
        for k, table in ((0, tables[0]), (3, tables[1])):
            face = jnp.sqrt(lookup(table, wires[inner]) * lookup(table, next_wire))
            fields[k][inner] = fields[k][inner] + face
        ends.append([tile for group in (*fields, wires) for tile in group])
    for place, (low, high) in enumerate(zip(*ends)):
        even_ref[place] = jnp.where(first, high, low)
        odd_ref[place] = jnp.where(first, low, high)


def own_pack_kernel(
    props_ref, storage_ref, ids_ref, bc_ref, fields_ref, wire_ref, even_ref, odd_ref,
):
    rows = ids_ref.shape[0]
    spot = lane()
    tables = wide_tables(props_ref)
    fields = [[] for _ in range(4)]
    wires = []
    for x in range(rows):
        values, wire = own_row(tables, storage_ref, ids_ref, bc_ref, x, spot)
        wire_ref[x] = wire
        wires.append(wire)
        for k in range(4):
            fields_ref[k, x] = values[k]
        for k, value in enumerate(fold_beyond(values, wire, tables, sublane())):
            fields[k].append(value)
    pack_y(fields, wires, even_ref, odd_ref)


def corner_pack_kernel(props_ref, xe_ref, xo_ref, even_ref, odd_ref):
    row = sublane()
    tables = wide_tables(props_ref)
    fields, wire = halo_x(xe_ref, xo_ref)
    for i in (MARGIN - 1, MARGIN):
        for k, value in enumerate(fold_beyond([field[i] for field in fields], wire[i + 1], tables, row)):
            fields[k][i] = value
    fields = [condense(field, row) for field in fields]
    pack_y(fields, condense_wire(wire, row), even_ref, odd_ref)


def sweep_row(load, coeff, j, row, spot, rhs, count):
    sums = []
    for k in range(2):
        own, side = load(k, j, 0), load(k, j, 1)
        own_sum, side_sum = along_y(own, side, row, *((0.0, 0.0) if count == 2 else (None, None)))
        own_sum = own_sum + (along_z(own, spot) + (load(k, j - 1, 0) + load(k, j + 1, 0)))
        if count == 2:
            side_sum = side_sum + (along_z(side, spot) + (load(k, j - 1, 1) + load(k, j + 1, 1)))
        sums.append([own_sum, side_sum])
    if rhs is not None:
        sums[0][0] = sums[0][0] + rhs[0]
        sums[1][0] = sums[1][0] + rhs[1]
    out = []
    for tile in range(count):
        flow, heat = sums[0][tile], sums[1][tile]
        out.append(
            (
                coeff(0, j - 1, tile) * flow + coeff(1, j - 1, tile) * heat,
                coeff(2, j - 1, tile) * flow + coeff(3, j - 1, tile) * heat,
            )
        )
    return out


def reach_of(sweep, rows):
    reach = min(sweep, MARGIN)
    return [(x, 2 if max(-x, x - rows + 1) < sweep else 1) for x in range(-reach, rows + reach)]


def read_first(rows):
    written = [{(x + RIM, 0) for x in range(rows)}, set()]
    missing = []
    for sweep in range(1, SWEEPS):
        half = (sweep - 1) % 2
        reads = set()
        for x, count in reach_of(sweep, rows):
            j = x + RIM
            reads |= {(j, 0), (j, 1), (j - 1, 0), (j + 1, 0)}
            if count == 2:
                reads |= {(j - 1, 1), (j + 1, 1)}
        missing += [(half, *spot) for spot in sorted(reads - written[half])]
        written[half] |= reads
        written[1 - half] |= {(x + RIM, tile) for x, count in reach_of(sweep, rows) for tile in range(count)}
    return missing


def subdomain_sweeps(rhs_ref, coeff, solved_ref, rims_ref, even_ref, odd_ref, buffers, rows):
    row, spot = sublane(), lane()
    wide = rows + 2 * MARGIN
    zero = jnp.zeros(TILE, F32)
    for half, j, tile in read_first(rows):
        for k in range(2):
            buffers[2 * half + k][j, tile] = zero
    current, following = buffers[:2], buffers[2:]
    for x in range(rows):
        j = x + RIM
        flow, heat = rhs_ref[0, x], rhs_ref[1, x]
        current[0][j, 0] = coeff(0, j - 1, 0) * flow + coeff(1, j - 1, 0) * heat
        current[1][j, 0] = coeff(2, j - 1, 0) * flow + coeff(3, j - 1, 0) * heat
    first, _, _ = position("gy")
    even_low = (row < 4) != first
    last = []
    for sweep in range(1, SWEEPS):
        load = functools.cache(functools.partial(lambda pair, k, j, tile: pair[k][j, tile], current))
        for x, count in reach_of(sweep, rows):
            j = x + RIM
            rhs = (rhs_ref[0, x], rhs_ref[1, x]) if 0 <= x < rows else None
            out = sweep_row(load, coeff, j, row, spot, rhs, count)
            if sweep < SWEEPS - 1:
                for tile in range(count):
                    following[0][j, tile] = out[tile][0]
                    following[1][j, tile] = out[tile][1]
            else:
                i = j - 1
                (own_q, own_t), (side_q, side_t) = out
                solved_ref[0, i], solved_ref[1, i] = own_q, own_t
                last.append((side_q, side_t))
                for k, side in enumerate((side_q, side_t)):
                    line = (i // SUB, pl.ds(i % SUB, 1))
                    rims_ref[(2 * k, *line)] = side[7:8]
                    rims_ref[(2 * k + 1, *line)] = side[0:1]
        current, following = following, current
    corners = [condense([last[i][k] for i in [*range(MARGIN), *range(rows + MARGIN, wide)]], row) for k in range(2)]
    for i, (flow, heat) in enumerate(last[MARGIN : rows + MARGIN] + list(zip(*corners))):
        heat = half_turn(heat)
        even_ref[i] = jnp.where(even_low, heat, flow)
        odd_ref[i] = jnp.where(even_low, flow, heat)
    rows_even, rows_odd = jnp.where(first, 7, 0), jnp.where(first, 0, 7)
    for k in range(2):
        spots = [(solved_ref, (k, i)) for i in range(wide)]
        rim_rows(even_ref, odd_ref, rows + 5 + k * (wide // SUB), spots, rows_even, rows_odd)


def getter(own_ref, own_side_ref, rest_ref, rest_side_ref):
    rows = own_ref.shape[1]

    def coeff(k, i, tile):
        ref, rest, start, count = (own_ref, rest_ref, MARGIN, rows)
        if tile:
            ref, rest, start, count = (own_side_ref, rest_side_ref, MARGIN + 1, rows - 2)
        if start <= i < start + count:
            return ref[k, i - start]
        return rest[k, i if i < start else i - count]

    return coeff


def diagonal(tiles, index, spot):
    j, last_up, last_down = index
    own_sum, side_sum = along_y(tiles(j, 0), tiles(j, 1), sublane(), last_up, last_down)
    out = []
    for tile, total in ((0, own_sum), (1, side_sum)):
        if tile == 1 and last_up is None:
            break
        centre = tiles(j, tile)
        total = total + along_z(centre, spot) + (tiles(j - 1, tile) + tiles(j + 1, tile))
        out.append(centre * total)
    return out


def block_tiles(stores, sums, scales, wire):
    press, cross, lower, heat = stores
    gp, gt = scales
    outside = jnp.where(wire > 0.0, 0.0, 1.0)
    a = press + sums[0] + outside
    d = heat + sums[1] + outside
    inverse = 1.0 / (a * d + cross * lower)
    pp, pt, tt = gp * gp * inverse, gp * gt * inverse, gt * gt * inverse
    return a, d, (pp * d, pt * cross, -(pt * lower), tt * a)


def root_tables(props_ref):
    tables = wide_tables(props_ref)
    return [jnp.sqrt(jnp.maximum(table, 0.0)) for table in tables[:2]], tables[2]


def own_coefficients_kernel(
    props_ref, fields_ref, wire_ref, xe_ref, xo_ref, ye_ref, yo_ref, source_ref,
    own_ref, own_side_ref, image_ref, scale_ref, rhs_ref, roots_ref, roots_side_ref,
):
    rows = wire_ref.shape[0]
    spot = lane()
    roots, carried = root_tables(props_ref)
    _, x_wire = halo_x(xe_ref, xo_ref)
    sides = unpack_wire(ye_ref, yo_ref, rows, rows)
    wire = x_wire[:RIM] + [wire_ref[x] for x in range(rows)] + x_wire[RIM:]
    for g in range(2):
        for j, value in enumerate(wire):
            roots_ref[g, j] = lookup(roots[g], value)
        for x in range(rows):
            roots_side_ref[g, x] = lookup(roots[g], sides[x])
    for x in range(rows):
        inner = 0 < x < rows - 1
        sums = []
        for g in range(2):
            tiles = lambda j, tile: roots_side_ref[g, j - RIM] if tile else roots_ref[g, j]
            lines = (0.0, 0.0) if inner else (None, None)
            sums.append(diagonal(tiles, (x + RIM, *lines), spot))
        stores = [fields_ref[k, x] for k in range(4)]
        gp, gt = (roots_ref[g, x + RIM] for g in range(2))
        a, d, coeffs = block_tiles(stores, (sums[0][0], sums[1][0]), (gp, gt), wire_ref[x])
        for k in range(4):
            own_ref[k, x] = coeffs[k]
        over_p, over_t = 1.0 / gp, 1.0 / gt
        over = over_p * over_t
        image_ref[0, x] = a * (over_p * over_p)
        image_ref[1, x] = -(stores[1] * over)
        image_ref[2, x] = stores[2] * over
        image_ref[3, x] = d * (over_t * over_t)
        for k, value in enumerate((gp, gt, over_p, over_t, lookup(carried, wire_ref[x]))):
            scale_ref[k, x] = value
        rhs_ref[0, x] = source_ref[0, x] * over_p
        rhs_ref[1, x] = source_ref[1, x] * over_t
        if inner:
            stores = unpack_fields(ye_ref, yo_ref, rows, x)
            scales = [roots_side_ref[g, x] for g in range(2)]
            _, _, coeffs = block_tiles(stores, (sums[0][1], sums[1][1]), scales, sides[x])
            for k in range(4):
                own_side_ref[k, x - 1] = coeffs[k]


def first_solve_kernel(
    props_ref, xe_ref, xo_ref, ye_ref, yo_ref, ce_ref, co_ref,
    own_ref, own_side_ref, rhs_ref, roots_ref, roots_side_ref,
    rest_ref, rest_side_ref, solved_ref, rims_ref, even_ref, odd_ref,
    corner_roots_ref, *buffers,
):
    rows = own_ref.shape[1]
    wide = rows + 2 * MARGIN
    spot = lane()
    roots, _ = root_tables(props_ref)
    x_fields, x_wire = halo_x(xe_ref, xo_ref)
    row = sublane()
    sides = unpack_wire(ce_ref, co_ref, 5, 8)
    sides = expand_wire(sides, row)
    corner_stores = [unpack_fields(ce_ref, co_ref, 5, i) for i in range(5)]
    corner_stores = [expand([stores[k] for stores in corner_stores], row) for k in range(4)]
    own_sides = unpack_wire(ye_ref, yo_ref, rows, rows)
    for g in range(2):
        for j, value in enumerate(sides):
            corner_roots_ref[g, j] = lookup(roots[g], value)
    for i in list(range(RIM)) + list(range(wide - RIM, wide)):
        j, x = i + 1, i - MARGIN
        own_row = 0 <= x < rows
        sums = []
        for g in range(2):

            def tiles(j, tile):
                if not tile:
                    return roots_ref[g, j]
                if RIM <= j < RIM + rows:
                    return roots_side_ref[g, j - RIM]
                return corner_roots_ref[g, j if j < RIM else j - rows]

            sums.append((diagonal(tiles, (j, 0.0, 0.0), spot), tiles(j, 0), tiles(j, 1)))
        corner = i if i < MARGIN else i - rows
        if not own_row:
            stores = [x_fields[k][corner] for k in range(4)]
            scales = (sums[0][1], sums[1][1])
            spare = x_wire[j if j < RIM else j - rows]
            _, _, coeffs = block_tiles(stores, (sums[0][0][0], sums[1][0][0]), scales, spare)
            for k in range(4):
                rest_ref[k, corner] = coeffs[k]
            stores = [corner_stores[k][corner] for k in range(4)]
            spare = sides[j if j < RIM else j - rows]
        else:
            stores = unpack_fields(ye_ref, yo_ref, rows, x)
            spare = own_sides[x]
        scales = (sums[0][2], sums[1][2])
        _, _, coeffs = block_tiles(stores, (sums[0][0][1], sums[1][0][1]), scales, spare)
        for k in range(4):
            rest_side_ref[k, i if i < RIM else i - (rows - 2)] = coeffs[k]
    coeff = getter(own_ref, own_side_ref, rest_ref, rest_side_ref)
    subdomain_sweeps(rhs_ref, coeff, solved_ref, rims_ref, even_ref, odd_ref, buffers, rows)


def fold_y_kernel(solved_ref, rims_ref, ye_ref, yo_ref, summed_ref, edges_ref, even_ref, odd_ref):
    wide = solved_ref.shape[1]
    row = sublane()
    first, has_low, has_high = position("gy")
    rows = wide - 2 * MARGIN
    tiles = [[], []]
    for i in range(rows + 5):
        low, high = from_sides(first, ye_ref[i], yo_ref[i])
        low = jnp.where(has_low, low, 0.0)
        high = jnp.where(has_high, high, 0.0)
        tiles[0].append(jnp.where(row < 4, low, high))
        tiles[1].append(half_turn(jnp.where(row < 4, high, low)))
    for k in range(2):
        corners = expand(tiles[k][rows:], row)
        for spot, reach in enumerate((1, 2, 3, 4, 4, 3, 2, 1)):
            if reach < 4:
                corners[spot] = jnp.where((row < reach) | (row >= SUB - reach), corners[spot], 0.0)
        for i, value in enumerate(corners[:MARGIN] + tiles[k][:rows] + corners[MARGIN:]):
            summed_ref[k, i] = solved_ref[k, i] + value
    count = wide // SUB
    for k in range(2):
        for tile in range(count):
            spot = rows + 5 + k * count + tile
            low, high = from_sides(first, ye_ref[spot], yo_ref[spot])
            edges_ref[2 * k, tile] = rims_ref[2 * k, tile] + jnp.where(has_low, low, 0.0)
            edges_ref[2 * k + 1, tile] = rims_ref[2 * k + 1, tile] + jnp.where(has_high, high, 0.0)
    first, _, _ = position("gx")
    margin_even = jnp.where(first, wide - MARGIN, 0)
    margin_odd = jnp.where(first, 0, wide - MARGIN)
    rim_even = jnp.where(first, wide - MARGIN - 1, MARGIN)
    rim_odd = jnp.where(first, MARGIN, wide - MARGIN - 1)
    for k in range(2):
        base = k * (MARGIN + 2)
        for ref, margin, rim in ((even_ref, margin_even, rim_even), (odd_ref, margin_odd, rim_odd)):
            ref[pl.ds(base, MARGIN)] = summed_ref[k, pl.ds(margin, MARGIN)]
            ref[base + MARGIN] = summed_ref[k, rim]
        to_low = jnp.where(row < 4, edges_ref[2 * k, 0], half_turn(edges_ref[2 * k + 1, 0]))
        last = count - 1
        to_high = jnp.where(row < 4, half_turn(edges_ref[2 * k + 1, last]), edges_ref[2 * k, last])
        even_ref[base + MARGIN + 1] = jnp.where(first, to_high, to_low)
        odd_ref[base + MARGIN + 1] = jnp.where(first, to_low, to_high)


def fold_x(summed_ref, edges_ref, xe_ref, xo_ref, field_refs, edge_ref):
    wide = summed_ref.shape[1]
    rows = wide - 2 * MARGIN
    row = sublane()
    first, has_low, has_high = position("gx")
    for k in range(2):
        base = k * (MARGIN + 2)
        low, high = from_sides(first, xe_ref[pl.ds(base, MARGIN + 2)], xo_ref[pl.ds(base, MARGIN + 2)])
        low = jnp.where(has_low, low, 0.0)
        high = jnp.where(has_high, high, 0.0)
        for x in range(-1, rows + 1):
            value = summed_ref[k, x + MARGIN]
            if 0 <= x < MARGIN:
                value = value + low[x]
            if rows - MARGIN <= x < rows:
                value = value + high[x - (rows - MARGIN)]
            if x == -1:
                value = value + low[MARGIN]
            if x == rows:
                value = value + high[MARGIN]
            field_refs[k][x + 1] = value
        from_low, from_high = low[MARGIN + 1], high[MARGIN + 1]
        last = edge_ref.shape[1] - 1
        for end in range(2):
            for tile in range(last + 1):
                value = edges_ref[2 * k + end, tile]
                if tile == 0:
                    part = half_turn(from_low) if end == 1 else from_low
                    value = value + jnp.where(row < 4, 0.0, part)
                if tile == last:
                    part = half_turn(from_high) if end == 1 else from_high
                    value = value + jnp.where(row < 4, part, 0.0)
                edge_ref[2 * k + end, tile] = value


def image_row(field_refs, edge_ref, image_ref, x, row, spot):
    sums = []
    i = x + MARGIN
    for k, ref in enumerate(field_refs):
        own = ref[x + 1]
        down, up = (
            jnp.broadcast_to(edge_ref[2 * k + end, i // SUB, pl.ds(i % SUB, 1)], TILE) for end in range(2)
        )
        total = jnp.where(row == 7, up, up_y(own)) + jnp.where(row == 0, down, down_y(own))
        sums.append(total + along_z(own, spot) + (ref[x] + ref[x + 2]))
    flow, heat = field_refs[0][x + 1], field_refs[1][x + 1]
    return (
        image_ref[0, x] * flow + image_ref[1, x] * heat - sums[0],
        image_ref[2, x] * flow + image_ref[3, x] * heat - sums[1],
    )


def keep_direction(direction_ref, scale_ref, field_refs, x):
    heat = field_refs[1][x + 1] * scale_ref[3, x]
    direction_ref[1, x] = heat
    direction_ref[0, x] = field_refs[0][x + 1] * scale_ref[2, x] - scale_ref[4, x] * heat


def gram_rows(pairs, row, offset):
    total = jnp.zeros(TILE, F32)
    for index, value in enumerate(pairs):
        line = jnp.broadcast_to(jnp.sum(value, axis=0, keepdims=True), TILE)
        total = total + jnp.where(row == index + offset, line, 0.0)
    return total


def step_kernel(
    summed_ref, edges_ref, xe_ref, xo_ref, own_ref, own_side_ref, rest_ref, rest_side_ref, image_ref, scale_ref, source_ref,
    rhs_ref, q_ref, t_ref, solved_ref, rims_ref, even_ref, odd_ref, edge_ref, *buffers,
):
    rows = source_ref.shape[1]
    row, spot = sublane(), lane()
    fields = (q_ref, t_ref)
    fold_x(summed_ref, edges_ref, xe_ref, xo_ref, fields, edge_ref)
    for x in range(rows):
        for k, part in enumerate(image_row(fields, edge_ref, image_ref, x, row, spot)):
            rhs_ref[k, x] = part - source_ref[k, x] * scale_ref[2 + k, x]
    coeff = getter(own_ref, own_side_ref, rest_ref, rest_side_ref)
    subdomain_sweeps(rhs_ref, coeff, solved_ref, rims_ref, even_ref, odd_ref, buffers, rows)


def power_kernel(
    rhs_ref, q_ref, t_ref, scale_ref, source_ref, direction_ref, power_ref, shifted_ref, shift_ref, gram_ref
):
    rows = source_ref.shape[1]
    row, spot = sublane(), lane()
    square = along = jnp.zeros(TILE, F32)
    for x in range(rows):
        keep_direction(direction_ref, scale_ref, (q_ref, t_ref), x)
        for k in range(2):
            source = source_ref[k, x]
            power = rhs_ref[k, x] * scale_ref[k, x]
            power_ref[k, x] = power
            square = square + source * source
            along = along + source * power
    square_sum, along_sum = (
        jnp.sum(jnp.sum(value, axis=0, keepdims=True), axis=1, keepdims=True) for value in (square, along)
    )
    shift = jnp.broadcast_to(along_sum / jnp.maximum(square_sum, 1e-30), TILE)
    shift_ref[...] = shift
    products = [square, jnp.zeros(TILE, F32), jnp.zeros(TILE, F32)]
    for x in range(rows):
        for k in range(2):
            source = source_ref[k, x]
            shifted = power_ref[k, x] - shift * source
            shifted_ref[k, x] = shifted
            products[1] = products[1] + source * shifted
            products[2] = products[2] + shifted * shifted
    gram_ref[...] = gram_rows(products, row, 0) + jnp.where((row == 6) & (spot == 0), shift, 0.0)


def last_kernel(
    summed_ref, edges_ref, xe_ref, xo_ref, image_ref, scale_ref,
    source_ref, power_ref, shifted_in_ref, shift_ref, gram_in_ref,
    direction_ref, second_ref, gram_ref, q_ref, t_ref, edge_ref,
):
    rows = source_ref.shape[1]
    row, spot = sublane(), lane()
    fields = (q_ref, t_ref)
    fold_x(summed_ref, edges_ref, xe_ref, xo_ref, fields, edge_ref)
    products = [jnp.zeros(TILE, F32) for _ in range(3)]
    for x in range(rows):
        keep_direction(direction_ref, scale_ref, fields, x)
        for k, part in enumerate(image_row(fields, edge_ref, image_ref, x, row, spot)):
            power = power_ref[k, x]
            second = part * scale_ref[k, x] - power
            second_ref[k, x] = second
            shifted = second - shift_ref[...] * power
            products[0] = products[0] + source_ref[k, x] * shifted
            products[1] = products[1] + shifted_in_ref[k, x] * shifted
            products[2] = products[2] + shifted * shifted
    total = jnp.sum(gram_in_ref[...] + gram_rows(products, row, 3), axis=1, keepdims=True)
    line = jnp.sum(jnp.where(row == spot, jnp.broadcast_to(total, TILE), 0.0), axis=0, keepdims=True)
    gram_ref[...] = jnp.broadcast_to(line, gram_ref.shape)


def combine_kernel(
    gram_ref, source_ref, power_ref, second_ref, one_ref, two_ref,
    adjoint_hbm, residual_hbm, basis_hbm, adjoint_ref, residual_ref, basis_ref, sems, *, scale,
):
    parts = gram_ref[...]
    spot = lax.broadcasted_iota(jnp.int32, parts.shape, 1)
    p00, p01, p11, p02, p12, p22, shift_of = (
        jnp.sum(jnp.where(spot == k, parts, 0.0), axis=1, keepdims=True) for k in range(7)
    )
    total = lambda value: jnp.sum(value, axis=0, keepdims=True)
    g00 = total(p00)
    shift = total(shift_of * p00) / jnp.maximum(g00, 1e-30)
    e = shift_of - shift
    f = e * shift_of
    mixed = p02 + e * p01 + f * p00
    g01 = total(p01 + e * p00)
    g11 = total(p11 + e * (2.0 * p01 + e * p00))
    g02 = total(mixed)
    g12 = total(p12 + e * p11 + f * p01 + e * mixed)
    g22 = total(p22 + 2.0 * (e * p12 + f * p02 + e * f * p01) + e * e * p11 + f * f * p00)
    grown = 1.0 + shift
    beta2 = g00 + EPSILON
    beta = jnp.sqrt(beta2)
    less = (grown * EPSILON - g01) / beta2
    h11 = (grown * g00 + g01) / beta2
    square = (less * less * g00 + 2.0 * less * g01 + g11) / beta2
    square = jnp.maximum(square, 0.0)
    h21 = jnp.sqrt(square + EPSILON)
    b = 1.0 / (beta * h21)
    a = less * b
    c = a - shift * b
    along_r, along_p = c * g01 + b * g02, c * g11 + b * g12
    h12 = grown * EPSILON * h11 * b / beta + along_r / beta
    d2 = a * along_r + b * along_p
    unit = 1.0 / (square + EPSILON)
    short = grown * EPSILON * unit - d2
    h22 = grown * square * unit + d2
    c0 = a * short - h12 / beta
    c1 = b * short + c
    c2 = b
    square = c0 * (c0 * g00 + 2.0 * (c1 * g01 + c2 * g02)) + c1 * (c1 * g11 + 2.0 * c2 * g12) + c2 * c2 * g22
    h32 = jnp.sqrt(jnp.maximum(square, 0.0) + EPSILON)
    a = c
    c0, c1 = c0 - shift * c1, c1 - shift * c2
    n0, n1, n2 = h21 * h32, -h11 * h32, h11 * h22 - h12 * h21
    factor = beta * n0 / (n0 * n0 + n1 * n1 + n2 * n2)
    f0, f1, f2 = factor * n0, factor * n1, factor * n2
    y2 = -f2 / h32
    y1 = (h11 * (beta - f0 - h12 * y2) - h21 * (f1 + h22 * y2)) / (h11 * h11 + h21 * h21)
    over = 1.0 / h32
    v0, v1, v2 = c0 * over, c1 * over, c2 * over
    wide = lambda value: jnp.broadcast_to(value, TILE)
    z_one, z_two = wide(y1 / beta + y2 * a), wide(y2 * b)
    r0, r1, r2 = wide(f0 / beta + f1 * a + f2 * v0), wide(f1 * b + f2 * v1), wide(f2 * v2)
    s0, s1, s2 = wide(scale * v0), wide(scale * v1), wide(scale * v2)
    copies = []
    half = source_ref.shape[1] // 2
    for k, part in ((0, 0), (0, 1), (1, 0), (1, 1)):
        for x in range(part * half, part * half + half):
            source, power, second = source_ref[k, x], power_ref[k, x], second_ref[k, x]
            adjoint_ref[k, x] = z_one * one_ref[k, x] + z_two * two_ref[k, x]
            residual_ref[k, x] = r0 * source + r1 * power + r2 * second
            basis_ref[k, x] = s0 * source + s1 * power + s2 * second
        pairs = ((adjoint_ref, adjoint_hbm), (residual_ref, residual_hbm), (basis_ref, basis_hbm))
        for index, (src, dst) in enumerate(pairs):
            spots = (k, pl.ds(part * half, half))
            copy = pltpu.make_async_copy(src.at[spots], dst.at[spots], sems.at[2 * k + part, index])
            copy.start()
            copies.append(copy)
    for copy in copies:
        copy.wait()


def call(kernel, outs, scratch=(), name=None, inside=pltpu.VMEM, outside=pltpu.VMEM, cost=None):
    def run(*args):
        return pl.pallas_call(
            kernel,
            out_shape=[
                jax.ShapeDtypeStruct(*(spec if isinstance(spec[0], tuple) else (spec, F32))) for spec in outs
            ],
            in_specs=[pl.BlockSpec(memory_space=inside)] * len(args),
            out_specs=[pl.BlockSpec(memory_space=outside)] * len(outs),
            scratch_shapes=[pltpu.VMEM(spec, F32) if isinstance(spec, tuple) else spec for spec in scratch],
            compiler_params=pltpu.CompilerParams(vmem_limit_bytes=32 * 1024 * 1024),
            name=name,
            cost_estimate=cost,
        )(*args)

    return run


def exchange(axis, even, odd):
    n_x, n_y = lax.axis_size("gx"), lax.axis_size("gy")
    count = lax.axis_size(axis)
    pairs = [(i, i ^ 1) for i in range(count)]
    others = []
    for x in range(n_x):
        for y in range(n_y):
            place = x if axis == "gx" else y
            if 0 < place < count - 1:
                partner = ((place - 1) ^ 1) + 1
                target = (partner, y) if axis == "gx" else (x, partner)
            else:
                target = (x, y ^ 1) if axis == "gx" else (x ^ (n_x // 2), y)
            others.append((x * n_y + y, target[0] * n_y + target[1]))
    return lax.ppermute(even, axis, pairs), lax.ppermute(odd, ("gx", "gy"), others)


def shards(adjoint_source, storage, soil_ids, bc_mask, soil_props):
    rows, _, depth = soil_ids.shape
    wide = rows + 2 * MARGIN
    devices = lax.axis_size("gx") * lax.axis_size("gy")
    cells = 2.0 * rows * soil_ids.shape[1] * depth * devices
    own = (rows, *TILE)
    x_slab = (5 * MARGIN, *TILE)
    held = (SUB, rows)
    *raw, x_even, x_odd = call(
        first_pack_kernel,
        [soil_props.shape, (4, *own), (own, jnp.int32), (held, jnp.int32), x_slab, x_slab],
        [pltpu.SemaphoreType.DMA((4,))],
        name="first_pack",
        inside=pltpu.HBM,
    )(*(pltpu.with_memory_space_constraint(x, pltpu.HBM) for x in (soil_props, storage, soil_ids, bc_mask.T)))
    xe, xo = exchange("gx", x_even, x_odd)
    slab = y_slab(rows, rows)
    fields, wire, y_even, y_odd = call(own_pack_kernel, [(4, *own), own, slab, slab], name="own_pack")(*raw)
    ye, yo = exchange("gy", y_even, y_odd)
    slab = y_slab(5, 8)
    weight = pl.CostEstimate(flops=10**11, bytes_accessed=10**9, transcendentals=0)
    even, odd = call(corner_pack_kernel, [slab, slab], name="corner_pack", cost=weight)(soil_props, xe, xo)
    ce, co = exchange("gy", even, odd)
    count = wide // SUB
    own_coeff, own_side, image, scales, rhs, roots, roots_side = call(
        own_coefficients_kernel,
        [(4, *own), (4, rows - 2, *TILE), (4, *own), (5, *own), (2, *own)]
        + [(2, rows + 2 * RIM, *TILE), (2, *own)],
        name="own_coefficients",
    )(soil_props, fields, wire, xe, xo, ye, yo, adjoint_source)
    buffers = [(wide + 2, 2, *TILE)] * 4
    slab = (rows + 5 + 2 * count, *TILE)
    solved_shapes = [(2, wide, *TILE), (4, count, *TILE), slab, slab]
    rest, rest_side, solved, edges, even, odd = call(
        first_solve_kernel,
        [(4, 2 * MARGIN, *TILE), (4, 2 * RIM, *TILE)] + solved_shapes,
        [(2, 2 * RIM, *TILE)] + buffers,
        name="first_solve",
    )(soil_props, xe, xo, ye, yo, ce, co, own_coeff, own_side, rhs, roots, roots_side)
    coeffs = (own_coeff, own_side, rest, rest_side)

    slab = (2 * (MARGIN + 2), *TILE)
    fold_shapes = [(2, wide, *TILE), (4, count, *TILE), slab, slab]
    ye, yo = exchange("gy", even, odd)
    summed, edges, even, odd = call(fold_y_kernel, fold_shapes, name="fold_y")(solved, edges, ye, yo)
    xe, xo = exchange("gx", even, odd)
    halo = [(rows + 2, *TILE)] * 2 + [(4, count, *TILE)]
    rhs, q, t, solved, edges, even, odd = call(
        step_kernel,
        [(2, *own), halo[0], halo[0]] + solved_shapes,
        halo[2:] + buffers,
        name="second_solve",
    )(summed, edges, xe, xo, *coeffs, image, scales, adjoint_source)
    one, power, shifted, shift, gram = call(power_kernel, [(2, *own)] * 3 + [TILE, TILE], name="first_power")(
        rhs, q, t, scales, adjoint_source
    )

    ye, yo = exchange("gy", even, odd)
    summed, edges, even, odd = call(fold_y_kernel, fold_shapes, name="fold_y")(solved, edges, ye, yo)
    xe, xo = exchange("gx", even, odd)
    two, second, gram = call(
        last_kernel, [(2, *own), (2, *own), (devices, LANE)], halo, name="last_image"
    )(summed, edges, xe, xo, image, scales, adjoint_source, power, shifted, shift, gram)
    gram = lax.all_to_all(gram, ("gx", "gy"), 0, 0, tiled=True)
    return tuple(
        call(
            functools.partial(combine_kernel, scale=math.sqrt(cells)),
            [(2, *own)] * 3,
            [(2, *own)] * 3 + [pltpu.SemaphoreType.DMA((4, 3))],
            name="combine",
            outside=pltpu.HBM,
        )(gram, adjoint_source, power, second, one, two)
    )


def solution(mesh):
    in_specs = (
        P(None, "gx", "gy", None),
        P(None, "gx", "gy", None),
        P("gx", "gy", None),
        P("gx", "gy"),
        P(),
    )
    out_specs = (P(None, "gx", "gy", None), P(None, "gx", "gy", None), P(None, "gx", "gy", None))
    return jax.shard_map(shards, mesh=mesh, in_specs=in_specs, out_specs=out_specs, check_vma=False)
```
